32 devices in a mesh: ctx: 8 (over z, y), wa: 4 (over x, core).
Axes of the slice: x: 2, y: 2, z: 4, core: 2. Of those that a mesh axis runs over, the one named last changes fastest.
Arguments:
- tokens: bfloat16 [1024, 2048], P('ctx'), may hold values from -6 to 6
- positions: int32 [1024], P('ctx'), may hold values from 0 to 511, as said below
- routes: int32 [1024, 8], P(('ctx', 'wa')), may hold values from 0 to 31, all different within a row; in each aligned block of 32 rows (0 to 31, 32 to 63, ...) at most 10 rows name the same one
- query_weight: bfloat16 [2048, 4096], P(None, 'wa'), may hold values from -0.125 to 0.125
- key_matrix: bfloat16 [2048, 512], P(None, 'wa'), may hold values from -0.125 to 0.125
- value_matrix: bfloat16 [2048, 512], P(None, 'wa'), may hold values from -0.125 to 0.125
- out_weight: bfloat16 [4096, 2048], P('wa'), may hold values from -1 to 1
- query_gain: float32 [128], replicated, may hold values from 0.5 to 1.5
- key_gain: float32 [128], replicated, may hold values from 0.5 to 1.5
- input_norm: float32 [2048], replicated, may hold values from 0.5 to 1.5
- post_norm: float32 [2048], replicated, may hold values from 0.5 to 1.5
- router: bfloat16 [2048, 32], replicated, may hold values from -0.0625 to 0.0625
- gate_weight: bfloat16 [32, 2048, 768], P(('ctx', 'wa')), may hold values from -0.125 to 0.125
- up_weight: bfloat16 [32, 2048, 768], P(('ctx', 'wa')), may hold values from -0.125 to 0.125
- down_weight: bfloat16 [32, 768, 2048], P(('ctx', 'wa')), may hold values from -0.625 to 0.625
- cotangent: bfloat16 [1024, 2048], P(('ctx', 'wa')), may hold values from -6 to 6
Outputs:
- output: bfloat16 [1024, 2048], P(('ctx', 'wa'))
- grad_tokens: bfloat16 [1024, 2048], P('ctx')
- grad_query_weight: float32 [2048, 4096], P('ctx', 'wa')
- grad_key_weight: float32 [2048, 512], P('ctx', 'wa')
- grad_value_weight: float32 [2048, 512], P('ctx', 'wa')
- grad_out_weight: float32 [4096, 2048], P('wa', 'ctx')
- grad_query_gain: float32 [128], replicated
- grad_key_gain: float32 [128], replicated
- grad_input_norm: float32 [2048], P('ctx')
- grad_post_norm: float32 [2048], replicated
- grad_router: float32 [2048, 32], replicated
- grad_gate_weight: float32 [32, 2048, 768], P(('ctx', 'wa'))
- grad_up_weight: float32 [32, 2048, 768], P(('ctx', 'wa'))
- grad_down_weight: float32 [32, 768, 2048], P(('ctx', 'wa'))
The draws below stay inside these ranges and needn't reach their ends.
Inputs may be any that keep to these rules, and one draw needn't show every extreme that they name: In sequence order, each sequence's positions are 0 at place 0 and from one place to the next either rise by one or return to 0; in one of the 2 sequences they never return to 0. `routes`: each row names 8 different experts. Within each aligned block of 32 rows (the rows of one device) no expert is named more than 10 times, and in some block one expert is named exactly 10 times.
All inputs are finite; a program needn't handle non-finite values.
Results may differ from the reference program's by a relative error of at most 0.024.
Values may be sent and summed in bfloat16 or wider, within the bound.
No kernel may reach another device: no remote copies, remote signals or barrier semaphores. Data moves between devices by JAX's collectives and lax.ppermute only.
A program may use at most 128 MiB of HBM per device.

```python
import math
import jax
import jax.numpy as jnp
import numpy as np
from jax import lax

MODEL_DIM = 2048
QUERY_HEADS = 32
KEY_VALUE_HEADS = 4
HEAD_DIM = 128
FF = 768
TOPK = 8
SEQS = 2
BLK = 32
LENGTH = 512
TOTAL_TOKENS = 1024
QR = 32
EXPERTS = 32
CAP = 10
N_CTX = 8


def draw_positions(key, part):
    key = jax.random.fold_in(key, 7)
    seq_length = 2 * BLK * N_CTX
    index_list = jnp.arange(seq_length, dtype=jnp.int32)
    cuts = jax.random.randint(jax.random.fold_in(key, 1), (SEQS, seq_length), 0, seq_length) < 4
    whole_seq = jax.random.randint(jax.random.fold_in(key, 2), (), 0, SEQS)
    not_whole = jnp.arange(SEQS, dtype=jnp.int32)[:, None] != whole_seq
    begins = (index_list[None, :] == 0) | cuts & not_whole
    marks = jnp.where(begins, index_list[None, :], 0)
    first_place = lax.cummax(marks, axis=1)
    by_place = index_list[None, :] - first_place
    owner_id = index_list // (2 * BLK)
    inner_id = index_list % BLK
    late_half = index_list % (2 * BLK) // BLK
    places = jnp.where(late_half == 0, owner_id * BLK + inner_id, (2 * N_CTX - 1 - owner_id) * BLK + inner_id)
    stored = by_place[:, places].reshape(SEQS, N_CTX, 2 * BLK)
    return jnp.swapaxes(stored, 0, 1).reshape(-1).astype(jnp.int32)


def block_levels(key, extent, shards, least, high):
    def one(position, parts):
        heights = jax.random.uniform(jax.random.fold_in(jax.random.fold_in(key, 6), position), (parts,), jnp.float32, least / len(shards), high / len(shards))
        return jnp.repeat(jnp.exp(heights), extent[position] // parts).reshape((-1,) + (1,) * (len(extent) - position - 1))

    factor_of = one(*shards[0])
    for cut in shards[1:]:
        factor_of = factor_of * one(*cut)
    return factor_of


def shared_out(own_key, own, number, rows, amount, top, most, lean):
    sequence = jax.random.permutation(own_key, amount)
    packed, usual = shares(amount, rows * top, most, lean, True), shares(amount, rows * top, most, lean, False)
    places = jnp.arange(amount)

    def named(lengths, offset_by):
        used = int((lengths > 0).sum())
        fixed = max(1, used // 4)
        passed = fixed + (places - fixed + offset_by * (used - fixed)) % max(1, amount - fixed)
        return jnp.zeros((amount,), jnp.int32).at[sequence[jnp.where(places < fixed, places, passed)]].set(jnp.asarray(lengths, jnp.int32))

    lengths = jnp.where(number % 4 == 0, named(packed, number // 4), named(usual, number - number // 4 - 1))
    mixed = jax.random.permutation(jax.random.fold_in(own, 3), amount)
    giver, receiver = mixed[0:amount // 2 * 2:2], mixed[1:amount // 2 * 2:2]
    room = jnp.minimum(lengths[giver] - 1, most - lengths[receiver]) // 2
    room = jnp.where((giver == sequence[0]) | (receiver == sequence[0]) | (lengths[receiver] == 0), 0, jnp.maximum(room, 0))
    passed = jax.random.randint(jax.random.fold_in(own, 4), (amount // 2,), 0, 1 << 20) % (room + 1)
    lengths = lengths.at[giver].add(-passed).at[receiver].add(passed)
    labels = jnp.searchsorted(jnp.cumsum(lengths), jnp.arange(rows * top), side="right").astype(jnp.int32)
    grid = labels.reshape(top, rows).T
    grid = grid[jax.random.permutation(jax.random.fold_in(own, 1), rows)]
    offset_by = jax.random.randint(jax.random.fold_in(own, 2), (rows, 1), 0, top)
    return jnp.take_along_axis(grid, (jnp.arange(top)[None, :] + offset_by) % top, axis=1)


def shares(amount, total, bound, slope, full):
    portions = [(1 << 20) // math.isqrt(grade ** slope) + 1 for grade in range(1, amount + 1)]
    largest = bound if full else min(bound, max(-(-total // amount), total * portions[0] // sum(portions)))
    least = 1 if total - largest >= amount - 1 else 0
    holding, surplus = [largest] + [least] * (amount - 1), total - largest - least * (amount - 1)
    while surplus > 0:
        free = [i for i in range(1, amount) if holding[i] < largest] or [i for i in range(1, amount) if holding[i] < bound]
        whole, remaining = sum([portions[i] for i in free]), surplus
        for i in free:
            addition = min(bound - holding[i], max(1, remaining * portions[i] // whole), surplus)
            holding[i] = holding[i] + addition
            surplus = surplus - addition
    return np.array(holding)


def gaussian(own_key, shape, deviation, bound, shards=(), kind=jnp.bfloat16):
    loudness = block_levels(own_key, shape, shards, -0.22, 0.18) if shards else 1.0
    array = jax.random.normal(own_key, shape, jnp.float32) * deviation * loudness
    return jnp.minimum(jnp.maximum(array, -bound), bound).astype(kind)


def setup_inputs(seed: int = 0) -> dict:
    key_of = jax.random.split(jax.random.key(seed), 17)
    tokens = gaussian(key_of[0], (TOTAL_TOKENS, MODEL_DIM), 1.0, 6.0, ((0, 8),))
    positions = draw_positions(jax.random.fold_in(key_of[16], 71), 0)
    routes_keys = jax.random.split(jax.random.fold_in(key_of[2], 1), TOTAL_TOKENS // QR)
    routes_turns = jax.random.permutation(jax.random.fold_in(key_of[2], 3), TOTAL_TOKENS // QR)
    routes = jax.vmap(lambda own, number: shared_out(jax.random.fold_in(key_of[2], 2), own, number, QR, EXPERTS, TOPK, CAP, 1))(routes_keys, routes_turns).reshape((TOTAL_TOKENS, TOPK))
    query_weight = gaussian(key_of[3], (MODEL_DIM, QUERY_HEADS * HEAD_DIM), MODEL_DIM ** -0.5, 0.125, ((1, 4),))
    key_matrix = gaussian(key_of[4], (MODEL_DIM, KEY_VALUE_HEADS * HEAD_DIM), MODEL_DIM ** -0.5, 0.125, ((1, 4),))
    value_matrix = gaussian(key_of[5], (MODEL_DIM, KEY_VALUE_HEADS * HEAD_DIM), MODEL_DIM ** -0.5, 0.125, ((1, 4),))
    out_weight = gaussian(key_of[6], (QUERY_HEADS * HEAD_DIM, MODEL_DIM), (QUERY_HEADS * HEAD_DIM // 128) ** -0.5, 1.0, ((0, 4),))
    query_gain = jnp.clip(1.0 + 0.1 * jax.random.normal(key_of[7], (HEAD_DIM,), jnp.float32), 0.5, 1.5)
    key_gain = jnp.clip(1.0 + 0.1 * jax.random.normal(key_of[8], (HEAD_DIM,), jnp.float32), 0.5, 1.5)
    input_norm = jnp.clip(1.0 + 0.1 * jax.random.normal(key_of[9], (MODEL_DIM,), jnp.float32), 0.5, 1.5)
    post_norm = jnp.clip(1.0 + 0.1 * jax.random.normal(key_of[10], (MODEL_DIM,), jnp.float32), 0.5, 1.5)
    router = gaussian(key_of[11], (MODEL_DIM, EXPERTS), (4 * MODEL_DIM) ** -0.5, 0.0625)
    gate_weight = gaussian(key_of[12], (EXPERTS, MODEL_DIM, FF), MODEL_DIM ** -0.5, 0.125, ((0, 32),))
    up_weight = gaussian(key_of[13], (EXPERTS, MODEL_DIM, FF), MODEL_DIM ** -0.5, 0.125, ((0, 32),))
    down_weight = gaussian(key_of[14], (EXPERTS, FF, MODEL_DIM), (FF // 8) ** -0.5, 0.625, ((0, 32),))
    cotangent = gaussian(key_of[15], (TOTAL_TOKENS, MODEL_DIM), 1.0, 6.0, ((0, 32),))
    return dict(tokens=tokens, positions=positions, routes=routes, query_weight=query_weight, key_matrix=key_matrix, value_matrix=value_matrix, out_weight=out_weight, query_gain=query_gain, key_gain=key_gain, input_norm=input_norm, post_norm=post_norm, router=router, gate_weight=gate_weight, up_weight=up_weight, down_weight=down_weight, cotangent=cotangent)


@jax.custom_vjp
def reduced_copy(v):
    return lax.optimization_barrier(v.astype(jnp.bfloat16)).astype(jnp.float32)

@jax.custom_vjp
def reduced_backward(v):
    return v

def low_keep(v):
    return (reduced_copy(v), None)

def low_pass(kept, grad):
    return (grad,)

def back_keep(v):
    return (v, None)

def back_low(kept, grad):
    return (reduced_copy(grad),)
reduced_copy.defvjp(low_keep, low_pass)
reduced_backward.defvjp(back_keep, back_low)
EPSILON = 1e-06
EXACT_MODE = lax.Precision.HIGHEST

def norm_rows(values, gain):
    return values * lax.rsqrt(lax.optimization_barrier(jnp.mean(values * values, axis=-1, keepdims=True)) + EPSILON) * gain

def turn_half(values):
    half_dim = values.shape[-1] // 2
    return jnp.concatenate([-values[..., half_dim:], values[..., :half_dim]], axis=-1)

def rotate(values, cosine_table, sine_table):
    return values * cosine_table + turn_half(values) * sine_table

def angle_tables(positions, head_size):
    half_dim = head_size // 2
    frequency = jnp.exp(jnp.arange(half_dim, dtype=jnp.float32) * (-2.0 * math.log(1000000.0) / head_size))
    angles = positions.astype(jnp.float32)[:, None] * frequency[None, :]
    angles = jnp.concatenate([angles, angles], axis=-1)
    return (jnp.cos(angles)[:, None, :], jnp.sin(angles)[:, None, :])

def place_index(index_list, owners, part_len):
    owner_id = index_list // (2 * part_len)
    inner_id = index_list % part_len
    late_half = index_list % (2 * part_len) // part_len
    return jnp.where(late_half == 0, owner_id * part_len + inner_id, (2 * owners - 1 - owner_id) * part_len + inner_id)

def attend_sequence(queries, key_rows, value_rows, doc_start, places):
    seq_length = queries.shape[0]
    query_tile_block = min(512, seq_length)
    group_width = QUERY_HEADS // KEY_VALUE_HEADS
    scaling = 1.0 / math.sqrt(HEAD_DIM)

    def one_block(pieces):
        query_portion, start_part, place_part = pieces
        grouped_heads = query_portion.reshape(query_tile_block, KEY_VALUE_HEADS, group_width, HEAD_DIM)
        scores = jnp.einsum('qkgd,lkd->kgql', grouped_heads, key_rows, precision=EXACT_MODE) * scaling
        scores = reduced_backward(scores)
        visible = (places[None, :] <= place_part[:, None]) & (places[None, :] >= start_part[:, None])
        scores = jnp.where(visible[None, None], scores, -1e+30)
        row_max = lax.optimization_barrier(jnp.max(scores, axis=-1, keepdims=True))
        weights = jnp.exp(scores - row_max)
        weights = weights / lax.optimization_barrier(jnp.sum(weights, axis=-1, keepdims=True))
        attended = jnp.einsum('kgql,lkd->qkgd', reduced_copy(weights), value_rows, precision=EXACT_MODE)
        return attended.reshape(query_tile_block, QUERY_HEADS * HEAD_DIM)
    block_total = seq_length // query_tile_block
    pieces = (queries.reshape(block_total, query_tile_block, QUERY_HEADS, HEAD_DIM), doc_start.reshape(block_total, query_tile_block), places.reshape(block_total, query_tile_block))
    return lax.map(jax.checkpoint(one_block), pieces).reshape(seq_length, QUERY_HEADS * HEAD_DIM)

def by_sequence(values):
    shaped = values.reshape((N_CTX, SEQS, 2 * BLK) + values.shape[1:])
    return jnp.swapaxes(shaped, 0, 1).reshape((SEQS, LENGTH) + values.shape[1:])

def to_storage(values):
    shaped = values.reshape((SEQS, N_CTX, 2 * BLK) + values.shape[2:])
    return jnp.swapaxes(shaped, 0, 1).reshape((TOTAL_TOKENS,) + values.shape[2:])

def decoder_layer(tokens, query_weight, key_matrix, value_matrix, out_weight, query_gain, key_gain, input_norm, post_norm, router, gate_weight, up_weight, down_weight, positions, routes):
    attention_input = reduced_copy(norm_rows(tokens, input_norm))
    queries = reduced_backward(jnp.dot(attention_input, query_weight, precision=EXACT_MODE)).reshape(TOTAL_TOKENS, QUERY_HEADS, HEAD_DIM)
    keys_unnormed = reduced_backward(jnp.dot(attention_input, key_matrix, precision=EXACT_MODE)).reshape(TOTAL_TOKENS, KEY_VALUE_HEADS, HEAD_DIM)
    values_reduced = reduced_copy(reduced_backward(jnp.dot(attention_input, value_matrix, precision=EXACT_MODE))).reshape(TOTAL_TOKENS, KEY_VALUE_HEADS, HEAD_DIM)
    cosine_table, sine_table = angle_tables(positions, HEAD_DIM)
    query_rot = reduced_copy(rotate(norm_rows(queries, query_gain), cosine_table, sine_table))
    key_rot = reduced_copy(rotate(norm_rows(keys_unnormed, key_gain), cosine_table, sine_table))
    places = place_index(jnp.arange(LENGTH, dtype=jnp.int32), N_CTX, BLK)
    doc_start = places[None, :] - by_sequence(positions)
    seq_queries = by_sequence(query_rot)
    seq_keys = by_sequence(key_rot)
    seq_values = by_sequence(values_reduced)
    attended = jnp.stack([attend_sequence(seq_queries[s], seq_keys[s], seq_values[s], doc_start[s], places) for s in range(SEQS)])
    attended_low = reduced_copy(reduced_backward(to_storage(attended)))
    branch = reduced_backward(jnp.dot(attended_low, out_weight, precision=EXACT_MODE))
    hidden = tokens + branch
    ffn_input = reduced_copy(norm_rows(hidden, post_norm))
    logits = jnp.dot(ffn_input, router, precision=EXACT_MODE)
    chosen = jnp.take_along_axis(logits, routes, axis=1)
    gate_probs = jnp.exp(chosen - lax.optimization_barrier(jnp.max(chosen, axis=-1, keepdims=True)))
    gate_probs = gate_probs / lax.optimization_barrier(jnp.sum(gate_probs, axis=-1, keepdims=True))
    block_total = TOTAL_TOKENS // QR
    flat_routes = routes.reshape(block_total, QR * TOPK)
    route_hot = (flat_routes[..., None] == jnp.arange(EXPERTS, dtype=jnp.int32)).astype(jnp.int32)
    slot_index = lax.optimization_barrier(jnp.sum((jnp.cumsum(route_hot, axis=1) - 1) * route_hot, axis=-1))
    slot_rows = (jnp.arange(block_total, dtype=jnp.int32)[:, None] * CAP + slot_index).reshape(-1)
    expert_ids = flat_routes.reshape(-1)
    token_ids = jnp.arange(TOTAL_TOKENS * TOPK, dtype=jnp.int32) // TOPK
    slot_table = jnp.full((EXPERTS, block_total * CAP), TOTAL_TOKENS, jnp.int32).at[expert_ids, slot_rows].set(token_ids)
    padded = jnp.concatenate([ffn_input, jnp.zeros((1, MODEL_DIM), jnp.float32)], axis=0)
    rows_in = reduced_backward(padded[slot_table])
    gate_part = reduced_backward(jnp.einsum('erd,edf->erf', rows_in, gate_weight, precision=EXACT_MODE))
    up_part = reduced_backward(jnp.einsum('erd,edf->erf', rows_in, up_weight, precision=EXACT_MODE))
    activation = reduced_copy(jax.nn.silu(gate_part) * up_part)
    rows_out = reduced_copy(reduced_backward(jnp.einsum('erf,efd->erd', activation, down_weight, precision=EXACT_MODE)))
    picked = rows_out[expert_ids, slot_rows].reshape(TOTAL_TOKENS, TOPK, MODEL_DIM)
    return hidden + lax.optimization_barrier(jnp.sum(gate_probs[..., None] * picked, axis=1))

def reference(tokens, positions, routes, query_weight, key_matrix, value_matrix, out_weight, query_gain, key_gain, input_norm, post_norm, router, gate_weight, up_weight, down_weight, cotangent):
    floats = [a.astype(jnp.float32) for a in (tokens, query_weight, key_matrix, value_matrix, out_weight, query_gain, key_gain, input_norm, post_norm, router, gate_weight, up_weight, down_weight)]

    def forward(*weights_in):
        return decoder_layer(*weights_in, positions, routes)
    result, pullback = jax.vjp(forward, *floats)
    gradients = pullback(cotangent.astype(jnp.float32))
    return (result.astype(jnp.bfloat16), gradients[0].astype(jnp.bfloat16), gradients[1], gradients[2], gradients[3], gradients[4], gradients[5], gradients[6], gradients[7], gradients[8], gradients[9], gradients[10], gradients[11], gradients[12])
```

```python
import math

import jax
import jax.numpy as jnp
import numpy as np
from jax import lax
from jax.sharding import PartitionSpec as P

SEQS = 2


EPSILON = 1e-06
EXACT_MODE = lax.Precision.HIGHEST


def norm_stats(values):
    return lax.rsqrt(jnp.mean(values * values, axis=-1, keepdims=True) + EPSILON)


def norm_backward(grad_normed, normed, inverse, gain):
    scaled = grad_normed * gain
    return inverse * (scaled - normed * jnp.mean(scaled * normed, axis=-1, keepdims=True))


def turn_half(values):
    half_dim = values.shape[-1] // 2
    return jnp.concatenate([-values[..., half_dim:], values[..., :half_dim]], axis=-1)


def turn_back(values):
    half_dim = values.shape[-1] // 2
    return jnp.concatenate([values[..., half_dim:], -values[..., :half_dim]], axis=-1)


def angle_tables(positions, head_size):
    half_dim = head_size // 2
    frequency = jnp.exp(
        jnp.arange(half_dim, dtype=jnp.float32) * (-2.0 * math.log(1000000.0) / head_size)
    )
    angles = positions.astype(jnp.float32)[:, None] * frequency[None, :]
    angles = jnp.concatenate([angles, angles], axis=-1)
    return (jnp.cos(angles)[:, None, :], jnp.sin(angles)[:, None, :])


def place_index(index_list, owners, part_len):
    owner_id = index_list // (2 * part_len)
    inner_id = index_list % part_len
    late_half = index_list % (2 * part_len) // part_len
    return jnp.where(
        late_half == 0,
        owner_id * part_len + inner_id,
        (2 * owners - 1 - owner_id) * part_len + inner_id,
    )


def contract_last(left, right):
    return lax.dot_general(
        left, right, (((1,), (1,)), ((), ())), preferred_element_type=jnp.float32
    )


def contract_first(left, right):
    return lax.dot_general(
        left, right, (((0,), (0,)), ((), ())), preferred_element_type=jnp.float32
    )


def xor_permute(value, axis, offset):
    if isinstance(axis, str):
        count = lax.axis_size(axis)
    else:
        count = math.prod(lax.axis_size(name) for name in axis)
    return lax.ppermute(value, axis, [(i, i ^ offset) for i in range(count)])


def xor_reorder(blocks, index):
    count = blocks.shape[0]
    bit = 1
    while bit < count:
        shaped = blocks.reshape((count // (2 * bit), 2, bit) + blocks.shape[1:])
        flipped = jnp.concatenate([shaped[:, 1:], shaped[:, :1]], axis=1)
        blocks = jnp.where((index // bit) % 2 == 1, flipped, shaped).reshape(blocks.shape)
        bit *= 2
    return blocks


def gather_wa(value):
    wa_count = lax.axis_size("wa")
    blocks = [value] + [xor_permute(value, "wa", k) for k in range(1, wa_count)]
    return xor_reorder(jnp.stack(blocks), lax.axis_index("wa")).reshape(
        (-1,) + value.shape[1:]
    )


def scatter_wa(partial, quarter):
    wa_count = lax.axis_size("wa")
    wa_id = lax.axis_index("wa")
    total = lax.dynamic_slice_in_dim(partial, wa_id * quarter, quarter, 0).astype(jnp.float32)
    for k in range(1, wa_count):
        piece = lax.dynamic_slice_in_dim(partial, (wa_id ^ k) * quarter, quarter, 0)
        total = total + xor_permute(piece.astype(jnp.bfloat16), "wa", k).astype(jnp.float32)
    return total


def lead_offsets(ctx_count):
    return [j * (ctx_count // 4) for j in range(1, 4)]


def low_bits(ctx_count):
    bits, bit = [], 1
    while bit < ctx_count // 4:
        bits.append(bit)
        bit *= 2
    return bits


def gather_steps(value, steps):
    held, offsets = value, [0]
    wa_count = lax.axis_size("wa")
    for axis, partners in steps:
        unit = wa_count if axis == "ctx" else 1
        held = jnp.concatenate([held] + [xor_permute(held, axis, k) for k in partners], axis=0)
        offsets = offsets + [o ^ (k * unit) for k in partners for o in offsets]
    return held, offsets


def gather_ctx(value, lead_first):
    ctx_count = lax.axis_size("ctx")
    lead = [("ctx", lead_offsets(ctx_count))]
    low = [("ctx", [bit]) for bit in low_bits(ctx_count)]
    held, offsets = gather_steps(value, lead + low if lead_first else low + lead)
    order = np.argsort(np.array(offsets))
    rows = value.shape[0]
    return jnp.concatenate([held[i * rows : (i + 1) * rows] for i in order], axis=0)


def exchange_ctx(pieces):
    return [pieces[0]] + [xor_permute(pieces[k], "ctx", k) for k in range(1, len(pieces))]


def on_device(
    tokens,
    positions,
    routes,
    query_weight,
    key_matrix,
    value_matrix,
    out_weight,
    query_gain,
    key_gain,
    input_norm,
    post_norm,
    router,
    gate_weight,
    up_weight,
    down_weight,
    cotangent,
):
    ctx_count = lax.axis_size("ctx")
    wa_count = lax.axis_size("wa")
    ctx_id = lax.axis_index("ctx")
    wa_id = lax.axis_index("wa")
    device_id = ctx_id * wa_count + wa_id
    row_count, model_width = tokens.shape
    seq_span = row_count // SEQS
    part_len = seq_span // 2
    quarter = row_count // wa_count
    head_size = query_gain.shape[0]
    head_count = query_weight.shape[1] // head_size
    seq_length = seq_span * ctx_count
    scaling = 1.0 / math.sqrt(head_size)
    expert_count = router.shape[1]
    top_count = routes.shape[1]
    devices = ctx_count * wa_count
    rest = ctx_count // 4
    planes = rest * wa_count
    capacity = max(2, (5 * quarter * top_count + 4 * expert_count - 1) // (4 * expert_count))
    slot_rows = devices * capacity
    bf16, f32 = jnp.bfloat16, jnp.float32

    route_low = jnp.pad(routes.astype(bf16), ((0, 0), (0, 128 - top_count)))
    cot_payload = jnp.concatenate([cotangent, route_low], axis=1)
    cot_all = lax.all_gather(cot_payload, ("ctx", "wa"), axis=0, tiled=True)

    tokens_wide = tokens.astype(f32)
    inv_in = norm_stats(tokens_wide)
    normed_in = tokens_wide * inv_in
    attention_input = (normed_in * input_norm).astype(bf16)
    keys_unnormed = jnp.dot(attention_input, key_matrix, preferred_element_type=f32)
    values_low = jnp.dot(attention_input, value_matrix, preferred_element_type=f32).astype(bf16)
    cosine_table, sine_table = angle_tables(positions, head_size)
    cosine_flat, sine_flat = cosine_table[:, 0], sine_table[:, 0]
    inv_key = norm_stats(keys_unnormed)
    normed_key = keys_unnormed * inv_key
    scaled_key = normed_key * key_gain
    key_rot = (scaled_key * cosine_flat + turn_half(scaled_key) * sine_flat).astype(bf16)
    keys_all = gather_ctx(key_rot, True)
    values_all = gather_ctx(values_low, False)
    queries_raw = jnp.dot(attention_input, query_weight, preferred_element_type=f32).reshape(
        row_count, head_count, head_size
    )
    inv_query = norm_stats(queries_raw)
    normed_query = queries_raw * inv_query
    scaled_query = normed_query * query_gain
    query_rot = (scaled_query * cosine_table + turn_half(scaled_query) * sine_table).astype(bf16)

    width_part = model_width // ctx_count
    input_pieces = exchange_ctx(
        [
            lax.dynamic_slice_in_dim(attention_input, (ctx_id ^ k) * width_part, width_part, 1)
            for k in range(ctx_count)
        ]
    )
    input_columns = jnp.concatenate(input_pieces, axis=0)

    block_ctx = ctx_id ^ jnp.arange(ctx_count, dtype=jnp.int32)
    local = jnp.arange(seq_span, dtype=jnp.int32)
    key_places = place_index(
        (block_ctx[:, None] * seq_span + local[None, :]).reshape(-1), ctx_count, part_len
    )
    query_places = place_index(ctx_id * seq_span + local, ctx_count, part_len)
    doc_start = query_places[None, :] - positions.reshape(SEQS, seq_span)
    visible = (key_places[None, None, :] <= query_places[None, :, None]) & (
        key_places[None, None, :] >= doc_start[:, :, None]
    )
    by_head = query_rot.reshape(SEQS, seq_span, head_count, head_size).transpose(0, 2, 1, 3)

    def of_sequence(gathered):
        shaped = gathered.reshape(ctx_count, SEQS, seq_span, head_size)
        return shaped.transpose(1, 0, 2, 3).reshape(SEQS, seq_length, head_size)

    keys_seq, values_seq = of_sequence(keys_all), of_sequence(values_all)
    scores = jnp.einsum("shqd,sld->shql", by_head, keys_seq, preferred_element_type=f32) * scaling
    scores = jnp.where(visible[:, None], scores, -1e30)
    top_score = jnp.max(scores, axis=-1, keepdims=True)
    weights = jnp.exp(scores - top_score)
    weights = weights / jnp.sum(weights, axis=-1, keepdims=True)
    weights_low = weights.astype(bf16)
    attended = jnp.einsum("shql,sld->shqd", weights_low, values_seq, preferred_element_type=f32)
    attended_low = (
        attended.transpose(0, 2, 1, 3).reshape(row_count, head_count * head_size).astype(bf16)
    )
    attended_all = lax.all_gather(attended_low, "ctx", axis=0, tiled=True)
    row_start = wa_id * quarter
    branch = scatter_wa(
        jnp.dot(attended_low, out_weight, preferred_element_type=f32).astype(bf16), quarter
    )
    hidden = lax.dynamic_slice_in_dim(tokens_wide, row_start, quarter, 0) + branch
    inv_post = norm_stats(hidden)
    normed_post = hidden * inv_post
    ffn_input = (normed_post * post_norm).astype(bf16)

    lead_step = [("ctx", lead_offsets(ctx_count))]
    low_steps = [("ctx", [bit]) for bit in low_bits(ctx_count)]
    x_steps = [("wa", [bit]) for bit in (2,) if wa_count == 4]
    core_step = [("wa", [1])]
    cut_a, cut_b = 3 * model_width // 8, 3 * model_width // 4
    ffn_pieces = [
        gather_steps(ffn_input[:, :cut_a], lead_step + low_steps + x_steps + core_step),
        gather_steps(ffn_input[:, cut_a:cut_b], lead_step + x_steps + low_steps + core_step),
        gather_steps(ffn_input[:, cut_b:], x_steps + low_steps + lead_step + core_step),
    ]

    cot_rows_all = cot_all[:, :model_width]
    routes_all = cot_all[:, model_width : model_width + top_count].astype(jnp.int32)
    routes_blocks = routes_all.reshape(devices, quarter, top_count)
    expert_range = jnp.arange(expert_count, dtype=jnp.int32)
    triangle = (
        jnp.arange(quarter)[:, None] >= jnp.arange(quarter)[None, :]
    ).astype(bf16)

    def dense_slots(block_routes):
        hot = jnp.any(block_routes[..., None] == expert_range, axis=-2)
        counts = jnp.einsum(
            "ut,bte->bue", triangle, hot.astype(bf16), preferred_element_type=f32
        )
        return hot, jnp.where(hot, counts - 1.0, -1.0)

    named = jnp.any(routes_blocks == device_id, axis=-1)
    named_counts = jnp.dot(named.astype(bf16), triangle.T, preferred_element_type=f32)
    slot_nat = jnp.where(named, named_counts - 1.0, -1.0).astype(jnp.int32)
    offset_nat = jnp.arange(devices, dtype=jnp.int32) ^ device_id

    def block_place(offset):
        ctx_part, wa_part = offset // wa_count, offset % wa_count
        return ((ctx_part % rest) * wa_count + wa_part) * 4 + ctx_part // rest

    target_nat = jnp.where(slot_nat >= 0, block_place(offset_nat)[:, None] * capacity + slot_nat, -1)
    target_xor = xor_reorder(target_nat, device_id)
    row_range = jnp.arange(slot_rows, dtype=jnp.int32)

    def pick_matrix(targets):
        return (targets.reshape(-1)[None, :] == row_range[:, None]).astype(bf16)

    pick_nat = pick_matrix(target_nat)
    cot_rows = jnp.dot(pick_nat, cot_rows_all, preferred_element_type=f32).astype(bf16)
    hot_all = jnp.any(routes_all[..., None] == expert_range, axis=-2)
    row_hot = jnp.dot(pick_nat, hot_all.astype(bf16), preferred_element_type=f32) > 0.5
    down_weight, gate_weight, up_weight = down_weight[0], gate_weight[0], up_weight[0]
    grad_activation_raw = contract_last(cot_rows, down_weight)

    rows_in = jnp.concatenate(
        [
            jnp.dot(
                pick_matrix(jnp.stack([target_xor[o] for o in offsets])),
                held,
                preferred_element_type=f32,
            ).astype(bf16)
            for held, offsets in ffn_pieces
        ],
        axis=1,
    )

    def chosen_softmax(hot, logits):
        masked = jnp.where(hot, logits, -1e30)
        exps = jnp.where(hot, jnp.exp(logits - jnp.max(masked, axis=-1, keepdims=True)), 0.0)
        total = jnp.sum(exps, axis=-1, keepdims=True)
        return exps / jnp.where(total > 0.0, total, 1.0)

    row_logits = jnp.dot(rows_in, router, preferred_element_type=f32)
    row_probs = chosen_softmax(row_hot, row_logits)
    own_expert = expert_range[None, :] == device_id
    row_prob = jnp.sum(jnp.where(own_expert, row_probs, 0.0), axis=-1, keepdims=True)
    gate_part = jnp.dot(rows_in, gate_weight, preferred_element_type=f32)
    up_part = jnp.dot(rows_in, up_weight, preferred_element_type=f32)
    sig_gate = jax.nn.sigmoid(gate_part)
    lifted = gate_part * sig_gate
    activation = (lifted * up_part).astype(bf16)
    expert_out = jnp.dot(activation, down_weight, preferred_element_type=f32).astype(bf16)
    grad_gate_rows = jnp.sum(
        cot_rows.astype(f32) * expert_out.astype(f32), axis=-1, keepdims=True
    )
    grad_activation = row_prob * grad_activation_raw
    grad_gate_part = (
        grad_activation * up_part * sig_gate * (1.0 + gate_part * (1.0 - sig_gate))
    ).astype(bf16)
    grad_up_part = (grad_activation * lifted).astype(bf16)
    grad_expert_in = (
        contract_last(grad_gate_part, gate_weight) + contract_last(grad_up_part, up_weight)
    ).astype(bf16)
    gate_high = grad_gate_rows.astype(bf16).astype(f32)
    gate_low = grad_gate_rows - gate_high
    extra = jnp.concatenate(
        [jnp.where(own_expert, gate_high, 0.0), jnp.where(own_expert, gate_low, 0.0)], axis=1
    ).astype(bf16)
    extra = jnp.pad(extra, ((0, 0), (0, -extra.shape[1] % 128)))

    lead_units = [0] + [k * wa_count for k in lead_offsets(ctx_count)]
    lead_routes = xor_reorder(routes_blocks, device_id)
    lead_routes = jnp.stack([lead_routes[k] for k in lead_units])
    lead_hot, lead_slots = dense_slots(lead_routes)
    own_routes_hot = lead_hot[0]
    plane_experts = device_id ^ (row_range // (4 * capacity))
    spread = (expert_range[:, None] == plane_experts[None, :]).astype(bf16)
    slot_of_row = jnp.dot(
        lead_slots.reshape(4 * quarter, expert_count).astype(bf16),
        spread,
        preferred_element_type=f32,
    )
    lead_of_token = jnp.arange(4 * quarter, dtype=jnp.int32) // quarter
    combine = (
        (slot_of_row == (row_range % capacity).astype(f32)[None, :])
        & (lead_of_token[:, None] == (row_range // capacity % 4)[None, :])
    ).astype(bf16)

    def send_back(rows):
        group = 4 * capacity
        arrived = [rows[:group]] + [
            xor_permute(rows[k * group : (k + 1) * group], ("ctx", "wa"), k)
            for k in range(1, planes)
        ]
        summed = jnp.dot(
            combine, jnp.concatenate(arrived, axis=0), preferred_element_type=f32
        )
        total = summed[:quarter]
        for j, k in enumerate(lead_offsets(ctx_count), start=1):
            piece = summed[j * quarter : (j + 1) * quarter].astype(bf16)
            total = total + xor_permute(piece, "ctx", k).astype(f32)
        return total

    returned = send_back(jnp.concatenate([grad_expert_in, extra], axis=1))
    grad_ffn = returned[:, :model_width]
    grad_gate = (
        returned[:, model_width : model_width + expert_count]
        + returned[:, model_width + expert_count : model_width + 2 * expert_count]
    )
    gate_probs = chosen_softmax(
        own_routes_hot, jnp.dot(ffn_input, router, preferred_element_type=f32)
    )
    grad_logits = gate_probs * (
        grad_gate - jnp.sum(gate_probs * grad_gate, axis=-1, keepdims=True)
    )
    grad_ffn = grad_ffn + lax.dot_general(
        grad_logits, router.astype(f32), (((1,), (1,)), ((), ())), precision=EXACT_MODE
    )
    grad_post_part = jnp.sum(grad_ffn * normed_post, axis=0)
    grad_out = cotangent.astype(f32)
    grad_hidden = grad_out + norm_backward(grad_ffn, normed_post, inv_post, post_norm)
    grad_branch = gather_wa(grad_hidden.astype(bf16))
    grad_attended = contract_last(grad_branch, out_weight).astype(bf16)
    grad_heads = grad_attended.reshape(SEQS, seq_span, head_count, head_size).transpose(0, 2, 1, 3)

    delta = jnp.sum(grad_heads.astype(f32) * attended, axis=-1, keepdims=True)
    grad_weights = jnp.einsum(
        "shqd,sld->shql", grad_heads, values_seq, preferred_element_type=f32
    )
    grad_scores = (weights_low.astype(f32) * (grad_weights - delta)).astype(bf16)
    grad_values_part = jnp.einsum(
        "shql,shqd->sld", weights_low, grad_heads, preferred_element_type=f32
    )
    grad_keys_part = (
        jnp.einsum("shql,shqd->sld", grad_scores, by_head, preferred_element_type=f32) * scaling
    )
    grad_query_rot = (
        jnp.einsum("shql,sld->shqd", grad_scores, keys_seq, preferred_element_type=f32) * scaling
    )
    grad_kv = jnp.concatenate([grad_keys_part, grad_values_part], axis=-1).astype(bf16)
    grad_kv = grad_kv.reshape(SEQS, ctx_count, seq_span, 2 * head_size)
    grad_kv = [
        piece.astype(f32)
        for piece in exchange_ctx(
            [grad_kv[:, k].reshape(row_count, 2 * head_size) for k in range(ctx_count)]
        )
    ]
    grad_kv_own = sum(grad_kv[1:], grad_kv[0])
    grad_values_low = grad_kv_own[:, head_size:].astype(bf16)
    grad_key_rot = grad_kv_own[:, :head_size]
    grad_key_normed = grad_key_rot * cosine_flat + turn_back(grad_key_rot * sine_flat)
    grad_key_gain_part = jnp.sum(grad_key_normed * normed_key, axis=0)
    grad_keys_low = norm_backward(grad_key_normed, normed_key, inv_key, key_gain).astype(bf16)
    grad_query_rot = grad_query_rot.transpose(0, 2, 1, 3).reshape(
        row_count, head_count, head_size
    )
    grad_query_normed = grad_query_rot * cosine_table + turn_back(grad_query_rot * sine_table)
    grad_query_gain_part = jnp.sum(grad_query_normed * normed_query, axis=(0, 1))
    grad_queries_low = (
        norm_backward(grad_query_normed, normed_query, inv_query, query_gain)
        .reshape(row_count, -1)
        .astype(bf16)
    )
    half = grad_queries_low.shape[1] // 2
    queries_first = gather_ctx(grad_queries_low[:, :half], True)
    queries_second = gather_ctx(grad_queries_low[:, half:], False)
    grad_in_part = (
        contract_last(grad_queries_low, query_weight)
        + contract_last(grad_keys_low, key_matrix)
        + contract_last(grad_values_low, value_matrix)
    )
    grad_in = scatter_wa(grad_in_part.astype(bf16), quarter)
    kv_all = gather_ctx(jnp.concatenate([grad_keys_low, grad_values_low], axis=1), True)
    own_inv = lax.dynamic_slice_in_dim(inv_in, row_start, quarter, 0)
    own_normed = lax.dynamic_slice_in_dim(normed_in, row_start, quarter, 0)
    grad_input_part = jnp.sum(grad_in * own_normed, axis=0)
    grad_tokens = gather_wa(
        (grad_hidden + norm_backward(grad_in, own_normed, own_inv, input_norm)).astype(bf16)
    )
    grad_query_weight = jnp.concatenate(
        [contract_first(input_columns, queries_first), contract_first(input_columns, queries_second)],
        axis=1,
    )
    grad_kv_weight = contract_first(input_columns, kv_all)
    grad_key_weight, grad_value_weight = (
        grad_kv_weight[:, :head_size],
        grad_kv_weight[:, head_size:],
    )

    branch_pieces = exchange_ctx(
        [
            lax.dynamic_slice_in_dim(grad_branch, (ctx_id ^ k) * width_part, width_part, 1)
            for k in range(ctx_count)
        ]
    )
    branch_columns = xor_reorder(jnp.stack(branch_pieces), ctx_id).reshape(-1, width_part)
    grad_out_weight = contract_first(attended_all, branch_columns)
    grad_rows = (row_prob * cot_rows.astype(f32)).astype(bf16)
    grad_down_weight = contract_first(activation, grad_rows)
    grad_gate_weight = contract_first(rows_in, grad_gate_part)
    grad_up_weight = contract_first(rows_in, grad_up_part)
    gated_out, _ = lax.optimization_barrier(
        ((row_prob * expert_out.astype(f32)).astype(bf16), grad_branch)
    )
    output = (hidden + send_back(gated_out)).astype(bf16)

    grad_router_part = lax.dot_general(
        ffn_input.astype(f32), grad_logits, (((0,), (0,)), ((), ())), precision=EXACT_MODE
    )
    router_rows = model_width // devices
    first_sums = jnp.concatenate(
        [
            grad_router_part.reshape(devices, router_rows * expert_count),
            grad_post_part.reshape(devices, router_rows),
        ],
        axis=1,
    )
    first_sums = jnp.sum(
        lax.all_to_all(first_sums, ("ctx", "wa"), split_axis=0, concat_axis=0, tiled=True), axis=0
    )
    first_all = lax.all_to_all(
        jnp.broadcast_to(first_sums[None], (devices,) + first_sums.shape),
        ("ctx", "wa"),
        split_axis=0,
        concat_axis=0,
        tiled=True,
    )
    grad_router = first_all[:, : router_rows * expert_count].reshape(model_width, expert_count)
    grad_post_norm = first_all[:, router_rows * expert_count :].reshape(model_width)

    gains = jnp.concatenate([grad_query_gain_part, grad_key_gain_part])
    last_sums = jnp.concatenate(
        [
            jnp.repeat(grad_input_part.reshape(ctx_count, width_part), wa_count, axis=0),
            jnp.broadcast_to(gains[None], (devices, 2 * head_size)),
        ],
        axis=1,
    )
    last_sums = jnp.sum(
        lax.all_to_all(last_sums, ("ctx", "wa"), split_axis=0, concat_axis=0, tiled=True), axis=0
    )
    grad_input_norm = last_sums[:width_part]
    grad_query_gain = last_sums[width_part : width_part + head_size]
    grad_key_gain = last_sums[width_part + head_size :]
    return (
        output,
        grad_tokens,
        grad_query_weight,
        grad_key_weight,
        grad_value_weight,
        grad_out_weight,
        grad_query_gain,
        grad_key_gain,
        grad_input_norm,
        grad_post_norm,
        grad_router,
        grad_gate_weight[None],
        grad_up_weight[None],
        grad_down_weight[None],
    )


def solution(mesh):
    return jax.shard_map(
        on_device,
        mesh=mesh,
        in_specs=(
            P("ctx", None),
            P("ctx"),
            P(("ctx", "wa"), None),
            P(None, "wa"),
            P(None, "wa"),
            P(None, "wa"),
            P("wa", None),
            P(),
            P(),
            P(),
            P(),
            P(),
            P(("ctx", "wa"), None, None),
            P(("ctx", "wa"), None, None),
            P(("ctx", "wa"), None, None),
            P(("ctx", "wa"), None),
        ),
        out_specs=(
            P(("ctx", "wa"), None),
            P("ctx", None),
            P("ctx", "wa"),
            P("ctx", "wa"),
            P("ctx", "wa"),
            P("wa", "ctx"),
            P(),
            P(),
            P("ctx"),
            P(),
            P(),
            P(("ctx", "wa"), None, None),
            P(("ctx", "wa"), None, None),
            P(("ctx", "wa"), None, None),
        ),
        check_vma=False,
    )
```

```python
import math

import jax
import jax.numpy as jnp
import numpy as np
from jax import lax
from jax.experimental import pallas as pl
from jax.experimental.pallas import tpu as pltpu
from jax.sharding import Mesh
from jax.sharding import PartitionSpec as P

SEQS = 2


EPSILON = 1e-06
BF16, F32, I32 = jnp.bfloat16, jnp.float32, jnp.int32


def dot(left, right):
    return jnp.dot(left, right, preferred_element_type=F32)


def contract_last(left, right):
    return lax.dot_general(
        left, right, (((1,), (1,)), ((), ())), preferred_element_type=F32
    )


def contract_first(left, right):
    return lax.dot_general(
        left, right, (((0,), (0,)), ((), ())), preferred_element_type=F32
    )


def split_low(values):
    high = values.astype(BF16)
    return high, (values - high.astype(F32)).astype(BF16)


def norm_stats(values):
    return lax.rsqrt(jnp.mean(values * values, axis=-1, keepdims=True) + EPSILON)


def norm_backward(grad_normed, normed, inverse, gain):
    scaled = grad_normed * gain
    return inverse * (scaled - normed * jnp.mean(scaled * normed, axis=-1, keepdims=True))


def half_turn(values):
    return pltpu.roll(values, values.shape[-1] // 2, values.ndim - 1)


def angle_tables(positions, head_size):
    half_dim = head_size // 2
    frequency = jnp.exp(
        jnp.arange(half_dim, dtype=F32) * (-2.0 * math.log(1000000.0) / head_size)
    )
    angles = positions.astype(F32)[:, None] * frequency[None, :]
    cosine, sine = jnp.cos(angles), jnp.sin(angles)
    return (
        jnp.concatenate([cosine, cosine], axis=-1),
        jnp.concatenate([-sine, sine], axis=-1),
    )


def xor_permute(value, axis, offset):
    names = (axis,) if isinstance(axis, str) else axis
    count = math.prod(lax.axis_size(name) for name in names)
    return lax.ppermute(value, axis, [(i, i ^ offset) for i in range(count)])


def exchange(pieces, axis):
    return [pieces[0]] + [xor_permute(pieces[k], axis, k) for k in range(1, len(pieces))]


def gather_ctx_pieces(value):
    low_count = lax.axis_size("low")
    held = {j * low_count: v for j, v in enumerate(exchange([value] * 4, "lead"))}
    bit = 1
    while bit < low_count:
        held.update({k ^ bit: xor_permute(v, "low", bit) for k, v in list(held.items())})
        bit *= 2
    return [held[k] for k in range(4 * low_count)]


def gather_wa_pieces(value):
    over = xor_permute(value, "wa", 2)
    return [value, xor_permute(value, "wa", 1), over, xor_permute(over, "wa", 1)]


def gather(value, axis):
    return lax.all_gather(value, axis, axis=0, tiled=True)


def swap(value, axes):
    return lax.all_to_all(value, axes, split_axis=0, concat_axis=0, tiled=True)


class Incoming:
    def __init__(self, ref, copies):
        self.ref, self.copies = ref, dict(enumerate(copies))
        self.step = ref.shape[-1] // len(copies)
        self.shape, self.dtype, self.ndim = ref.shape, ref.dtype, ref.ndim

    def ready(self):
        for k in list(self.copies):
            self.copies.pop(k).wait()
        return self.ref

    def part(self, k):
        if k in self.copies:
            self.copies.pop(k).wait()
        return self.ref[:, k * self.step : (k + 1) * self.step]

    def __getitem__(self, index):
        return self.ready()[index]


class Outgoing:
    def __init__(self, ref, copies):
        self.ref, self.copies, self.sent = ref, copies, set()
        self.shape, self.dtype, self.ndim = ref.shape, ref.dtype, ref.ndim

    def send(self, part=None):
        for k, copy in enumerate(self.copies):
            if k not in self.sent and part in (None, k):
                copy.start()
                self.sent.add(k)

    def __getitem__(self, index):
        return self.ref[index]

    def __setitem__(self, index, value):
        self.ref[index] = value


class Near:
    def __init__(self, value):
        self.value = value


class Rows:
    def __init__(self, value, first, count):
        self.value, self.first, self.count = value, first, count


def near(values):
    return [Near(value) for value in values]


def vcall(body, outs, *operands, scratch=(), after=(), split=None, flops=0, megabytes=24):
    split = split or {}
    close = [isinstance(o, Near) for o in operands]
    ranges = {i: (o.first, o.count) for i, o in enumerate(operands) if isinstance(o, Rows)}
    operands = [o.value if isinstance(o, (Near, Rows)) else o for o in operands]
    close_out = [len(o) > 2 for o in outs]
    outs = [o[:2] for o in outs]
    places = [i for i, o in enumerate(operands) if o.ndim > 1 and not close[i]]
    far_outs = [i for i, c in enumerate(close_out) if not c]
    arrays = [
        jax.ShapeDtypeStruct((ranges[i][1],) + operands[i].shape[1:], operands[i].dtype)
        if i in ranges
        else operands[i]
        for i in places
    ]
    sizes = [o.size * o.dtype.itemsize for o in arrays]
    in_parts = [split.get(i, 1) for i in places]
    out_parts = [split.get(-1 - i, 1) for i in far_outs]
    count = len(arrays)

    def kernel(*refs):
        given = list(refs[: len(operands)])
        rest = refs[len(operands) + len(after) :]
        results, rest = rest[: len(outs)], rest[len(outs) :]
        inner = count + len(far_outs)
        buffers, sems, own = rest[:inner], rest[inner], rest[inner + 1 :]
        used = 0
        incoming = []
        for k, i in enumerate(places):
            source, target, parts = given[i], buffers[k], in_parts[k]
            if i in ranges:
                source = source.at[pl.ds(*ranges[i])]
            copies = []
            for c in range(parts):
                step = source.shape[-1] // parts
                if parts > 1:
                    piece = (slice(None), pl.ds(c * step, step))
                    copy = pltpu.make_async_copy(source.at[piece], target.at[piece], sems.at[used])
                else:
                    copy = pltpu.make_async_copy(source, target, sems.at[used])
                copies.append(copy)
                used += 1
            incoming.append(copies)
            given[i] = Incoming(target, copies)
        for c in range(max(in_parts, default=0)):
            for k in sorted(range(count), key=lambda k: sizes[k] / in_parts[k]):
                if c < in_parts[k]:
                    incoming[k][c].start()
        leaving = [Outgoing(result, []) for result in results]
        for k, i in enumerate(far_outs):
            result, source, parts = results[i], buffers[count + k], out_parts[k]
            copies = []
            for c in range(parts):
                step = result.shape[0] // parts
                if parts > 1:
                    piece = pl.ds(c * step, step)
                    copy = pltpu.make_async_copy(source.at[piece], result.at[piece], sems.at[used])
                else:
                    copy = pltpu.make_async_copy(source, result, sems.at[used])
                copies.append(copy)
                used += 1
            leaving[i] = Outgoing(source, copies)
        body(*given, *leaving, *own)
        for value in given:
            if isinstance(value, Incoming):
                value.ready()
        for value in leaving:
            value.send()
        for value in leaving:
            for copy in value.copies:
                copy.wait()

    moved = sum(sizes) + sum(math.prod(s) * jnp.dtype(d).itemsize for s, d in outs)
    in_hbm = pl.BlockSpec(memory_space=pltpu.HBM)

    def pinned(value):
        return pltpu.with_memory_space_constraint(value, pltpu.HBM)

    return pl.pallas_call(
        kernel,
        out_shape=[
            jax.ShapeDtypeStruct(s, d) if c else pltpu.HBM(s, d)
            for (s, d), c in zip(outs, close_out)
        ],
        in_specs=[
            pl.BlockSpec(memory_space=pltpu.SMEM)
            if o.ndim == 1
            else (pl.BlockSpec(memory_space=pltpu.VMEM) if c else in_hbm)
            for o, c in zip(operands, close)
        ]
        + [in_hbm] * len(after),
        out_specs=[pl.BlockSpec(memory_space=pltpu.VMEM) if c else in_hbm for c in close_out],
        scratch_shapes=[pltpu.VMEM(o.shape, o.dtype) for o in arrays]
        + [pltpu.VMEM(*outs[i]) for i in far_outs]
        + [pltpu.SemaphoreType.DMA((max(1, sum(in_parts) + sum(out_parts)),))]
        + list(scratch),
        compiler_params=pltpu.CompilerParams(vmem_limit_bytes=megabytes << 20),
        cost_estimate=pl.CostEstimate(flops=flops, bytes_accessed=moved, transcendentals=0),
    )(*[pinned(o) if i in places else o for i, o in enumerate(operands)], *[pinned(o) for o in after])


def as_column(row):
    count = row.shape[1]
    here = row_index((count, count)) == lane_index((count, count))
    return jnp.sum(jnp.where(here, row.astype(F32), 0.0), axis=-1, keepdims=True)


def lane_index(shape):
    return lax.broadcasted_iota(I32, shape, len(shape) - 1)


def row_index(shape):
    return lax.broadcasted_iota(I32, shape, len(shape) - 2)


def kv_kernel(tok, gain, wk, wv, cos, sin, key_gain, a_out, kv_out, raw_out):
    wide = tok[...].astype(F32)
    low = (wide * norm_stats(wide) * gain[...]).astype(BF16)
    a_out[...] = low
    size = wk.shape[1]
    raw = dot(low, wk[...])
    raw_out[...] = raw
    scaled = raw * norm_stats(raw) * key_gain[...]
    kv_out[:, :size] = (scaled * cos[...] + half_turn(scaled) * sin[...]).astype(BF16)
    kv_out[:, size:] = dot(low, wv[...]).astype(BF16)


def query_kernel(a, wq, cos, sin, query_gain, q_out, raw_out):
    size = cos.shape[1]
    span = a.shape[0] // SEQS
    for h in range(wq.shape[1] // size):
        if h % 2 == 0:
            pair = dot(a[...], wq[:, h * size : (h + 2) * size])
        raw = pair[:, (h % 2) * size : (h % 2 + 1) * size]
        scaled = raw * norm_stats(raw) * query_gain[...]
        rot = (scaled * cos[...] + half_turn(scaled) * sin[...]).astype(BF16)
        for s in range(SEQS):
            q_out[s, h * span : (h + 1) * span] = rot[s * span : (s + 1) * span]
            raw_out[s, h * span : (h + 1) * span] = raw[s * span : (s + 1) * span]


def attend_kernel(count, ids, q, pos, wo, *refs):
    kv, (k_out, v_out, p_out, att_out) = refs[:count], refs[count : count + 4]
    pieces, scr = refs[count + 4 : -1], refs[-1]
    ctx = ids[0]
    span = pos.shape[1] // SEQS
    part = span // 2
    size = q.shape[2]
    rows = q.shape[1]
    length = count * span
    scaling = 1.0 / math.sqrt(size)

    def place_of(owner, inner):
        late = (2 * count - 1 - owner) * part + inner - part
        return jnp.where(inner < part, owner * part + inner, late)

    lane = lane_index((span, length))
    key_place = place_of(lane >> (span.bit_length() - 1), lane & (span - 1))
    query_place = place_of(ctx, row_index((span, length)))
    for s in range(SEQS):
        for j in range(count):
            here = pl.ds(pl.multiple_of((ctx ^ j) * span, span), span)
            k_out[s, here] = kv[j][s * span : (s + 1) * span, :size]
            v_out[s, here] = kv[j][s * span : (s + 1) * span, size:]
        start = query_place - as_column(pos[:, s * span : (s + 1) * span]).astype(I32)
        visible = (key_place <= query_place) & (key_place >= start)
        scores = contract_last(q[s], k_out[s]) * scaling
        scores = scores.reshape(rows // span, span, length)
        scores = jnp.where(visible[None], scores, -1e30)
        weights = jnp.exp(scores - jnp.max(scores, axis=-1, keepdims=True))
        weights = weights / jnp.sum(weights, axis=-1, keepdims=True)
        low = weights.reshape(rows, length).astype(BF16)
        p_out[s] = low
        attended = dot(low, v_out[s]).astype(BF16)
        for h in range(rows // span):
            att_out[s * span : (s + 1) * span, h * size : (h + 1) * size] = attended[
                h * span : (h + 1) * span
            ]
    for out in (k_out, v_out, p_out, att_out):
        out.send()
    split_rows(ids[1], dot(att_out[...], wo[...]), pieces, scr)


def split_rows(wa, full, pieces, scr):
    quarter = pieces[0].shape[0]
    scr[...] = full.astype(BF16)
    for k, piece in enumerate(pieces):
        first = pl.multiple_of((wa ^ k) * quarter, quarter)
        piece[...] = scr[pl.ds(first, quarter)]


def join_rows(wa, pieces, out):
    quarter = pieces[0].shape[0]
    for k, piece in enumerate(pieces):
        out[pl.ds(pl.multiple_of((wa ^ k) * quarter, quarter), quarter)] = piece[...]


def added(pieces):
    total = pieces[0][...].astype(F32)
    for piece in pieces[1:]:
        total = total + piece[...].astype(F32)
    return total


def own_rows(ids, array, quarter):
    return array[pl.ds(pl.multiple_of(ids[1] * quarter, quarter), quarter)].astype(F32)


def hot_routes(columns, width):
    lane = lane_index((columns[0].shape[0], width))
    hot = columns[0] == lane
    for column in columns[1:]:
        hot = hot | (column == lane)
    return hot


def hidden_kernel(ids, tok, routes, post_norm, router, cot_rows, *refs):
    pieces, (send, hidden_out, prob_out, cot_out) = refs[:-4], refs[-4:]
    cot_out[...] = cot_rows[...]
    cot_out.send()
    quarter, width = pieces[0].shape
    experts = router.shape[0]
    hidden = own_rows(ids, tok, quarter) + added(pieces)
    hidden_out[...] = hidden
    ffn = (hidden * norm_stats(hidden) * post_norm[...]).astype(BF16)
    named = [as_column(routes[j : j + 1]).astype(I32) for j in range(routes.shape[0])]
    hot = hot_routes(named, experts)
    logits = contract_last(ffn, router[...])
    masked = jnp.where(hot, logits, -1e30)
    exps = jnp.where(hot, jnp.exp(logits - jnp.max(masked, axis=-1, keepdims=True)), 0.0)
    probs = exps / jnp.sum(exps, axis=-1, keepdims=True)
    prob_out[...] = probs
    high, low = split_low(probs)
    send[:, :width] = ffn
    if send.shape[1] > width + 2 * experts:
        send[:, width:] = jnp.zeros((quarter, send.shape[1] - width), BF16)
    send[:, width : width + experts] = high
    send[:, width + experts : width + 2 * experts] = low


def pack_kernel(cot, routes, out):
    quarter, width = cot.shape
    out[:, :width] = cot[...]
    lane = lane_index((quarter, 128))
    named = jnp.zeros((quarter, 128), F32)
    for j in range(routes.shape[0]):
        named = jnp.where(lane == j, as_column(routes[j : j + 1]), named)
    out[:, width:] = named.astype(BF16)


def route_kernel(experts, top, planes, ids, columns, *refs):
    pieces, (t_out, rows_out, scr) = refs[:4], refs[4:]
    quarter = pieces[0].shape[0]
    width = rows_out.shape[1]
    total = 4 * quarter
    lanes = -(-experts // 128) * 128
    for k, piece in enumerate(pieces):
        scr[pl.ds(pl.multiple_of((ids[3] ^ k) * quarter, quarter), quarter)] = piece[...]
    named = scr[:, width : width + 128].astype(F32).astype(I32)
    hot = hot_routes([named[:, j : j + 1] for j in range(top)], lanes)
    row, col = row_index((total, total)), lane_index((total, total))
    shift = quarter.bit_length() - 1
    before = (row >= col) & ((row >> shift) == (col >> shift))
    counts = dot(before.astype(F32).astype(BF16), hot.astype(F32).astype(BF16))
    slots = jnp.where(hot, counts - 1.0, -1.0).astype(BF16)
    slot_rows = columns.shape[1]
    spread = row_index((lanes, slot_rows)) == (ids[3] * planes + columns[0:1])
    slot = dot(slots, spread.astype(F32).astype(BF16))
    lead = row_index((total, slot_rows)) >> shift
    chosen = (slot == columns[2:3].astype(F32)) & (lead == columns[1:2])
    chosen = chosen.astype(F32).astype(BF16)
    t_out[...] = chosen
    t_out.send()
    rows_out[...] = contract_first(chosen, scr[:, :width]).astype(BF16)


def split_groups(mine, scr, pieces):
    group = pieces[0].shape[0]
    for k, piece in enumerate(pieces):
        first = pl.multiple_of((mine ^ k) * group, group)
        piece[...] = scr[pl.ds(first, group)].astype(BF16)
        piece.send()


def join_groups(mine, pieces, scr):
    group = pieces[0].shape[0]
    for k, piece in enumerate(pieces):
        first = pl.multiple_of((mine ^ k) * group, group)
        scr[pl.ds(first, group)] = piece[...].astype(F32)
    return scr[...].astype(BF16)


def pick_kernel(ids, chosen, *refs):
    pieces, (rows_out, scr) = refs[:4], refs[4:]
    quarter = pieces[0].shape[0]
    for k, piece in enumerate(pieces):
        scr[pl.ds(pl.multiple_of((ids[3] ^ k) * quarter, quarter), quarter)] = piece[...]
    rows_out[...] = contract_first(chosen[...], scr[...]).astype(BF16)


def cot_rows_kernel(wd, rows, grad_out):
    grad_out[...] = contract_last(rows[...], wd[...])


def expert_kernel(experts, ids, wg, wu, grad_raw, rows_in, act_out, dg_out, du_out, prob_out, back):
    width = wg.shape[0]
    extra = rows_in.shape[1] - width
    total = rows_in.shape[0]
    rows = rows_in[:, :width]
    lane = lane_index((total, extra))
    mine_high, mine_low = lane == ids[2], lane == ids[2] + experts
    prob = jnp.sum(
        jnp.where(mine_high | mine_low, rows_in[:, width:].astype(F32), 0.0),
        axis=-1,
        keepdims=True,
    )
    prob_out[...] = jnp.broadcast_to(prob, prob_out.shape)
    gate_grad = jnp.zeros((total, 1), F32)
    step = wg.shape[1] // 3
    for c in range(3):
        here = slice(c * step, (c + 1) * step)
        gate, up = dot(rows, wg.part(c)), dot(rows, wu.part(c))
        sig = jax.nn.sigmoid(gate)
        lifted = gate * sig
        act = (lifted * up).astype(BF16)
        act_out[:, here] = act
        raw = grad_raw[:, here]
        gate_grad = gate_grad + jnp.sum(act.astype(F32) * raw, axis=-1, keepdims=True)
        grad_act = prob * raw
        dg_out[:, here] = (grad_act * up * sig * (1.0 + gate * (1.0 - sig))).astype(BF16)
        du_out[:, here] = (grad_act * lifted).astype(BF16)
    for out in (act_out, dg_out, du_out, prob_out):
        out.send()
    grad_in = contract_last(dg_out[...], wg[...]) + contract_last(du_out[...], wu[...])
    back[:, :width] = grad_in.astype(BF16)
    high = gate_grad.astype(BF16).astype(F32)
    tail = jnp.where(mine_high, high, jnp.where(mine_low, gate_grad - high, 0.0))
    back[:, width:] = tail.astype(BF16)


def output_kernel(hidden, *refs):
    refs[-1][...] = (hidden[...] + added(refs[:-1])).astype(BF16)


def expert_weights_kernel(rows, dg, du, act, cot_rows, prob, gate_out, up_out, down_out):
    width, units = gate_out.shape
    step = width // 4
    for c in range(4):
        here = slice(c * step, (c + 1) * step)
        left = rows[:, here]
        gate_out[here] = contract_first(left, dg[...])
        gate_out.send(c)
        up_out[here] = contract_first(left, du[...])
        up_out.send(c)
    grad_rows = (cot_rows[...].astype(F32) * prob[:, 0:1]).astype(BF16)
    step = units // 3
    for c in range(3):
        here = slice(c * step, (c + 1) * step)
        down_out[here] = contract_first(act[:, here], grad_rows)
        down_out.send(c)


def out_rows_kernel(ids, act, wd, prob, *refs):
    pieces, scr = refs[:-1], refs[-1]
    scr[...] = dot(act[...], wd[...]).astype(BF16).astype(F32) * prob[:, 0:1]
    split_groups(ids[4], scr, pieces)


def combine_kernel(groups, ids, chosen, *refs):
    rows = refs[0][...] if groups == 1 else join_groups(ids[4], refs[:groups], refs[-1])
    own, sends, scr = refs[groups], refs[groups + 1 : groups + 4], refs[groups + 4]
    quarter = own.shape[0]
    scr[...] = dot(chosen[...], rows)
    for k, out in enumerate((own,) + sends):
        first = pl.multiple_of((ids[3] ^ k) * quarter, quarter)
        out[...] = scr[pl.ds(first, quarter)].astype(out.dtype)
        out.send()


def grad_hidden_kernel(ids, hidden_ref, prob_ref, router, cot, post_norm, att_in, *refs):
    pieces, (low_out, col_out) = refs[:4], refs[4:]
    width = hidden_ref.shape[1]
    experts = router.shape[0]
    total = added(pieces)
    gate_grad = total[:, width : width + experts] + total[:, width + experts : width + 2 * experts]
    prob = prob_ref[...]
    grad_logits = prob * (gate_grad - jnp.sum(prob * gate_grad, axis=-1, keepdims=True))
    high, low = split_low(grad_logits)
    grad_ffn = total[:, :width] + (dot(high, router[...]) + dot(low, router[...]))
    hidden = hidden_ref[...]
    inverse = norm_stats(hidden)
    normed = hidden * inverse
    ffn = (normed * post_norm[...]).astype(BF16)
    grad = cot[...].astype(F32) + norm_backward(grad_ffn, normed, inverse, post_norm[...])
    grad = grad.astype(BF16)
    low_out[...] = grad
    router_part = (contract_first(high, ffn) + contract_first(low, ffn)).astype(BF16)
    post = jnp.sum(grad_ffn * normed, axis=0, keepdims=True)
    post = jnp.where(row_index((experts, width)) == 0, post, 0.0).astype(BF16)
    quarter, count = hidden.shape[0], col_out.shape[0]
    part = width // count
    mine = att_in[pl.ds(pl.multiple_of(ids[1] * quarter, quarter), quarter)]
    for k in range(count):
        here = slice(k * part, (k + 1) * part)
        col_out[k, :quarter, :part] = mine[:, here]
        col_out[k, :quarter, part:] = grad[:, here]
        col_out[k, quarter:, :part] = router_part[:, here]
        col_out[k, quarter:, part:] = post[:, here]


def attend_back_kernel(
    count, ids, q, keys, values, p, raw_ref, wo, cos, sin, gain, *refs
):
    pieces, (gq_out, gain_out, kv_out, branch_out, dq_scr) = refs[:4], refs[4:]
    join_rows(ids[1], pieces, branch_out)
    branch_out.send()
    size, rows = q.shape[2], q.shape[1]
    span = branch_out.shape[0] // SEQS
    heads = rows // span
    scaling = 1.0 / math.sqrt(size)
    grad_att = contract_last(branch_out[...], wo[...]).astype(BF16)
    gain_sum = jnp.zeros((1, size), F32)
    for s in range(SEQS):
        rows_s = grad_att[s * span : (s + 1) * span]
        for h in range(heads):
            dq_scr[h * span : (h + 1) * span] = rows_s[:, h * size : (h + 1) * size]
        grad_o = dq_scr[...]
        low = p[s]
        grad_p = contract_last(grad_o, values[s])
        weights = low.astype(F32)
        delta = jnp.sum(weights * grad_p, axis=-1, keepdims=True)
        grad_s = (weights * (grad_p - delta)).astype(BF16)
        grad_v = contract_first(low, grad_o).astype(BF16)
        grad_k = (contract_first(grad_s, q[s]) * scaling).astype(BF16)
        for j in range(count):
            kv_out[j, s * span : (s + 1) * span, :size] = grad_k[j * span : (j + 1) * span]
            kv_out[j, s * span : (s + 1) * span, size:] = grad_v[j * span : (j + 1) * span]
        grad_q = dot(grad_s, keys[s]) * scaling
        cosine, sine = cos[s * span : (s + 1) * span], sin[s * span : (s + 1) * span]
        for h in range(heads):
            grad_rot = grad_q[h * span : (h + 1) * span]
            grad_normed = grad_rot * cosine - half_turn(grad_rot) * sine
            raw = raw_ref[s, h * span : (h + 1) * span]
            inverse = norm_stats(raw)
            normed = raw * inverse
            gain_sum = gain_sum + jnp.sum(grad_normed * normed, axis=0, keepdims=True)
            gq_out[s * span : (s + 1) * span, h * size : (h + 1) * size] = norm_backward(
                grad_normed, normed, inverse, gain[...]
            ).astype(BF16)
    gain_out[...] = gain_sum


def query_in_kernel(gq, wq, cols, out, col_out):
    count, height, double = cols.shape
    quarter = (col_out.shape[0] - height) // (count - 1)
    experts = height - quarter
    total = jnp.zeros((experts, double), F32)
    for k in range(count):
        col_out[k * quarter : (k + 1) * quarter] = cols[k, :quarter]
        total = total + cols[k, quarter:].astype(F32)
    col_out[count * quarter :] = total.astype(BF16)
    out[...] = contract_last(gq[...], wq[...])


def grad_in_kernel(ids, from_q, raw_ref, cos, sin, gain, wk, wv, parts, kv_out, gain_out, own_out, send_out, scr):
    size = wk.shape[1]
    total = added([parts[k] for k in range(parts.shape[0])])
    grad_v = total[:, size:].astype(BF16)
    grad_rot = total[:, :size]
    grad_normed = grad_rot * cos[...] - half_turn(grad_rot) * sin[...]
    raw = raw_ref[...]
    inverse = norm_stats(raw)
    normed = raw * inverse
    gain_out[...] = jnp.sum(grad_normed * normed, axis=0, keepdims=True)
    grad_k = norm_backward(grad_normed, normed, inverse, gain[...]).astype(BF16)
    kv_out[:, :size] = grad_k
    kv_out[:, size:] = grad_v
    full = from_q[...] + contract_last(grad_k, wk[...]) + contract_last(grad_v, wv[...])
    scr[...] = full.astype(BF16)
    half = own_out.shape[0]
    for out, core in ((send_out, 1 - ids[1] % 2), (own_out, ids[1] % 2)):
        out[...] = scr[pl.ds(pl.multiple_of(core * half, half), half)]


def half_kernel(own, other, out):
    out[...] = added((own, other)).astype(BF16)


def token_rows_kernel(ids, tok, gain, branch, own, other, q_gain, k_gain, *refs):
    sums, (rows_out, parts_out) = refs[:4], refs[4:]
    half = own.shape[0]
    wa_count = lax.axis_size("wa")
    mine = pl.ds(pl.multiple_of(ids[1] % 2 * half, half), half)
    grad_in = added((own, other))
    wide = tok[mine].astype(F32)
    inverse = norm_stats(wide)
    normed = wide * inverse
    rows_out[...] = (
        branch[mine].astype(F32) + norm_backward(grad_in, normed, inverse, gain[...])
    ).astype(BF16)
    gain_part = 0.5 * jnp.sum(grad_in * normed, axis=0, keepdims=True)
    total = added(sums)
    experts, part = total.shape[0], total.shape[1] // 2
    step = part // wa_count
    router_part, post = total[:, :step], total[:1, part : part + step]
    for w in range(1, wa_count):
        here = ids[1] == w
        router_part = jnp.where(here, total[:, w * step : (w + 1) * step], router_part)
        post = jnp.where(here, total[:1, part + w * step : part + (w + 1) * step], post)
    base = experts // 2
    parts_out[...] = jnp.zeros(parts_out.shape, F32)
    count = parts_out.shape[0] // wa_count
    for d in range(count * wa_count):
        parts_out[d, :base, :step] = router_part[:base]
        parts_out[d, :base, 64 : 64 + step] = router_part[base:]
        parts_out[d, base : base + 1, :step] = post
        parts_out[d, base + 1 : base + 2] = q_gain[...]
        parts_out[d, base + 2 : base + 3] = k_gain[...]
        first = d // wa_count * part
        for j in range(-(-part // 128)):
            lanes = min(128, part)
            parts_out[d, base + 3 + j : base + 4 + j, :lanes] = gain_part[
                :, first + j * 128 : first + j * 128 + lanes
            ]


def sums_kernel(parts, router_out, post_out, q_out, k_out, gain_out):
    devices = parts.shape[0]
    experts, step = router_out.shape[0], router_out.shape[1] // devices
    base = experts // 2
    total = parts[0, base:]
    for d in range(1, devices):
        total = total + parts[d, base:]
    q_out[...] = total[1:2]
    k_out[...] = total[2:3]
    part = gain_out.shape[1]
    for j in range(-(-part // 128)):
        lanes = min(128, part)
        gain_out[:, j * 128 : j * 128 + lanes] = total[3 + j : 4 + j, :lanes]
    group = 128 // step
    for g in range(devices // group):
        held = range(g * group, (g + 1) * group)
        here = slice(g * 128, (g + 1) * 128)
        router_out[:base, here] = jnp.concatenate([parts[d, :base, :step] for d in held], axis=1)
        router_out[base:, here] = jnp.concatenate(
            [parts[d, :base, 64 : 64 + step] for d in held], axis=1
        )
        post_out[:, here] = jnp.concatenate([parts[d, base : base + 1, :step] for d in held], axis=1)


def join_kernel(ids, own, other, out):
    half = own.shape[0]
    for source, core in ((own, ids[1] % 2), (other, 1 - ids[1] % 2)):
        out[pl.ds(pl.multiple_of(core * half, half), half)] = source[...]


def token_order(wa, pieces, count, first, scr):
    part = scr.shape[1]
    wa_count = len(pieces)
    quarter = scr.shape[0] // (wa_count * count)
    for k, piece in enumerate(pieces):
        for c in range(count):
            row = pl.multiple_of((c * wa_count + (wa ^ k)) * quarter, quarter)
            scr[pl.ds(row, quarter)] = piece[c * quarter : (c + 1) * quarter, first : first + part]
    return scr[...]


def out_weight_kernel(count, ids, attended, *refs):
    pieces, (out, scr) = refs[:4], refs[4:]
    part = scr.shape[1]
    out[...] = contract_first(attended[...], token_order(ids[1], pieces, count, part, scr))


def in_weight_kernel(count, ids, queries, *refs):
    pieces, kvs = refs[:4], refs[4 : 4 + count]
    wq_out, wk_out, wv_out, left, narrow = refs[4 + count :]
    rows, size = kvs[0].shape[0], wk_out.shape[1]
    mine = token_order(ids[1], pieces, count, 0, left)
    wq_out[...] = contract_first(mine, queries[...])
    wq_out.send()
    for k, piece in enumerate(kvs):
        narrow[pl.ds(pl.multiple_of((ids[0] ^ k) * rows, rows), rows)] = piece[...]
    both = contract_first(mine, narrow[...])
    wk_out[...] = both[:, :size]
    wv_out[...] = both[:, size:]


def bind(body, *sizes):
    return lambda *refs: body(*sizes, *refs)


def on_device(
    tokens,
    positions,
    routes,
    query_weight,
    key_matrix,
    value_matrix,
    out_weight,
    query_gain,
    key_gain,
    input_norm,
    post_norm,
    router,
    gate_weight,
    up_weight,
    down_weight,
    cotangent,
):
    lead_count, low_count = lax.axis_size("lead"), lax.axis_size("low")
    ctx_count = lead_count * low_count
    wa_count = lax.axis_size("wa")
    lead_id = lax.axis_index("lead")
    wa_id = lax.axis_index("wa")
    ctx_id = lead_id * low_count + lax.axis_index("low")
    plane_id = lax.axis_index("low") * wa_count + wa_id
    ids = jnp.stack([ctx_id, wa_id, ctx_id * wa_count + wa_id, lead_id, plane_id]).astype(I32)
    row_count, width = tokens.shape
    span = row_count // SEQS
    quarter = row_count // wa_count
    size = query_gain.shape[0]
    local_width = query_weight.shape[1]
    heads = local_width // size
    length = span * ctx_count
    experts = router.shape[1]
    top = routes.shape[1]
    hidden_units = gate_weight.shape[2]
    devices = ctx_count * wa_count
    planes = low_count * wa_count
    part = width // ctx_count
    capacity = max(2, (5 * quarter * top + 4 * experts - 1) // (4 * experts))
    group = -(-4 * capacity // 16) * 16 if planes > 8 else 4 * capacity
    slot_rows = planes * group
    extra = -(-2 * experts // 128) * 128
    everywhere, plane, blocks = ("lead", "low", "wa"), ("low", "wa"), ("lead", "low")
    gate_weight, up_weight, down_weight = gate_weight[0], up_weight[0], down_weight[0]
    input_norm, post_norm = input_norm[None], post_norm[None]
    query_gain, key_gain = query_gain[None], key_gain[None]

    cosine, sine = angle_tables(positions, size)
    attention_input, kv_own, keys_raw = vcall(
        kv_kernel,
        [
            ((row_count, width), BF16),
            ((row_count, 2 * size), BF16, "near"),
            ((row_count, size), F32),
        ],
        tokens, input_norm, key_matrix, value_matrix, cosine, sine, key_gain,
        flops=4 * row_count * width * size,
    )
    kv_all = exchange([kv_own] * ctx_count, blocks)

    q_heads, queries_raw = vcall(
        query_kernel,
        [
            ((SEQS, heads * span, size), BF16),
            ((SEQS, heads * span, size), F32),
        ],
        attention_input, query_weight, cosine, sine, query_gain,
        flops=2 * row_count * width * local_width,
    )

    (cot_send,) = vcall(
        pack_kernel,
        [((quarter, width + 128), BF16, "near")],
        cotangent, routes.T,
        after=[q_heads],
    )
    cot_pieces = exchange([cot_send] * 4, "lead")

    keys_seq, values_seq, weights_low, attended_low, *branch = vcall(
        bind(attend_kernel, ctx_count),
        [
            ((SEQS, length, size), BF16),
            ((SEQS, length, size), BF16),
            ((SEQS, heads * span, length), BF16),
            ((row_count, local_width), BF16),
        ]
        + [((quarter, width), BF16, "near")] * wa_count,
        ids, q_heads, positions[None], out_weight, *near(kv_all),
        scratch=[pltpu.VMEM((row_count, width), BF16)],
        flops=2 * row_count * width * local_width + 4 * row_count * local_width * length,
        megabytes=48,
    )
    inner = np.arange(slot_rows) % group
    columns = np.zeros((8, slot_rows), np.int32)
    columns[0] = np.arange(slot_rows) // group
    columns[1] = np.minimum(inner // capacity, 3)
    columns[2] = np.where(inner < 4 * capacity, inner % capacity, -5)
    chosen, cot_rows = vcall(
        bind(route_kernel, experts, top, planes),
        [((row_count, slot_rows), BF16), ((slot_rows, width), BF16, "near")],
        ids, jnp.asarray(columns), *near(cot_pieces),
        after=[branch[0]],
        scratch=[pltpu.VMEM((4 * quarter, width + 128), BF16)],
        flops=2 * slot_rows * row_count * width,
    )
    attended_all = gather(attended_low, blocks)
    branch = exchange(branch, "wa")
    send, hidden, probs, cot_rows = vcall(
        hidden_kernel,
        [
            ((quarter, width + extra), BF16, "near"),
            ((quarter, width), F32),
            ((quarter, experts), F32),
            ((slot_rows, width), BF16),
        ],
        ids, tokens, routes.T, post_norm, router.T, Near(cot_rows), *near(branch),
        flops=2 * quarter * width * experts,
    )

    cot_rows = swap(cot_rows, plane)
    (grad_raw,) = vcall(
        cot_rows_kernel,
        [((slot_rows, hidden_units), F32)],
        down_weight, cot_rows,
        flops=2 * slot_rows * hidden_units * width,
    )

    (rows_in,) = vcall(
        pick_kernel,
        [((slot_rows, width + extra), BF16)],
        ids, chosen, *near(exchange([send] * 4, "lead")),
        after=[cot_rows],
        scratch=[pltpu.VMEM((row_count, width + extra), BF16)],
        flops=2 * slot_rows * row_count * width,
    )
    rows_in = swap(rows_in, plane)
    activation, grad_gate_part, grad_up_part, row_prob, back = vcall(
        bind(expert_kernel, experts),
        [
            ((slot_rows, hidden_units), BF16),
            ((slot_rows, hidden_units), BF16),
            ((slot_rows, hidden_units), BF16),
            ((slot_rows, 128), F32),
            ((slot_rows, width + extra), BF16),
        ],
        ids, gate_weight, up_weight, grad_raw, Near(rows_in),
        after=[attended_all],
        split={1: 3, 2: 3},
        flops=8 * slot_rows * hidden_units * width,
        megabytes=48,
    )

    grad_gate_weight, grad_up_weight, grad_down_weight = vcall(
        expert_weights_kernel,
        [
            ((width, hidden_units), F32),
            ((width, hidden_units), F32),
            ((hidden_units, width), F32),
        ],
        rows_in, grad_gate_part, grad_up_part, activation, cot_rows, row_prob,
        split={-1: 4, -2: 4, -3: 3},
        flops=6 * slot_rows * hidden_units * width,
        megabytes=40,
    )

    def to_tokens(groups, after):
        columns_out = groups[0].shape[1]
        scratch = [pltpu.VMEM((row_count, columns_out), F32)]
        if len(groups) > 1:
            scratch.append(pltpu.VMEM((slot_rows, columns_out), F32))
        return vcall(
            bind(combine_kernel, len(groups)),
            [((quarter, columns_out), F32, "near")] + [((quarter, columns_out), BF16, "near")] * 3,
            ids, chosen, *near(groups),
            after=after,
            scratch=scratch,
            flops=2 * slot_rows * row_count * width,
        )

    back_pieces = exchange(to_tokens([swap(back, plane)], [grad_gate_weight]), "lead")
    out_groups = vcall(
        out_rows_kernel,
        [((group, width), BF16)] * planes,
        ids, activation, down_weight, row_prob,
        after=back_pieces[1:2],
        scratch=[pltpu.VMEM((slot_rows, width), F32)],
        flops=2 * slot_rows * hidden_units * width,
    )
    out_sends = out_groups
    out_groups = exchange(out_groups, plane)
    grad_low, weight_columns = vcall(
        grad_hidden_kernel,
        [
            ((quarter, width), BF16, "near"),
            ((ctx_count, quarter + experts, 2 * part), BF16),
        ],
        ids, hidden, probs, router.T, cotangent, post_norm, attention_input, *near(back_pieces),
        after=out_sends[:1],
        flops=4 * quarter * width * experts,
    )

    weight_columns = swap(weight_columns, blocks)
    grad_pieces = gather_wa_pieces(grad_low)
    grad_queries, query_gain_part, kv_parts, grad_branch = vcall(
        bind(attend_back_kernel, ctx_count),
        [
            ((row_count, local_width), BF16),
            ((1, size), F32),
            ((ctx_count, row_count, 2 * size), BF16),
            ((row_count, width), BF16),
        ],
        ids, q_heads, keys_seq, values_seq, weights_low, queries_raw, out_weight,
        cosine, sine, query_gain, *near(grad_pieces),
        after=[weight_columns],
        scratch=[pltpu.VMEM((heads * span, size), BF16)],
        flops=2 * row_count * width * local_width + 8 * row_count * local_width * length,
        megabytes=48,
    )
    kv_parts = swap(kv_parts, blocks)
    queries_all = gather(grad_queries, blocks)
    from_queries, weight_columns = vcall(
        query_in_kernel,
        [((row_count, width), F32), ((ctx_count * quarter + experts, 2 * part), BF16)],
        grad_queries, query_weight, weight_columns,
        flops=2 * row_count * width * local_width,
    )
    grad_kv, key_gain_part, grad_in_own, grad_in_send = vcall(
        grad_in_kernel,
        [
            ((row_count, 2 * size), BF16, "near"),
            ((1, size), F32),
            ((row_count // 2, width), BF16, "near"),
            ((row_count // 2, width), BF16, "near"),
        ],
        ids, from_queries, keys_raw, cosine, sine, key_gain, key_matrix, value_matrix, Near(kv_parts),
        scratch=[pltpu.VMEM((row_count, width), BF16)],
        flops=4 * row_count * width * size,
    )
    (grad_in_half,) = vcall(
        half_kernel,
        [((row_count // 2, width), BF16, "near")],
        Near(grad_in_own), Near(xor_permute(grad_in_send, "wa", 1)),
        after=out_groups[1:],
    )
    column_pieces = gather_wa_pieces(weight_columns)
    (grad_out_weight,) = vcall(
        bind(out_weight_kernel, ctx_count),
        [((local_width, part), F32)],
        ids, attended_all, *column_pieces,
        scratch=[pltpu.VMEM((ctx_count * row_count, part), BF16)],
        flops=2 * ctx_count * row_count * local_width * part,
    )
    sums_at = ctx_count * quarter
    token_rows, small_parts = vcall(
        token_rows_kernel,
        [
            ((row_count // 2, width), BF16, "near"),
            ((devices, -(-(experts // 2 + 3 + -(-part // 128)) // 8) * 8, 128), F32),
        ],
        ids, tokens, input_norm, grad_branch,
        Near(grad_in_half), Near(xor_permute(grad_in_half, "wa", 2)),
        query_gain_part, key_gain_part,
        *[Rows(piece, sums_at, experts) for piece in column_pieces],
        after=[grad_out_weight],
    )
    (grad_tokens,) = vcall(
        join_kernel,
        [((row_count, width), BF16)],
        ids, Near(token_rows), Near(xor_permute(token_rows, "wa", 1)),
    )
    grad_kv_all = gather_ctx_pieces(grad_kv)

    grad_query_weight, grad_key_weight, grad_value_weight = vcall(
        bind(in_weight_kernel, ctx_count),
        [((part, local_width), F32), ((part, size), F32), ((part, size), F32)],
        ids, queries_all, *column_pieces, *grad_kv_all,
        scratch=[
            pltpu.VMEM((ctx_count * row_count, part), BF16),
            pltpu.VMEM((ctx_count * row_count, 2 * size), BF16),
        ],
        flops=2 * ctx_count * row_count * local_width * part,
        megabytes=48,
    )
    out_pieces = exchange(to_tokens(out_groups, [small_parts] + grad_kv_all[1:]), "lead")
    (output,) = vcall(
        output_kernel,
        [((quarter, width), BF16)],
        hidden, *near(out_pieces),
        after=[grad_tokens],
    )

    grad_router, grad_post_norm, grad_query_gain, grad_key_gain, grad_input_norm = vcall(
        sums_kernel,
        [
            ((experts, width), F32),
            ((1, width), F32),
            ((1, size), F32),
            ((1, size), F32),
            ((1, part), F32),
        ],
        swap(small_parts, everywhere),
    )
    return (
        output,
        grad_tokens,
        grad_query_weight,
        grad_key_weight,
        grad_value_weight,
        grad_out_weight,
        grad_query_gain[0],
        grad_key_gain[0],
        grad_input_norm[0],
        grad_post_norm[0],
        grad_router.T,
        grad_gate_weight[None],
        grad_up_weight[None],
        grad_down_weight[None],
    )


def solution(mesh):
    ctx_count, wa_count = mesh.devices.shape
    finer = Mesh(mesh.devices.reshape(4, ctx_count // 4, wa_count), ("lead", "low", "wa"))
    return jax.shard_map(
        on_device,
        mesh=finer,
        in_specs=(
            P(("lead", "low"), None),
            P(("lead", "low")),
            P(("lead", "low", "wa"), None),
            P(None, "wa"),
            P(None, "wa"),
            P(None, "wa"),
            P("wa", None),
            P(),
            P(),
            P(),
            P(),
            P(),
            P(("lead", "low", "wa"), None, None),
            P(("lead", "low", "wa"), None, None),
            P(("lead", "low", "wa"), None, None),
            P(("lead", "low", "wa"), None),
        ),
        out_specs=(
            P(("lead", "low", "wa"), None),
            P(("lead", "low"), None),
            P(("lead", "low"), "wa"),
            P(("lead", "low"), "wa"),
            P(("lead", "low"), "wa"),
            P("wa", ("lead", "low")),
            P(),
            P(),
            P(("lead", "low")),
            P(),
            P(),
            P(("lead", "low", "wa"), None, None),
            P(("lead", "low", "wa"), None, None),
            P(("lead", "low", "wa"), None, None),
        ),
        check_vma=False,
    )
```

```python
import math

import jax
import jax.numpy as jnp
import numpy as np
from jax import lax
from jax.experimental import pallas as pl
from jax.experimental.pallas import tpu as pltpu
from jax.sharding import Mesh
from jax.sharding import PartitionSpec as P

SEQS = 2


EPSILON = 1e-06
BF16, F32, I32 = jnp.bfloat16, jnp.float32, jnp.int32


def dot(left, right):
    return jnp.dot(left, right, preferred_element_type=F32)


def contract_last(left, right):
    return lax.dot_general(
        left, right, (((1,), (1,)), ((), ())), preferred_element_type=F32
    )


def contract_first(left, right):
    return lax.dot_general(
        left, right, (((0,), (0,)), ((), ())), preferred_element_type=F32
    )


def split_low(values):
    high = values.astype(BF16)
    return high, (values - high.astype(F32)).astype(BF16)


def norm_stats(values):
    return lax.rsqrt(jnp.mean(values * values, axis=-1, keepdims=True) + EPSILON)


def norm_backward(grad_normed, normed, inverse, gain):
    scaled = grad_normed * gain
    return inverse * (scaled - normed * jnp.mean(scaled * normed, axis=-1, keepdims=True))


def half_turn(values):
    return pltpu.roll(values, values.shape[-1] // 2, values.ndim - 1)


def xor_permute(value, axis, offset):
    names = (axis,) if isinstance(axis, str) else axis
    count = math.prod(lax.axis_size(name) for name in names)
    return lax.ppermute(value, axis, [(i, i ^ offset) for i in range(count)])


def exchange(pieces, axis):
    return [pieces[0]] + [xor_permute(pieces[k], axis, k) for k in range(1, len(pieces))]


def gather_ctx_pieces(value):
    low_count = lax.axis_size("low")
    held = {j * low_count: v for j, v in enumerate(exchange([value] * 4, "lead"))}
    bit = 1
    while bit < low_count:
        held.update({k ^ bit: xor_permute(v, "low", bit) for k, v in list(held.items())})
        bit *= 2
    return [held[k] for k in range(4 * low_count)]


def gather_wa_pieces(value):
    over = xor_permute(value, "wa", 2)
    return [value, xor_permute(value, "wa", 1), over, xor_permute(over, "wa", 1)]


def gather(value, axis):
    return lax.all_gather(value, axis, axis=0, tiled=True)


def swap(value, axes):
    return lax.all_to_all(value, axes, split_axis=0, concat_axis=0, tiled=True)


class Incoming:
    def __init__(self, ref, copies):
        self.ref, self.copies = ref, dict(enumerate(copies))
        self.step = ref.shape[-1] // len(copies)
        self.shape, self.dtype, self.ndim = ref.shape, ref.dtype, ref.ndim

    def ready(self):
        for k in list(self.copies):
            self.copies.pop(k).wait()
        return self.ref

    def part(self, k):
        if k in self.copies:
            self.copies.pop(k).wait()
        return self.ref[:, k * self.step : (k + 1) * self.step]

    def __getitem__(self, index):
        return self.ready()[index]


class Outgoing:
    def __init__(self, ref, copies):
        self.ref, self.copies, self.sent = ref, copies, set()
        self.shape, self.dtype, self.ndim = ref.shape, ref.dtype, ref.ndim

    def send(self, part=None):
        for k, copy in enumerate(self.copies):
            if k not in self.sent and part in (None, k):
                copy.start()
                self.sent.add(k)

    def __getitem__(self, index):
        return self.ref[index]

    def __setitem__(self, index, value):
        self.ref[index] = value


class Near:
    def __init__(self, value):
        self.value = value


class Rows:
    def __init__(self, value, first, count):
        self.value, self.first, self.count = value, first, count


def near(values):
    return [Near(value) for value in values]


def vcall(body, outs, *operands, scratch=(), after=(), split=None, flops=0, megabytes=24):
    split = split or {}
    close = [isinstance(o, Near) for o in operands]
    ranges = {i: (o.first, o.count) for i, o in enumerate(operands) if isinstance(o, Rows)}
    operands = [o.value if isinstance(o, (Near, Rows)) else o for o in operands]
    close_out = [len(o) > 2 for o in outs]
    outs = [o[:2] for o in outs]
    places = [i for i, o in enumerate(operands) if o.ndim > 1 and not close[i]]
    far_outs = [i for i, c in enumerate(close_out) if not c]
    arrays = [
        jax.ShapeDtypeStruct((ranges[i][1],) + operands[i].shape[1:], operands[i].dtype)
        if i in ranges
        else operands[i]
        for i in places
    ]
    sizes = [o.size * o.dtype.itemsize for o in arrays]
    in_parts = [split.get(i, 1) for i in places]
    out_parts = [split.get(-1 - i, 1) for i in far_outs]
    count = len(arrays)

    def kernel(*refs):
        given = list(refs[: len(operands)])
        rest = refs[len(operands) + len(after) :]
        results, rest = rest[: len(outs)], rest[len(outs) :]
        inner = count + len(far_outs)
        buffers, sems, own = rest[:inner], rest[inner], rest[inner + 1 :]
        used = 0
        incoming = []
        for k, i in enumerate(places):
            source, target, parts = given[i], buffers[k], in_parts[k]
            if i in ranges:
                source = source.at[pl.ds(*ranges[i])]
            copies = []
            for c in range(parts):
                step = source.shape[-1] // parts
                if parts > 1:
                    piece = (slice(None), pl.ds(c * step, step))
                    copy = pltpu.make_async_copy(source.at[piece], target.at[piece], sems.at[used])
                else:
                    copy = pltpu.make_async_copy(source, target, sems.at[used])
                copies.append(copy)
                used += 1
            incoming.append(copies)
            given[i] = Incoming(target, copies)
        for c in range(max(in_parts, default=0)):
            for k in sorted(range(count), key=lambda k: sizes[k] / in_parts[k]):
                if c < in_parts[k]:
                    incoming[k][c].start()
        leaving = [Outgoing(result, []) for result in results]
        for k, i in enumerate(far_outs):
            result, source, parts = results[i], buffers[count + k], out_parts[k]
            copies = []
            for c in range(parts):
                step = result.shape[0] // parts
                if parts > 1:
                    piece = pl.ds(c * step, step)
                    copy = pltpu.make_async_copy(source.at[piece], result.at[piece], sems.at[used])
                else:
                    copy = pltpu.make_async_copy(source, result, sems.at[used])
                copies.append(copy)
                used += 1
            leaving[i] = Outgoing(source, copies)
        body(*given, *leaving, *own)
        for value in given:
            if isinstance(value, Incoming):
                value.ready()
        for value in leaving:
            value.send()
        for value in leaving:
            for copy in value.copies:
                copy.wait()

    moved = sum(sizes) + sum(math.prod(s) * jnp.dtype(d).itemsize for s, d in outs)
    in_hbm = pl.BlockSpec(memory_space=pltpu.HBM)

    def pinned(value):
        return pltpu.with_memory_space_constraint(value, pltpu.HBM)

    return pl.pallas_call(
        kernel,
        out_shape=[
            jax.ShapeDtypeStruct(s, d) if c else pltpu.HBM(s, d)
            for (s, d), c in zip(outs, close_out)
        ],
        in_specs=[
            pl.BlockSpec(memory_space=pltpu.SMEM)
            if o.ndim == 1
            else (pl.BlockSpec(memory_space=pltpu.VMEM) if c else in_hbm)
            for o, c in zip(operands, close)
        ]
        + [in_hbm] * len(after),
        out_specs=[pl.BlockSpec(memory_space=pltpu.VMEM) if c else in_hbm for c in close_out],
        scratch_shapes=[pltpu.VMEM(o.shape, o.dtype) for o in arrays]
        + [pltpu.VMEM(*outs[i]) for i in far_outs]
        + [pltpu.SemaphoreType.DMA((max(1, sum(in_parts) + sum(out_parts)),))]
        + list(scratch),
        compiler_params=pltpu.CompilerParams(vmem_limit_bytes=megabytes << 20),
        cost_estimate=pl.CostEstimate(flops=flops, bytes_accessed=moved, transcendentals=0),
    )(*[pinned(o) if i in places else o for i, o in enumerate(operands)], *[pinned(o) for o in after])


def as_column(row):
    count = row.shape[1]
    here = row_index((count, count)) == lane_index((count, count))
    return jnp.sum(jnp.where(here, row.astype(F32), 0.0), axis=-1, keepdims=True)


def lane_index(shape):
    return lax.broadcasted_iota(I32, shape, len(shape) - 1)


def row_index(shape):
    return lax.broadcasted_iota(I32, shape, len(shape) - 2)


def kv_kernel(tok, gain, wk, wv, pos, rates, key_gain, a_out, kv_out, raw_out, cos, sin):
    wide = tok[...].astype(F32)
    low = (wide * norm_stats(wide) * gain[...]).astype(BF16)
    a_out[...] = low
    size = wk.shape[1]
    angles = as_column(pos[...]) * rates[...]
    cos[...] = jnp.cos(angles)
    sine = jnp.sin(angles)
    sin[...] = jnp.where(lane_index(sine.shape) < size // 2, -sine, sine)
    raw = dot(low, wk[...])
    raw_out[...] = raw
    scaled = raw * norm_stats(raw) * key_gain[...]
    key = (scaled * cos[...] + half_turn(scaled) * sin[...]).astype(BF16)
    value = dot(low, wv[...]).astype(BF16)
    kv_out[:, :size] = key
    kv_out[:, size:] = value


def query_kernel(a, wq, cos, sin, query_gain, q_out, raw_out):
    size = cos.shape[1]
    span = a.shape[0] // SEQS
    for h in range(wq.shape[1] // size):
        if h % 2 == 0:
            pair = dot(a[...], wq[:, h * size : (h + 2) * size])
        raw = pair[:, (h % 2) * size : (h % 2 + 1) * size]
        scaled = raw * norm_stats(raw) * query_gain[...]
        rot = (scaled * cos[...] + half_turn(scaled) * sin[...]).astype(BF16)
        for s in range(SEQS):
            q_out[s, h * span : (h + 1) * span] = rot[s * span : (s + 1) * span]
            raw_out[s, h * span : (h + 1) * span] = raw[s * span : (s + 1) * span]


def attend_kernel(count, ids, q, pos, wo, *refs):
    kv, (k_out, v_out, p_out, att_out) = refs[:count], refs[count : count + 4]
    pieces, scr = refs[count + 4 : -1], refs[-1]
    ctx = ids[0]
    span = pos.shape[1] // SEQS
    part = span // 2
    size = q.shape[2]
    rows = q.shape[1]
    length = count * span
    scaling = 1.0 / math.sqrt(size)

    def place_of(owner, inner):
        late = (2 * count - 1 - owner) * part + inner - part
        return jnp.where(inner < part, owner * part + inner, late)

    lane = lane_index((span, length))
    key_place = place_of(lane >> (span.bit_length() - 1), lane & (span - 1))
    query_place = place_of(ctx, row_index((span, length)))
    for s in range(SEQS):
        for j in range(count):
            here = pl.ds(pl.multiple_of((ctx ^ j) * span, span), span)
            k_out[s, here] = kv[j][s * span : (s + 1) * span, :size]
            v_out[s, here] = kv[j][s * span : (s + 1) * span, size:]
        start = query_place - as_column(pos[:, s * span : (s + 1) * span]).astype(I32)
        visible = (key_place <= query_place) & (key_place >= start)
        scores = contract_last(q[s], k_out[s]) * scaling
        scores = scores.reshape(rows // span, span, length)
        scores = jnp.where(visible[None], scores, -1e30)
        weights = jnp.exp(scores - jnp.max(scores, axis=-1, keepdims=True))
        weights = weights / jnp.sum(weights, axis=-1, keepdims=True)
        low = weights.reshape(rows, length).astype(BF16)
        p_out[s] = low
        attended = dot(low, v_out[s]).astype(BF16)
        for h in range(rows // span):
            att_out[s * span : (s + 1) * span, h * size : (h + 1) * size] = attended[
                h * span : (h + 1) * span
            ]
    for out in (k_out, v_out, p_out, att_out):
        out.send()
    split_rows(ids[1], dot(att_out[...], wo[...]), pieces, scr)


def split_rows(wa, full, pieces, scr):
    quarter = pieces[0].shape[0]
    scr[...] = full.astype(BF16)
    for k, piece in enumerate(pieces):
        first = pl.multiple_of((wa ^ k) * quarter, quarter)
        piece[...] = scr[pl.ds(first, quarter)]


def join_rows(wa, pieces, out):
    quarter = pieces[0].shape[0]
    for k, piece in enumerate(pieces):
        out[pl.ds(pl.multiple_of((wa ^ k) * quarter, quarter), quarter)] = piece[...]


def added(pieces):
    total = pieces[0][...].astype(F32)
    for piece in pieces[1:]:
        total = total + piece[...].astype(F32)
    return total


def own_rows(ids, array, quarter):
    return array[pl.ds(pl.multiple_of(ids[1] * quarter, quarter), quarter)].astype(F32)


def hot_routes(columns, width):
    lane = lane_index((columns[0].shape[0], width))
    hot = columns[0] == lane
    for column in columns[1:]:
        hot = hot | (column == lane)
    return hot


def hidden_kernel(ids, tok, routes, post_norm, router, *refs):
    pieces, (send, hidden_out, prob_out) = refs[:-3], refs[-3:]
    quarter, width = pieces[0].shape
    experts = router.shape[0]
    hidden = own_rows(ids, tok, quarter) + added(pieces)
    hidden_out[...] = hidden
    ffn = (hidden * norm_stats(hidden) * post_norm[...]).astype(BF16)
    named = [as_column(routes[j : j + 1]).astype(I32) for j in range(routes.shape[0])]
    hot = hot_routes(named, experts)
    logits = contract_last(ffn, router[...])
    masked = jnp.where(hot, logits, -1e30)
    exps = jnp.where(hot, jnp.exp(logits - jnp.max(masked, axis=-1, keepdims=True)), 0.0)
    probs = exps / jnp.sum(exps, axis=-1, keepdims=True)
    prob_out[...] = probs
    high, low = split_low(probs)
    send[:, :width] = ffn
    if send.shape[1] > width + 2 * experts:
        send[:, width:] = jnp.zeros((quarter, send.shape[1] - width), BF16)
    send[:, width : width + experts] = high
    send[:, width + experts : width + 2 * experts] = low


def pack_kernel(cot, routes, out):
    quarter, width = cot.shape
    out[:, :width] = cot[...]
    lane = lane_index((quarter, 128))
    named = jnp.zeros((quarter, 128), F32)
    for j in range(routes.shape[0]):
        named = jnp.where(lane == j, as_column(routes[j : j + 1]), named)
    out[:, width:] = named.astype(BF16)


def route_kernel(experts, top, planes, ids, columns, *refs):
    pieces, t_out, rows_out = refs[:4], refs[4], refs[5 : 5 + planes]
    scr, rows_scr = refs[5 + planes :]
    quarter = pieces[0].shape[0]
    width = rows_out[0].shape[1]
    total = 4 * quarter
    lanes = -(-experts // 128) * 128
    for k, piece in enumerate(pieces):
        scr[pl.ds(pl.multiple_of((ids[3] ^ k) * quarter, quarter), quarter)] = piece[...]
    named = scr[:, width : width + 128].astype(F32).astype(I32)
    hot = hot_routes([named[:, j : j + 1] for j in range(top)], lanes)
    row, col = row_index((total, total)), lane_index((total, total))
    shift = quarter.bit_length() - 1
    before = (row >= col) & ((row >> shift) == (col >> shift))
    counts = dot(before.astype(F32).astype(BF16), hot.astype(F32).astype(BF16))
    slots = jnp.where(hot, counts - 1.0, -1.0).astype(BF16)
    slot_rows = columns.shape[1]
    spread = row_index((lanes, slot_rows)) == (ids[3] * planes + columns[0:1])
    slot = dot(slots, spread.astype(F32).astype(BF16))
    lead = row_index((total, slot_rows)) >> shift
    chosen = (slot == columns[2:3].astype(F32)) & (lead == columns[1:2])
    chosen = chosen.astype(F32).astype(BF16)
    t_out[...] = chosen
    t_out.send()
    rows_scr[...] = contract_first(chosen, scr[:, :width])
    split_groups(ids[4], rows_scr, rows_out)


def split_groups(mine, scr, pieces):
    group = pieces[0].shape[0]
    for k, piece in enumerate(pieces):
        first = pl.multiple_of((mine ^ k) * group, group)
        piece[...] = scr[pl.ds(first, group)].astype(BF16)
        piece.send()


def join_groups(mine, pieces, scr):
    group = pieces[0].shape[0]
    for k, piece in enumerate(pieces):
        first = pl.multiple_of((mine ^ k) * group, group)
        scr[pl.ds(first, group)] = piece[...].astype(F32)
    return scr[...].astype(BF16)


def pick_kernel(ids, chosen, attended, att_in, *refs):
    pieces, (rows_out, attended_out, scr) = refs[:4], refs[4:]
    quarter = pieces[0].shape[0]
    for k, piece in enumerate(pieces):
        scr[pl.ds(pl.multiple_of((ids[3] ^ k) * quarter, quarter), quarter)] = piece[...]
    rows_out[...] = contract_first(chosen[...], scr[...]).astype(BF16)
    rows_out.send()
    count, wide = attended.shape
    attended_out[:count] = attended[...]
    mine = att_in[pl.ds(pl.multiple_of(ids[1] * quarter, quarter), quarter)]
    for j in range(mine.shape[1] // wide):
        row = count + j * quarter
        attended_out[row : row + quarter] = mine[:, j * wide : (j + 1) * wide]


def cot_rows_kernel(planes, ids, wd, *refs):
    pieces, (rows_out, grad_out, scr) = refs[:planes], refs[planes:]
    rows = join_groups(ids[4], pieces, scr)
    rows_out[...] = rows
    rows_out.send()
    grad_out[...] = contract_last(rows, wd[...])


def expert_kernel(experts, ids, wg, wu, grad_raw, rows_in, act_out, dg_out, du_out, prob_out, back):
    width = wg.shape[0]
    extra = rows_in.shape[1] - width
    total = rows_in.shape[0]
    rows = rows_in[:, :width]
    lane = lane_index((total, extra))
    mine_high, mine_low = lane == ids[2], lane == ids[2] + experts
    prob = jnp.sum(
        jnp.where(mine_high | mine_low, rows_in[:, width:].astype(F32), 0.0),
        axis=-1,
        keepdims=True,
    )
    prob_out[...] = jnp.broadcast_to(prob, prob_out.shape)
    gate_grad = jnp.zeros((total, 1), F32)
    step = wg.shape[1] // 3
    for c in range(3):
        here = slice(c * step, (c + 1) * step)
        gate, up = dot(rows, wg.part(c)), dot(rows, wu.part(c))
        sig = jax.nn.sigmoid(gate)
        lifted = gate * sig
        act = (lifted * up).astype(BF16)
        act_out[:, here] = act
        raw = grad_raw[:, here]
        gate_grad = gate_grad + jnp.sum(act.astype(F32) * raw, axis=-1, keepdims=True)
        grad_act = prob * raw
        dg_out[:, here] = (grad_act * up * sig * (1.0 + gate * (1.0 - sig))).astype(BF16)
        du_out[:, here] = (grad_act * lifted).astype(BF16)
    for out in (act_out, dg_out, du_out, prob_out):
        out.send()
    grad_in = contract_last(dg_out[...], wg[...]) + contract_last(du_out[...], wu[...])
    back[:, :width] = grad_in.astype(BF16)
    high = gate_grad.astype(BF16).astype(F32)
    tail = jnp.where(mine_high, high, jnp.where(mine_low, gate_grad - high, 0.0))
    back[:, width:] = tail.astype(BF16)


def expert_weights_kernel(rows, dg, du, act, cot_rows, prob, gate_out, up_out, down_out):
    width, units = gate_out.shape
    step = width // 4
    for c in range(4):
        here = slice(c * step, (c + 1) * step)
        left = rows[:, here]
        gate_out[here] = contract_first(left, dg[...])
        gate_out.send(c)
        up_out[here] = contract_first(left, du[...])
        up_out.send(c)
    grad_rows = (cot_rows[...].astype(F32) * prob[:, 0:1]).astype(BF16)
    step = units // 3
    for c in range(3):
        here = slice(c * step, (c + 1) * step)
        down_out[here] = contract_first(act[:, here], grad_rows)
        down_out.send(c)


def out_rows_kernel(act, wd, prob, rows_out):
    rows = dot(act[...], wd[...]).astype(BF16).astype(F32) * prob[:, 0:1]
    rows_out[...] = rows.astype(BF16)


def combine_kernel(ids, chosen, rows, *refs):
    pieces, scr = refs[:-1], refs[-1]
    quarter = pieces[0].shape[0]
    scr[...] = dot(chosen[...], rows[...])
    for k, out in enumerate(pieces):
        first = pl.multiple_of((ids[3] ^ k) * quarter, quarter)
        out[...] = scr[pl.ds(first, quarter)].astype(out.dtype)


def grad_hidden_kernel(ids, hidden_ref, prob_ref, router, cot, post_norm, *refs):
    pieces, low_out, lates, scr = refs[:4], refs[4], refs[5:9], refs[9]
    width = hidden_ref.shape[1]
    experts = router.shape[0]
    total = added(pieces)
    gate_grad = total[:, width : width + experts] + total[:, width + experts : width + 2 * experts]
    prob = prob_ref[...]
    grad_logits = prob * (gate_grad - jnp.sum(prob * gate_grad, axis=-1, keepdims=True))
    high, low = split_low(grad_logits)
    grad_ffn = total[:, :width] + (dot(high, router[...]) + dot(low, router[...]))
    hidden = hidden_ref[...]
    inverse = norm_stats(hidden)
    normed = hidden * inverse
    ffn = (normed * post_norm[...]).astype(BF16)
    grad = cot[...].astype(F32) + norm_backward(grad_ffn, normed, inverse, post_norm[...])
    grad = grad.astype(BF16)
    low_out[...] = grad
    router_part = (contract_first(high, ffn) + contract_first(low, ffn)).astype(BF16)
    post = jnp.sum(grad_ffn * normed, axis=0, keepdims=True)
    post = jnp.where(row_index((16, width)) == 0, post, 0.0).astype(BF16)
    quarter = hidden.shape[0]
    scr[:quarter] = grad
    scr[quarter : quarter + experts] = router_part
    scr[quarter + experts :] = post
    wide = lates[0].shape[1]
    for k, out in enumerate(lates):
        out[...] = scr[:, pl.ds(pl.multiple_of((ids[3] ^ k) * wide, wide), wide)]


def block_at(low, k, blocks):
    value = blocks[0].astype(F32)
    for b in range(1, len(blocks)):
        value = jnp.where((low ^ k) == b, blocks[b].astype(F32), value)
    return value.astype(blocks[0].dtype)


def attend_back_kernel(
    count, ids, q, keys, values, p, raw_ref, wo, cos, sin, gain, *refs
):
    pieces, (gq_out, gain_out, kv_out, branch_out, dq_scr) = refs[:4], refs[4:]
    join_rows(ids[1], pieces, branch_out)
    branch_out.send()
    size, rows = q.shape[2], q.shape[1]
    span = branch_out.shape[0] // SEQS
    heads = rows // span
    scaling = 1.0 / math.sqrt(size)
    step = branch_out.shape[1] // 4
    grad_att = contract_last(branch_out[:, :step], wo.part(0))
    for c in range(1, 4):
        grad_att = grad_att + contract_last(branch_out[:, c * step : (c + 1) * step], wo.part(c))
    grad_att = grad_att.astype(BF16)
    gain_sum = jnp.zeros((1, size), F32)
    for s in range(SEQS):
        rows_s = grad_att[s * span : (s + 1) * span]
        for h in range(heads):
            dq_scr[h * span : (h + 1) * span] = rows_s[:, h * size : (h + 1) * size]
        grad_o = dq_scr[...]
        low = p[s]
        grad_p = contract_last(grad_o, values[s])
        weights = low.astype(F32)
        delta = jnp.sum(weights * grad_p, axis=-1, keepdims=True)
        grad_s = (weights * (grad_p - delta)).astype(BF16)
        grad_v = contract_first(low, grad_o).astype(BF16)
        grad_k = (contract_first(grad_s, q[s]) * scaling).astype(BF16)
        for j in range(count):
            kv_out[j, s * span : (s + 1) * span, :size] = grad_k[j * span : (j + 1) * span]
            kv_out[j, s * span : (s + 1) * span, size:] = grad_v[j * span : (j + 1) * span]
        grad_q = dot(grad_s, keys[s]) * scaling
        cosine, sine = cos[s * span : (s + 1) * span], sin[s * span : (s + 1) * span]
        for h in range(heads):
            grad_rot = grad_q[h * span : (h + 1) * span]
            grad_normed = grad_rot * cosine - half_turn(grad_rot) * sine
            raw = raw_ref[s, h * span : (h + 1) * span]
            inverse = norm_stats(raw)
            normed = raw * inverse
            gain_sum = gain_sum + jnp.sum(grad_normed * normed, axis=0, keepdims=True)
            gq_out[s * span : (s + 1) * span, h * size : (h + 1) * size] = norm_backward(
                grad_normed, normed, inverse, gain[...]
            ).astype(BF16)
    gain_out[...] = gain_sum


def query_in_kernel(gq, wq, out):
    out[...] = contract_last(gq[...], wq[...])


def columns_kernel(lows, rows, ids, early, *refs):
    pieces, (col_out, late) = refs[:4], refs[4:]
    wide = col_out.shape[1] // 2
    part = wide // lows
    for k, piece in enumerate(pieces):
        late[ids[3] ^ k] = piece[...]
    quarter = rows
    experts = late.shape[1] - 16 - quarter
    per_row = early.shape[2] // wide
    row = early.shape[1] - 4 // per_row * quarter + ids[3] // per_row * quarter
    here = pl.ds(pl.multiple_of(row, quarter), quarter)
    lane = pl.ds(pl.multiple_of(ids[3] % per_row * wide, wide), wide)

    def place(target_rows, first, values):
        blocks = [values[:, b * part : (b + 1) * part] for b in range(lows)]
        for k in range(lows):
            col_out[target_rows, first + k * part : first + (k + 1) * part] = block_at(
                ids[5], k, blocks
            ).astype(BF16)

    total = jnp.zeros((late.shape[1] - quarter, wide), F32)
    for j in range(4):
        target = slice(j * quarter, (j + 1) * quarter)
        place(target, 0, early[j, here, lane])
        place(target, wide, late[j, :quarter])
        total = total + late[j, quarter:].astype(F32)
    target = slice(4 * quarter, 4 * quarter + experts)
    place(target, 0, total[:experts])
    post = jnp.where(row_index((experts, wide)) == 0, total[experts : experts + 1], 0.0)
    place(target, wide, post)


def grad_in_kernel(ids, from_q, raw_ref, cos, sin, gain, wk, wv, parts, kv_out, gain_out, own_out, send_out, scr):
    size = wk.shape[1]
    total = added([parts[k] for k in range(parts.shape[0])])
    grad_v = total[:, size:].astype(BF16)
    grad_rot = total[:, :size]
    grad_normed = grad_rot * cos[...] - half_turn(grad_rot) * sin[...]
    raw = raw_ref[...]
    inverse = norm_stats(raw)
    normed = raw * inverse
    gain_out[...] = jnp.sum(grad_normed * normed, axis=0, keepdims=True)
    grad_k = norm_backward(grad_normed, normed, inverse, gain[...]).astype(BF16)
    kv_out[:, :size] = grad_k
    kv_out[:, size:] = grad_v
    full = from_q[...] + contract_last(grad_k, wk[...]) + contract_last(grad_v, wv[...])
    scr[...] = full.astype(BF16)
    half = own_out.shape[0]
    for out, core in ((send_out, 1 - ids[1] % 2), (own_out, ids[1] % 2)):
        out[...] = scr[pl.ds(pl.multiple_of(core * half, half), half)]


def half_kernel(own, other, *refs):
    pieces, (out, sums_out, *sends) = refs[:4], refs[4:]
    out[...] = added((own, other)).astype(BF16)
    total = added(pieces)
    experts, part = total.shape[0], sums_out.shape[1]
    wide = total.shape[1] // 2
    for k, target in enumerate((sums_out, *sends)):
        target[:experts] = total[:, k * part : (k + 1) * part].astype(target.dtype)
        target[experts:] = total[:, wide + k * part : wide + (k + 1) * part].astype(target.dtype)


def token_rows_kernel(ids, tok, gain, branch, own, other, rows_out, gain_out):
    half = own.shape[0]
    mine = pl.ds(pl.multiple_of(ids[1] % 2 * half, half), half)
    grad_in = added((own, other))
    wide = tok[mine].astype(F32)
    inverse = norm_stats(wide)
    normed = wide * inverse
    rows_out[...] = (
        branch[mine].astype(F32) + norm_backward(grad_in, normed, inverse, gain[...])
    ).astype(BF16)
    gain_out[...] = 0.5 * jnp.sum(grad_in * normed, axis=0, keepdims=True)


def sums_kernel(parts, router_out, post_out, q_out, k_out, gain_out):
    devices = parts.shape[0]
    experts, step = router_out.shape[0], router_out.shape[1] // devices
    base = experts // 2
    total = parts[0, base:]
    for d in range(1, devices):
        total = total + parts[d, base:]
    q_out[...] = total[1:2]
    k_out[...] = total[2:3]
    part = gain_out.shape[1]
    for j in range(-(-part // 128)):
        lanes = min(128, part)
        gain_out[:, j * 128 : j * 128 + lanes] = total[3 + j : 4 + j, :lanes]
    group = 128 // step
    for g in range(devices // group):
        held = range(g * group, (g + 1) * group)
        here = slice(g * 128, (g + 1) * 128)
        router_out[:base, here] = jnp.concatenate([parts[d, :base, :step] for d in held], axis=1)
        router_out[base:, here] = jnp.concatenate(
            [parts[d, :base, 64 : 64 + step] for d in held], axis=1
        )
        post_out[:, here] = jnp.concatenate([parts[d, base : base + 1, :step] for d in held], axis=1)


def join_kernel(ids, own, other, gain_part, q_gain, k_gain, *refs):
    sums, (out, parts_out) = refs[:-2], refs[-2:]
    total = added(sums)
    wa_count = lax.axis_size("wa")
    experts, part = total.shape[0] // 2, total.shape[1]
    step = part // wa_count
    mine = total[:, :step]
    for w in range(1, wa_count):
        mine = jnp.where(ids[1] == w, total[:, w * step : (w + 1) * step], mine)
    router_part, post = mine[:experts], mine[experts : experts + 1]
    base = experts // 2
    parts_out[...] = jnp.zeros(parts_out.shape, F32)
    for d in range(parts_out.shape[0]):
        parts_out[d, :base, :step] = router_part[:base]
        parts_out[d, :base, 64 : 64 + step] = router_part[base:]
        parts_out[d, base : base + 1, :step] = post
        parts_out[d, base + 1 : base + 2] = q_gain[...]
        parts_out[d, base + 2 : base + 3] = k_gain[...]
        first = d // wa_count * part
        for j in range(-(-part // 128)):
            lanes = min(128, part)
            parts_out[d, base + 3 + j : base + 4 + j, :lanes] = gain_part[
                :, first + j * 128 : first + j * 128 + lanes
            ]
    parts_out.send()
    half = own.shape[0]
    for source, core in ((own, ids[1] % 2), (other, 1 - ids[1] % 2)):
        out[pl.ds(pl.multiple_of(core * half, half), half)] = source[...]


def token_order(wa, pieces, count, first, scr):
    part = scr.shape[1]
    wa_count = len(pieces)
    quarter = scr.shape[0] // (wa_count * count)
    for k, piece in enumerate(pieces):
        for c in range(count):
            row = pl.multiple_of((c * wa_count + (wa ^ k)) * quarter, quarter)
            scr[pl.ds(row, quarter)] = piece[c * quarter : (c + 1) * quarter, first : first + part]
    return scr[...]


def out_weight_kernel(ids, attended, *refs):
    pieces, (out, *sends) = refs[:4], refs[4:-2]
    scr, att_scr = refs[-2:]
    part, wide, rows = out.shape[1], scr.shape[1], scr.shape[0] // 4
    columns = token_order(ids[1], pieces, 4, wide, scr)
    for j in range(4):
        att_scr[j * rows : (j + 1) * rows] = attended[j, :rows]
    partial = contract_first(att_scr[...], columns)
    for k, target in enumerate((out, *sends)):
        target[...] = partial[:, k * part : (k + 1) * part].astype(target.dtype)


def in_weight_kernel(ids, queries, *refs):
    pieces, kvs, (own, *sends) = refs[:4], refs[4:8], refs[8:-2]
    left, rows = refs[-2:]
    part, width = own.shape[0], queries.shape[1]
    mine = token_order(ids[1], pieces, 4, 0, left)
    partial = contract_first(mine, queries[...])
    for k, send in enumerate(sends, start=1):
        send[:, :width] = partial[k * part : (k + 1) * part].astype(BF16)
    own[:, :width] = partial[:part]
    count = kvs[0].shape[0]
    for k, piece in enumerate(kvs):
        rows[pl.ds(pl.multiple_of((ids[3] ^ k) * count, count), count)] = piece[...]
    partial = contract_first(mine, rows[...])
    for k, send in enumerate(sends, start=1):
        send[:, width:] = partial[k * part : (k + 1) * part].astype(BF16)
        send.send()
    own[:, width:] = partial[:part]


def last_kernel(lows, parts, hidden, out_own, wo_own, win_own, *refs):
    outs, refs = refs[:3], refs[3:]
    wos, wins, refs = refs[: lows - 1], refs[lows - 1 : 2 * lows - 2], refs[2 * lows - 2 :]
    output, wo_out, wq_out, wk_out, wv_out = refs[:5]
    wo_out[...] = added((wo_own, *wos))
    wo_out.send()
    total = added((win_own, *wins))
    width, size = wq_out.shape[1], wk_out.shape[1]
    wq_out[...] = total[:, :width]
    wq_out.send()
    wk_out[...] = total[:, width : width + size]
    wv_out[...] = total[:, width + size :]
    output[...] = (hidden[...] + added((out_own, *outs))).astype(BF16)
    sums_kernel(parts, *refs[5:])


def bind(body, *sizes):
    return lambda *refs: body(*sizes, *refs)


def on_device(
    tokens,
    positions,
    routes,
    query_weight,
    key_matrix,
    value_matrix,
    out_weight,
    query_gain,
    key_gain,
    input_norm,
    post_norm,
    router,
    gate_weight,
    up_weight,
    down_weight,
    cotangent,
):
    lead_count, low_count = lax.axis_size("lead"), lax.axis_size("low")
    ctx_count = lead_count * low_count
    wa_count = lax.axis_size("wa")
    lead_id = lax.axis_index("lead")
    wa_id = lax.axis_index("wa")
    ctx_id = lead_id * low_count + lax.axis_index("low")
    plane_id = lax.axis_index("low") * wa_count + wa_id
    low_id = lax.axis_index("low")
    ids = jnp.stack([ctx_id, wa_id, ctx_id * wa_count + wa_id, lead_id, plane_id, low_id]).astype(I32)
    row_count, width = tokens.shape
    span = row_count // SEQS
    quarter = row_count // wa_count
    size = query_gain.shape[0]
    local_width = query_weight.shape[1]
    heads = local_width // size
    length = span * ctx_count
    experts = router.shape[1]
    top = routes.shape[1]
    hidden_units = gate_weight.shape[2]
    devices = ctx_count * wa_count
    planes = low_count * wa_count
    part = width // ctx_count
    capacity = max(2, (5 * quarter * top + 4 * experts - 1) // (4 * experts))
    group = -(-4 * capacity // 16) * 16 if planes > 8 else 4 * capacity
    slot_rows = planes * group
    extra = -(-2 * experts // 128) * 128
    everywhere, plane, blocks = ("lead", "low", "wa"), ("low", "wa"), ("lead", "low")
    gate_weight, up_weight, down_weight = gate_weight[0], up_weight[0], down_weight[0]
    input_norm, post_norm = input_norm[None], post_norm[None]
    query_gain, key_gain = query_gain[None], key_gain[None]

    halves = np.arange(size) % (size // 2)
    rates = np.exp(halves * (-2.0 * math.log(1000000.0) / size)).astype(np.float32)
    attention_input, kv_own, keys_raw, cosine, sine = vcall(
        kv_kernel,
        [
            ((row_count, width), BF16),
            ((row_count, 2 * size), BF16, "near"),
            ((row_count, size), F32),
            ((row_count, size), F32),
            ((row_count, size), F32),
        ],
        tokens, input_norm, key_matrix, value_matrix, positions[None], jnp.asarray(rates)[None],
        key_gain,
        flops=4 * row_count * width * size,
    )
    kv_all = exchange([kv_own] * ctx_count, blocks)

    q_heads, queries_raw = vcall(
        query_kernel,
        [
            ((SEQS, heads * span, size), BF16),
            ((SEQS, heads * span, size), F32),
        ],
        attention_input, query_weight, cosine, sine, query_gain,
        flops=2 * row_count * width * local_width,
    )

    (cot_send,) = vcall(
        pack_kernel,
        [((quarter, width + 128), BF16, "near")],
        cotangent, routes.T,
        after=[q_heads],
    )
    cot_pieces = exchange([cot_send] * 4, "lead")

    keys_seq, values_seq, weights_low, attended_low, *branch = vcall(
        bind(attend_kernel, ctx_count),
        [
            ((SEQS, length, size), BF16),
            ((SEQS, length, size), BF16),
            ((SEQS, heads * span, length), BF16),
            ((row_count, local_width), BF16),
        ]
        + [((quarter, width), BF16, "near")] * wa_count,
        ids, q_heads, positions[None], out_weight, *near(kv_all),
        scratch=[pltpu.VMEM((row_count, width), BF16)],
        flops=2 * row_count * width * local_width + 4 * row_count * local_width * length,
        megabytes=48,
    )
    branch = exchange(branch, "wa")

    inner = np.arange(slot_rows) % group
    columns = np.zeros((8, slot_rows), np.int32)
    columns[0] = np.arange(slot_rows) // group
    columns[1] = np.minimum(inner // capacity, 3)
    columns[2] = np.where(inner < 4 * capacity, inner % capacity, -5)
    chosen, *cot_groups = vcall(
        bind(route_kernel, experts, top, planes),
        [((row_count, slot_rows), BF16)] + [((group, width), BF16)] * planes,
        ids, jnp.asarray(columns), *near(cot_pieces),
        after=[branch[0]],
        scratch=[
            pltpu.VMEM((4 * quarter, width + 128), BF16),
            pltpu.VMEM((slot_rows, width), F32),
        ],
        flops=2 * slot_rows * row_count * width,
    )
    send, hidden, probs = vcall(
        hidden_kernel,
        [
            ((quarter, width + extra), BF16, "near"),
            ((quarter, width), F32),
            ((quarter, experts), F32),
        ],
        ids, tokens, routes.T, post_norm, router.T, *near(branch),
        after=[chosen],
        flops=2 * quarter * width * experts,
    )

    cot_groups = exchange(cot_groups, plane)
    cot_rows, grad_raw = vcall(
        bind(cot_rows_kernel, planes),
        [((slot_rows, width), BF16), ((slot_rows, hidden_units), F32)],
        ids, down_weight, *cot_groups,
        scratch=[pltpu.VMEM((slot_rows, width), F32)],
        flops=2 * slot_rows * hidden_units * width,
    )

    rows_in, early_rows = vcall(
        pick_kernel,
        [
            ((slot_rows, width + extra), BF16),
            ((row_count + width // local_width * quarter, local_width), BF16),
        ],
        ids, chosen, attended_low, attention_input, *near(exchange([send] * 4, "lead")),
        after=cot_groups[1:],
        scratch=[pltpu.VMEM((row_count, width + extra), BF16)],
        flops=2 * slot_rows * row_count * width,
    )
    rows_in = swap(rows_in, plane)
    early_all = gather(early_rows, "lead").reshape(4, -1, local_width)
    activation, grad_gate_part, grad_up_part, row_prob, back = vcall(
        bind(expert_kernel, experts),
        [
            ((slot_rows, hidden_units), BF16),
            ((slot_rows, hidden_units), BF16),
            ((slot_rows, hidden_units), BF16),
            ((slot_rows, 128), F32),
            ((slot_rows, width + extra), BF16),
        ],
        ids, gate_weight, up_weight, grad_raw, Near(rows_in),
        split={1: 3, 2: 3},
        flops=8 * slot_rows * hidden_units * width,
        megabytes=48,
    )

    grad_gate_weight, grad_up_weight, grad_down_weight = vcall(
        expert_weights_kernel,
        [
            ((width, hidden_units), F32),
            ((width, hidden_units), F32),
            ((hidden_units, width), F32),
        ],
        rows_in, grad_gate_part, grad_up_part, activation, cot_rows, row_prob,
        split={-1: 4, -2: 4, -3: 3},
        flops=6 * slot_rows * hidden_units * width,
        megabytes=40,
    )

    def to_tokens(rows, after):
        return vcall(
            combine_kernel,
            [((quarter, rows.shape[1]), F32, "near")]
            + [((quarter, rows.shape[1]), BF16, "near")] * 3,
            ids, chosen, Near(rows),
            after=after,
            scratch=[pltpu.VMEM((row_count, rows.shape[1]), F32)],
            flops=2 * slot_rows * row_count * width,
        )

    (out_rows,) = vcall(
        out_rows_kernel,
        [((slot_rows, width), BF16)],
        activation, down_weight, row_prob,
        after=[grad_gate_weight],
        flops=2 * slot_rows * hidden_units * width,
    )
    back = swap(back, plane)
    back_pieces = exchange(to_tokens(back, [out_rows, early_all]), "lead")
    out_rows = swap(out_rows, plane)
    grad_low, *late_rows = vcall(
        grad_hidden_kernel,
        [
            ((quarter, width), BF16, "near"),
        ]
        + [((quarter + experts + 16, width // 4), BF16, "near")] * 4,
        ids, hidden, probs, router.T, cotangent, post_norm, *near(back_pieces),
        scratch=[pltpu.VMEM((quarter + experts + 16, width), BF16)],
        flops=4 * quarter * width * experts,
    )

    grad_pieces = exchange([grad_low] * wa_count, "wa")
    late_all = exchange(late_rows, "lead")
    grad_queries, query_gain_part, kv_parts, grad_branch = vcall(
        bind(attend_back_kernel, ctx_count),
        [
            ((row_count, local_width), BF16),
            ((1, size), F32),
            ((ctx_count, row_count, 2 * size), BF16),
            ((row_count, width), BF16),
        ],
        ids, q_heads, keys_seq, values_seq, weights_low, queries_raw, out_weight,
        cosine, sine, query_gain, *near(grad_pieces),
        split={6: 4},
        after=[out_rows] + late_all[1:],
        scratch=[pltpu.VMEM((heads * span, size), BF16)],
        flops=2 * row_count * width * local_width + 8 * row_count * local_width * length,
        megabytes=48,
    )
    kv_parts = swap(kv_parts, blocks)
    queries_all = gather(grad_queries, "lead")
    out_sums = to_tokens(out_rows, [grad_queries])
    out_pieces = exchange(out_sums, "lead")
    (from_queries,) = vcall(
        query_in_kernel,
        [((row_count, width), F32)],
        grad_queries, query_weight,
        flops=2 * row_count * width * local_width,
    )
    (weight_columns,) = vcall(
        bind(columns_kernel, low_count, quarter),
        [((4 * quarter + experts, 2 * low_count * part), BF16)],
        ids, early_all, *late_all,
        after=[from_queries],
        scratch=[pltpu.VMEM((4, quarter + experts + 16, width // 4), BF16)],
    )
    grad_kv, key_gain_part, grad_in_own, grad_in_send = vcall(
        grad_in_kernel,
        [
            ((row_count, 2 * size), BF16, "near"),
            ((1, size), F32),
            ((row_count // 2, width), BF16, "near"),
            ((row_count // 2, width), BF16, "near"),
        ],
        ids, from_queries, keys_raw, cosine, sine, key_gain, key_matrix, value_matrix, Near(kv_parts),
        scratch=[pltpu.VMEM((row_count, width), BF16)],
        flops=4 * row_count * width * size,
    )
    column_pieces = gather_wa_pieces(weight_columns)
    grad_in_half, sums_own, *sends = vcall(
        half_kernel,
        [((row_count // 2, width), BF16, "near"), ((2 * experts, part), F32)]
        + [((2 * experts, part), BF16, "near")] * (low_count - 1),
        Near(grad_in_own), Near(xor_permute(grad_in_send, "wa", 1)),
        *[Rows(piece, 4 * quarter, experts) for piece in column_pieces],
    )
    sums = [sums_own] + [xor_permute(sends[k - 1], "low", k) for k in range(1, low_count)]
    grad_kv_all = exchange([grad_kv] * 4, "lead")
    out_weight_own, *sends = vcall(
        out_weight_kernel,
        [((local_width, part), F32)] + [((local_width, part), BF16)] * (low_count - 1),
        ids, early_all, *column_pieces,
        after=[grad_in_half],
        scratch=[
            pltpu.VMEM((4 * row_count, low_count * part), BF16),
            pltpu.VMEM((4 * row_count, local_width), BF16),
        ],
        flops=8 * row_count * low_count * local_width * part,
    )
    others = [xor_permute(sends[k - 1], "low", k) for k in range(1, low_count)]
    weight_own, *sends = vcall(
        in_weight_kernel,
        [((part, local_width + 2 * size), F32)]
        + [((part, local_width + 2 * size), BF16)] * (low_count - 1),
        ids, queries_all, *column_pieces, *near(grad_kv_all),
        after=[grad_in_half],
        scratch=[
            pltpu.VMEM((4 * row_count, low_count * part), BF16),
            pltpu.VMEM((4 * row_count, 2 * size), BF16),
        ],
        flops=8 * row_count * low_count * (local_width + 2 * size) * part,
    )
    weight_others = [xor_permute(sends[k - 1], "low", k) for k in range(1, low_count)]
    token_rows, grad_input_part = vcall(
        token_rows_kernel,
        [((row_count // 2, width), BF16, "near"), ((1, width), F32)],
        ids, tokens, input_norm, grad_branch,
        Near(grad_in_half), Near(xor_permute(grad_in_half, "wa", 2)),
        after=[out_weight_own],
    )
    grad_tokens, small_parts = vcall(
        join_kernel,
        [
            ((row_count, width), BF16),
            ((devices, -(-(experts // 2 + 3 + -(-part // 128)) // 8) * 8, 128), F32),
        ],
        ids, Near(token_rows), Near(xor_permute(token_rows, "wa", 1)),
        grad_input_part, query_gain_part, key_gain_part,
        *sums,
        after=others,
    )

    (
        output, grad_out_weight, grad_query_weight, grad_key_weight, grad_value_weight,
        grad_router, grad_post_norm, grad_query_gain, grad_key_gain, grad_input_norm,
    ) = vcall(
        bind(last_kernel, low_count),
        [
            ((quarter, width), BF16),
            ((local_width, part), F32),
            ((part, local_width), F32),
            ((part, size), F32),
            ((part, size), F32),
            ((experts, width), F32),
            ((1, width), F32),
            ((1, size), F32),
            ((1, size), F32),
            ((1, part), F32),
        ],
        Near(swap(small_parts, everywhere)), hidden, out_sums[0], out_weight_own, weight_own,
        *out_pieces[1:], *others, *weight_others,
    )
    return (
        output,
        grad_tokens,
        grad_query_weight,
        grad_key_weight,
        grad_value_weight,
        grad_out_weight,
        grad_query_gain[0],
        grad_key_gain[0],
        grad_input_norm[0],
        grad_post_norm[0],
        grad_router.T,
        grad_gate_weight[None],
        grad_up_weight[None],
        grad_down_weight[None],
    )


def solution(mesh):
    ctx_count, wa_count = mesh.devices.shape
    finer = Mesh(mesh.devices.reshape(4, ctx_count // 4, wa_count), ("lead", "low", "wa"))
    return jax.shard_map(
        on_device,
        mesh=finer,
        in_specs=(
            P(("lead", "low"), None),
            P(("lead", "low")),
            P(("lead", "low", "wa"), None),
            P(None, "wa"),
            P(None, "wa"),
            P(None, "wa"),
            P("wa", None),
            P(),
            P(),
            P(),
            P(),
            P(),
            P(("lead", "low", "wa"), None, None),
            P(("lead", "low", "wa"), None, None),
            P(("lead", "low", "wa"), None, None),
            P(("lead", "low", "wa"), None),
        ),
        out_specs=(
            P(("lead", "low", "wa"), None),
            P(("lead", "low"), None),
            P(("lead", "low"), "wa"),
            P(("lead", "low"), "wa"),
            P(("lead", "low"), "wa"),
            P("wa", ("lead", "low")),
            P(),
            P(),
            P(("lead", "low")),
            P(),
            P(),
            P(("lead", "low", "wa"), None, None),
            P(("lead", "low", "wa"), None, None),
            P(("lead", "low", "wa"), None, None),
        ),
        check_vma=False,
    )
```

```python
import math

import jax
import jax.numpy as jnp
import numpy as np
from jax import lax
from jax.experimental import pallas as pl
from jax.experimental.pallas import tpu as pltpu
from jax.sharding import Mesh
from jax.sharding import PartitionSpec as P

SEQS = 2


EPSILON = 1e-06
BF16, F32, I32 = jnp.bfloat16, jnp.float32, jnp.int32


def dot(left, right):
    return jnp.dot(left, right, preferred_element_type=F32)


def contract_last(left, right):
    return lax.dot_general(
        left, right, (((1,), (1,)), ((), ())), preferred_element_type=F32
    )


def contract_first(left, right):
    return lax.dot_general(
        left, right, (((0,), (0,)), ((), ())), preferred_element_type=F32
    )


def split_low(values):
    high = values.astype(BF16)
    return high, (values - high.astype(F32)).astype(BF16)


def norm_stats(values):
    return lax.rsqrt(jnp.mean(values * values, axis=-1, keepdims=True) + EPSILON)


def norm_backward(grad_normed, normed, inverse, gain):
    scaled = grad_normed * gain
    return inverse * (scaled - normed * jnp.mean(scaled * normed, axis=-1, keepdims=True))


def half_turn(values):
    return pltpu.roll(values, values.shape[-1] // 2, values.ndim - 1)


def xor_permute(value, axis, offset):
    names = (axis,) if isinstance(axis, str) else axis
    count = math.prod(lax.axis_size(name) for name in names)
    return lax.ppermute(value, axis, [(i, i ^ offset) for i in range(count)])


def exchange(pieces, axis):
    return [pieces[0]] + [xor_permute(pieces[k], axis, k) for k in range(1, len(pieces))]


def gather_ctx_pieces(value):
    low_count = lax.axis_size("low")
    held = {j * low_count: v for j, v in enumerate(exchange([value] * 4, "lead"))}
    bit = 1
    while bit < low_count:
        held.update({k ^ bit: xor_permute(v, "low", bit) for k, v in list(held.items())})
        bit *= 2
    return [held[k] for k in range(4 * low_count)]


def gather_wa_pieces(value):
    over = xor_permute(value, "wa", 2)
    return [value, xor_permute(value, "wa", 1), over, xor_permute(over, "wa", 1)]


def gather(value, axis):
    return lax.all_gather(value, axis, axis=0, tiled=True)


def swap(value, axes):
    return lax.all_to_all(value, axes, split_axis=0, concat_axis=0, tiled=True)


class Incoming:
    def __init__(self, ref, copies):
        self.ref, self.copies = ref, dict(enumerate(copies))
        self.step = ref.shape[-1] // len(copies)
        self.shape, self.dtype, self.ndim = ref.shape, ref.dtype, ref.ndim

    def ready(self):
        for k in list(self.copies):
            self.copies.pop(k).wait()
        return self.ref

    def part(self, k):
        if k in self.copies:
            self.copies.pop(k).wait()
        return self.ref[:, k * self.step : (k + 1) * self.step]

    def __getitem__(self, index):
        return self.ready()[index]


class Outgoing:
    def __init__(self, ref, copies):
        self.ref, self.copies, self.sent = ref, copies, set()
        self.shape, self.dtype, self.ndim = ref.shape, ref.dtype, ref.ndim

    def send(self, part=None):
        for k, copy in enumerate(self.copies):
            if k not in self.sent and part in (None, k):
                copy.start()
                self.sent.add(k)

    def __getitem__(self, index):
        return self.ref[index]

    def __setitem__(self, index, value):
        self.ref[index] = value


class Near:
    def __init__(self, value):
        self.value = value


class Rows:
    def __init__(self, value, first, count):
        self.value, self.first, self.count = value, first, count


def near(values):
    return [Near(value) for value in values]


def vcall(body, outs, *operands, scratch=(), after=(), split=None, flops=0, megabytes=24):
    split = split or {}
    close = [isinstance(o, Near) for o in operands]
    ranges = {i: (o.first, o.count) for i, o in enumerate(operands) if isinstance(o, Rows)}
    operands = [o.value if isinstance(o, (Near, Rows)) else o for o in operands]
    close_out = [len(o) > 2 for o in outs]
    outs = [o[:2] for o in outs]
    places = [i for i, o in enumerate(operands) if o.ndim > 1 and not close[i]]
    far_outs = [i for i, c in enumerate(close_out) if not c]
    arrays = [
        jax.ShapeDtypeStruct((ranges[i][1],) + operands[i].shape[1:], operands[i].dtype)
        if i in ranges
        else operands[i]
        for i in places
    ]
    sizes = [o.size * o.dtype.itemsize for o in arrays]
    in_parts = [split.get(i, 1) for i in places]
    out_parts = [split.get(-1 - i, 1) for i in far_outs]
    count = len(arrays)

    def kernel(*refs):
        given = list(refs[: len(operands)])
        rest = refs[len(operands) + len(after) :]
        results, rest = rest[: len(outs)], rest[len(outs) :]
        inner = count + len(far_outs)
        buffers, sems, own = rest[:inner], rest[inner], rest[inner + 1 :]
        used = 0
        incoming = []
        for k, i in enumerate(places):
            source, target, parts = given[i], buffers[k], in_parts[k]
            if i in ranges:
                source = source.at[pl.ds(*ranges[i])]
            copies = []
            for c in range(parts):
                step = source.shape[-1] // parts
                if parts > 1:
                    piece = (slice(None), pl.ds(c * step, step))
                    copy = pltpu.make_async_copy(source.at[piece], target.at[piece], sems.at[used])
                else:
                    copy = pltpu.make_async_copy(source, target, sems.at[used])
                copies.append(copy)
                used += 1
            incoming.append(copies)
            given[i] = Incoming(target, copies)
        for c in range(max(in_parts, default=0)):
            for k in sorted(range(count), key=lambda k: sizes[k] / in_parts[k]):
                if c < in_parts[k]:
                    incoming[k][c].start()
        leaving = [Outgoing(result, []) for result in results]
        for k, i in enumerate(far_outs):
            result, source, parts = results[i], buffers[count + k], out_parts[k]
            copies = []
            for c in range(parts):
                step = result.shape[0] // parts
                if parts > 1:
                    piece = pl.ds(c * step, step)
                    copy = pltpu.make_async_copy(source.at[piece], result.at[piece], sems.at[used])
                else:
                    copy = pltpu.make_async_copy(source, result, sems.at[used])
                copies.append(copy)
                used += 1
            leaving[i] = Outgoing(source, copies)
        body(*given, *leaving, *own)
        for value in given:
            if isinstance(value, Incoming):
                value.ready()
        for value in leaving:
            value.send()
        for value in leaving:
            for copy in value.copies:
                copy.wait()

    moved = sum(sizes) + sum(math.prod(s) * jnp.dtype(d).itemsize for s, d in outs)
    in_hbm = pl.BlockSpec(memory_space=pltpu.HBM)

    def pinned(value):
        return pltpu.with_memory_space_constraint(value, pltpu.HBM)

    return pl.pallas_call(
        kernel,
        out_shape=[
            jax.ShapeDtypeStruct(s, d) if c else pltpu.HBM(s, d)
            for (s, d), c in zip(outs, close_out)
        ],
        in_specs=[
            pl.BlockSpec(memory_space=pltpu.SMEM)
            if o.ndim == 1
            else (pl.BlockSpec(memory_space=pltpu.VMEM) if c else in_hbm)
            for o, c in zip(operands, close)
        ]
        + [in_hbm] * len(after),
        out_specs=[pl.BlockSpec(memory_space=pltpu.VMEM) if c else in_hbm for c in close_out],
        scratch_shapes=[pltpu.VMEM(o.shape, o.dtype) for o in arrays]
        + [pltpu.VMEM(*outs[i]) for i in far_outs]
        + [pltpu.SemaphoreType.DMA((max(1, sum(in_parts) + sum(out_parts)),))]
        + list(scratch),
        compiler_params=pltpu.CompilerParams(vmem_limit_bytes=megabytes << 20),
        cost_estimate=pl.CostEstimate(flops=flops, bytes_accessed=moved, transcendentals=0),
    )(*[pinned(o) if i in places else o for i, o in enumerate(operands)], *[pinned(o) for o in after])


def as_column(row):
    count = row.shape[1]
    here = row_index((count, count)) == lane_index((count, count))
    return jnp.sum(jnp.where(here, row.astype(F32), 0.0), axis=-1, keepdims=True)


def lane_index(shape):
    return lax.broadcasted_iota(I32, shape, len(shape) - 1)


def row_index(shape):
    return lax.broadcasted_iota(I32, shape, len(shape) - 2)


def kv_kernel(tok, gain, wk, wv, pos, rates, key_gain, a_out, kv_out, raw_out, cos, sin):
    wide = tok[...].astype(F32)
    low = (wide * norm_stats(wide) * gain[...]).astype(BF16)
    a_out[...] = low
    size = wk.shape[1]
    angles = as_column(pos[...]) * rates[...]
    cos[...] = jnp.cos(angles)
    sine = jnp.sin(angles)
    sin[...] = jnp.where(lane_index(sine.shape) < size // 2, -sine, sine)
    raw = dot(low, wk[...])
    raw_out[...] = raw
    scaled = raw * norm_stats(raw) * key_gain[...]
    key = (scaled * cos[...] + half_turn(scaled) * sin[...]).astype(BF16)
    value = dot(low, wv[...]).astype(BF16)
    kv_out[:, :size] = key
    kv_out[:, size:] = value


def query_kernel(a, wq, cos, sin, query_gain, q_out, raw_out):
    size = cos.shape[1]
    span = a.shape[0] // SEQS
    for h in range(wq.shape[1] // size):
        if h % 2 == 0:
            pair = dot(a[...], wq[:, h * size : (h + 2) * size])
        raw = pair[:, (h % 2) * size : (h % 2 + 1) * size]
        scaled = raw * norm_stats(raw) * query_gain[...]
        rot = (scaled * cos[...] + half_turn(scaled) * sin[...]).astype(BF16)
        for s in range(SEQS):
            q_out[s, h * span : (h + 1) * span] = rot[s * span : (s + 1) * span]
            raw_out[s, h * span : (h + 1) * span] = raw[s * span : (s + 1) * span]


def attend_kernel(count, ids, q, pos, wo, *refs):
    kv, (k_out, v_out, p_out, att_out) = refs[:count], refs[count : count + 4]
    pieces, scr = refs[count + 4 : -1], refs[-1]
    ctx = ids[0]
    span = pos.shape[1] // SEQS
    part = span // 2
    size = q.shape[2]
    rows = q.shape[1]
    length = count * span
    scaling = 1.0 / math.sqrt(size)

    def place_of(owner, inner):
        late = (2 * count - 1 - owner) * part + inner - part
        return jnp.where(inner < part, owner * part + inner, late)

    lane = lane_index((span, length))
    key_place = place_of(lane >> (span.bit_length() - 1), lane & (span - 1))
    query_place = place_of(ctx, row_index((span, length)))
    for s in range(SEQS):
        for j in range(count):
            here = pl.ds(pl.multiple_of((ctx ^ j) * span, span), span)
            k_out[s, here] = kv[j][s * span : (s + 1) * span, :size]
            v_out[s, here] = kv[j][s * span : (s + 1) * span, size:]
        start = query_place - as_column(pos[:, s * span : (s + 1) * span]).astype(I32)
        visible = (key_place <= query_place) & (key_place >= start)
        scores = contract_last(q[s], k_out[s]) * scaling
        scores = scores.reshape(rows // span, span, length)
        scores = jnp.where(visible[None], scores, -1e30)
        weights = jnp.exp(scores - jnp.max(scores, axis=-1, keepdims=True))
        weights = weights / jnp.sum(weights, axis=-1, keepdims=True)
        low = weights.reshape(rows, length).astype(BF16)
        p_out[s] = low
        attended = dot(low, v_out[s]).astype(BF16)
        for h in range(rows // span):
            att_out[s * span : (s + 1) * span, h * size : (h + 1) * size] = attended[
                h * span : (h + 1) * span
            ]
    for out in (k_out, v_out, p_out, att_out):
        out.send()
    split_rows(ids[1], dot(att_out[...], wo[...]), pieces, scr)


def split_rows(wa, full, pieces, scr):
    quarter = pieces[0].shape[0]
    scr[...] = full.astype(BF16)
    for k, piece in enumerate(pieces):
        first = pl.multiple_of((wa ^ k) * quarter, quarter)
        piece[...] = scr[pl.ds(first, quarter)]


def join_rows(wa, pieces, out):
    quarter = pieces[0].shape[0]
    for k, piece in enumerate(pieces):
        out[pl.ds(pl.multiple_of((wa ^ k) * quarter, quarter), quarter)] = piece[...]


def added(pieces):
    total = pieces[0][...].astype(F32)
    for piece in pieces[1:]:
        total = total + piece[...].astype(F32)
    return total


def own_rows(ids, array, quarter):
    return array[pl.ds(pl.multiple_of(ids[1] * quarter, quarter), quarter)].astype(F32)


def hot_routes(columns, width):
    lane = lane_index((columns[0].shape[0], width))
    hot = columns[0] == lane
    for column in columns[1:]:
        hot = hot | (column == lane)
    return hot


def hidden_kernel(ids, tok, routes, post_norm, router, *refs):
    pieces, (send, hidden_out, prob_out) = refs[:-3], refs[-3:]
    quarter, width = pieces[0].shape
    experts = router.shape[0]
    hidden = own_rows(ids, tok, quarter) + added(pieces)
    hidden_out[...] = hidden
    ffn = (hidden * norm_stats(hidden) * post_norm[...]).astype(BF16)
    named = [as_column(routes[j : j + 1]).astype(I32) for j in range(routes.shape[0])]
    hot = hot_routes(named, experts)
    logits = contract_last(ffn, router[...])
    masked = jnp.where(hot, logits, -1e30)
    exps = jnp.where(hot, jnp.exp(logits - jnp.max(masked, axis=-1, keepdims=True)), 0.0)
    probs = exps / jnp.sum(exps, axis=-1, keepdims=True)
    prob_out[...] = probs
    high, low = split_low(probs)
    send[:, :width] = ffn
    if send.shape[1] > width + 2 * experts:
        send[:, width:] = jnp.zeros((quarter, send.shape[1] - width), BF16)
    send[:, width : width + experts] = high
    send[:, width + experts : width + 2 * experts] = low


def pack_kernel(cot, routes, out):
    quarter, width = cot.shape
    out[:, :width] = cot[...]
    lane = lane_index((quarter, 128))
    named = jnp.zeros((quarter, 128), F32)
    for j in range(routes.shape[0]):
        named = jnp.where(lane == j, as_column(routes[j : j + 1]), named)
    out[:, width:] = named.astype(BF16)


def route_kernel(experts, top, planes, ids, columns, *refs):
    pieces, t_out, rows_out = refs[:4], refs[4], refs[5 : 5 + planes]
    scr, rows_scr = refs[5 + planes :]
    quarter = pieces[0].shape[0]
    width = rows_out[0].shape[1]
    total = 4 * quarter
    lanes = -(-experts // 128) * 128
    for k, piece in enumerate(pieces):
        scr[pl.ds(pl.multiple_of((ids[3] ^ k) * quarter, quarter), quarter)] = piece[...]
    named = scr[:, width : width + 128].astype(F32).astype(I32)
    hot = hot_routes([named[:, j : j + 1] for j in range(top)], lanes)
    row, col = row_index((total, total)), lane_index((total, total))
    shift = quarter.bit_length() - 1
    before = (row >= col) & ((row >> shift) == (col >> shift))
    counts = dot(before.astype(F32).astype(BF16), hot.astype(F32).astype(BF16))
    slots = jnp.where(hot, counts - 1.0, -1.0).astype(BF16)
    slot_rows = columns.shape[1]
    spread = row_index((lanes, slot_rows)) == (ids[3] * planes + columns[0:1])
    slot = dot(slots, spread.astype(F32).astype(BF16))
    lead = row_index((total, slot_rows)) >> shift
    chosen = (slot == columns[2:3].astype(F32)) & (lead == columns[1:2])
    chosen = chosen.astype(F32).astype(BF16)
    t_out[...] = chosen
    t_out.send()
    rows_scr[...] = contract_first(chosen, scr[:, :width])
    split_groups(ids[4], rows_scr, rows_out)


def split_groups(mine, scr, pieces):
    group = pieces[0].shape[0]
    for k, piece in enumerate(pieces):
        first = pl.multiple_of((mine ^ k) * group, group)
        piece[...] = scr[pl.ds(first, group)].astype(BF16)
        piece.send()


def join_groups(mine, pieces, scr):
    group = pieces[0].shape[0]
    for k, piece in enumerate(pieces):
        first = pl.multiple_of((mine ^ k) * group, group)
        scr[pl.ds(first, group)] = piece[...].astype(F32)
    return scr[...].astype(BF16)


def pick_kernel(ids, chosen, attended, att_in, *refs):
    pieces, (rows_out, attended_out, scr) = refs[:4], refs[4:]
    quarter = pieces[0].shape[0]
    for k, piece in enumerate(pieces):
        scr[pl.ds(pl.multiple_of((ids[3] ^ k) * quarter, quarter), quarter)] = piece[...]
    rows_out[...] = contract_first(chosen[...], scr[...]).astype(BF16)
    rows_out.send()
    count, wide = attended.shape
    attended_out[:count] = attended[...]
    mine = att_in[pl.ds(pl.multiple_of(ids[1] * quarter, quarter), quarter)]
    for j in range(mine.shape[1] // wide):
        row = count + j * quarter
        attended_out[row : row + quarter] = mine[:, j * wide : (j + 1) * wide]


def cot_rows_kernel(planes, ids, wd, *refs):
    pieces, (rows_out, grad_out, scr) = refs[:planes], refs[planes:]
    rows = join_groups(ids[4], pieces, scr)
    rows_out[...] = rows
    rows_out.send()
    grad_out[...] = contract_last(rows, wd[...])


def expert_kernel(experts, ids, wg, wu, grad_raw, rows_in, act_out, dg_out, du_out, prob_out, back):
    width = wg.shape[0]
    extra = rows_in.shape[1] - width
    total = rows_in.shape[0]
    rows = rows_in[:, :width]
    lane = lane_index((total, extra))
    mine_high, mine_low = lane == ids[2], lane == ids[2] + experts
    prob = jnp.sum(
        jnp.where(mine_high | mine_low, rows_in[:, width:].astype(F32), 0.0),
        axis=-1,
        keepdims=True,
    )
    prob_out[...] = jnp.broadcast_to(prob, prob_out.shape)
    gate_grad = jnp.zeros((total, 1), F32)
    step = wg.shape[1] // 3
    for c in range(3):
        here = slice(c * step, (c + 1) * step)
        gate, up = dot(rows, wg.part(c)), dot(rows, wu.part(c))
        sig = jax.nn.sigmoid(gate)
        lifted = gate * sig
        act = (lifted * up).astype(BF16)
        act_out[:, here] = act
        raw = grad_raw[:, here]
        gate_grad = gate_grad + jnp.sum(act.astype(F32) * raw, axis=-1, keepdims=True)
        grad_act = prob * raw
        dg_out[:, here] = (grad_act * up * sig * (1.0 + gate * (1.0 - sig))).astype(BF16)
        du_out[:, here] = (grad_act * lifted).astype(BF16)
    for out in (act_out, dg_out, du_out, prob_out):
        out.send()
    grad_in = contract_last(dg_out[...], wg[...]) + contract_last(du_out[...], wu[...])
    back[:, :width] = grad_in.astype(BF16)
    high = gate_grad.astype(BF16).astype(F32)
    tail = jnp.where(mine_high, high, jnp.where(mine_low, gate_grad - high, 0.0))
    back[:, width:] = tail.astype(BF16)


def expert_weights_kernel(rows, dg, du, act, cot_rows, prob, gate_out, up_out, down_out):
    width, units = gate_out.shape
    step = width // 4
    for c in range(4):
        here = slice(c * step, (c + 1) * step)
        left = rows[:, here]
        gate_out[here] = contract_first(left, dg[...])
        gate_out.send(c)
        up_out[here] = contract_first(left, du[...])
        up_out.send(c)
    grad_rows = (cot_rows[...].astype(F32) * prob[:, 0:1]).astype(BF16)
    step = units // 3
    for c in range(3):
        here = slice(c * step, (c + 1) * step)
        down_out[here] = contract_first(act[:, here], grad_rows)
        down_out.send(c)


def out_rows_kernel(act, wd, prob, rows_out):
    rows = dot(act[...], wd[...]).astype(BF16).astype(F32) * prob[:, 0:1]
    rows_out[...] = rows.astype(BF16)


def combine_kernel(ids, chosen, rows, *refs):
    pieces, scr = refs[:-1], refs[-1]
    quarter = pieces[0].shape[0]
    scr[...] = dot(chosen[...], rows[...])
    for k, out in enumerate(pieces):
        first = pl.multiple_of((ids[3] ^ k) * quarter, quarter)
        out[...] = scr[pl.ds(first, quarter)].astype(out.dtype)


def grad_hidden_kernel(ids, hidden_ref, prob_ref, router, cot, post_norm, *refs):
    pieces, low_out, lates, scr = refs[:4], refs[4], refs[5:9], refs[9]
    width = hidden_ref.shape[1]
    experts = router.shape[0]
    total = added(pieces)
    gate_grad = total[:, width : width + experts] + total[:, width + experts : width + 2 * experts]
    prob = prob_ref[...]
    grad_logits = prob * (gate_grad - jnp.sum(prob * gate_grad, axis=-1, keepdims=True))
    high, low = split_low(grad_logits)
    grad_ffn = total[:, :width] + (dot(high, router[...]) + dot(low, router[...]))
    hidden = hidden_ref[...]
    inverse = norm_stats(hidden)
    normed = hidden * inverse
    ffn = (normed * post_norm[...]).astype(BF16)
    grad = cot[...].astype(F32) + norm_backward(grad_ffn, normed, inverse, post_norm[...])
    grad = grad.astype(BF16)
    low_out[...] = grad
    router_part = (contract_first(high, ffn) + contract_first(low, ffn)).astype(BF16)
    post = jnp.sum(grad_ffn * normed, axis=0, keepdims=True)
    post = jnp.where(row_index((16, width)) == 0, post, 0.0).astype(BF16)
    quarter = hidden.shape[0]
    scr[:quarter] = grad
    scr[quarter : quarter + experts] = router_part
    scr[quarter + experts :] = post
    wide = lates[0].shape[1]
    for k, out in enumerate(lates):
        out[...] = scr[:, pl.ds(pl.multiple_of((ids[3] ^ k) * wide, wide), wide)]


def block_at(low, k, blocks):
    value = blocks[0].astype(F32)
    for b in range(1, len(blocks)):
        value = jnp.where((low ^ k) == b, blocks[b].astype(F32), value)
    return value.astype(blocks[0].dtype)


def attend_back_kernel(
    count, ids, q, keys, values, p, raw_ref, wo, cos, sin, gain, *refs
):
    pieces, (gq_out, gain_out, kv_out, branch_out, dq_scr) = refs[:4], refs[4:]
    join_rows(ids[1], pieces, branch_out)
    branch_out.send()
    size, rows = q.shape[2], q.shape[1]
    span = branch_out.shape[0] // SEQS
    heads = rows // span
    scaling = 1.0 / math.sqrt(size)
    step = branch_out.shape[1] // 4
    grad_att = contract_last(branch_out[:, :step], wo.part(0))
    for c in range(1, 4):
        grad_att = grad_att + contract_last(branch_out[:, c * step : (c + 1) * step], wo.part(c))
    grad_att = grad_att.astype(BF16)
    gain_sum = jnp.zeros((1, size), F32)
    for s in range(SEQS):
        rows_s = grad_att[s * span : (s + 1) * span]
        for h in range(heads):
            dq_scr[h * span : (h + 1) * span] = rows_s[:, h * size : (h + 1) * size]
        grad_o = dq_scr[...]
        low = p[s]
        grad_p = contract_last(grad_o, values[s])
        weights = low.astype(F32)
        delta = jnp.sum(weights * grad_p, axis=-1, keepdims=True)
        grad_s = (weights * (grad_p - delta)).astype(BF16)
        grad_v = contract_first(low, grad_o).astype(BF16)
        grad_k = (contract_first(grad_s, q[s]) * scaling).astype(BF16)
        for j in range(count):
            kv_out[j, s * span : (s + 1) * span, :size] = grad_k[j * span : (j + 1) * span]
            kv_out[j, s * span : (s + 1) * span, size:] = grad_v[j * span : (j + 1) * span]
        grad_q = dot(grad_s, keys[s]) * scaling
        cosine, sine = cos[s * span : (s + 1) * span], sin[s * span : (s + 1) * span]
        for h in range(heads):
            grad_rot = grad_q[h * span : (h + 1) * span]
            grad_normed = grad_rot * cosine - half_turn(grad_rot) * sine
            raw = raw_ref[s, h * span : (h + 1) * span]
            inverse = norm_stats(raw)
            normed = raw * inverse
            gain_sum = gain_sum + jnp.sum(grad_normed * normed, axis=0, keepdims=True)
            gq_out[s * span : (s + 1) * span, h * size : (h + 1) * size] = norm_backward(
                grad_normed, normed, inverse, gain[...]
            ).astype(BF16)
    gain_out[...] = gain_sum


def query_in_kernel(gq, wq, out):
    out[...] = contract_last(gq[...], wq[...])


def columns_kernel(lows, rows, ids, early, *refs):
    pieces, (col_out, late) = refs[:4], refs[4:]
    wide = col_out.shape[1] // 2
    part = wide // lows
    for k, piece in enumerate(pieces):
        late[ids[3] ^ k] = piece[...]
    quarter = rows
    experts = late.shape[1] - 16 - quarter
    per_row = early.shape[2] // wide
    row = early.shape[1] - 4 // per_row * quarter + ids[3] // per_row * quarter
    here = pl.ds(pl.multiple_of(row, quarter), quarter)
    lane = pl.ds(pl.multiple_of(ids[3] % per_row * wide, wide), wide)

    def place(target_rows, first, values):
        blocks = [values[:, b * part : (b + 1) * part] for b in range(lows)]
        for k in range(lows):
            col_out[target_rows, first + k * part : first + (k + 1) * part] = block_at(
                ids[5], k, blocks
            ).astype(BF16)

    total = jnp.zeros((late.shape[1] - quarter, wide), F32)
    for j in range(4):
        target = slice(j * quarter, (j + 1) * quarter)
        place(target, 0, early[j, here, lane])
        place(target, wide, late[j, :quarter])
        total = total + late[j, quarter:].astype(F32)
    target = slice(4 * quarter, 4 * quarter + experts)
    place(target, 0, total[:experts])
    post = jnp.where(row_index((experts, wide)) == 0, total[experts : experts + 1], 0.0)
    place(target, wide, post)


def grad_in_kernel(ids, from_q, raw_ref, cos, sin, gain, wk, wv, parts, kv_out, gain_out, own_out, send_out, scr):
    size = wk.shape[1]
    total = added([parts[k] for k in range(parts.shape[0])])
    grad_v = total[:, size:].astype(BF16)
    grad_rot = total[:, :size]
    grad_normed = grad_rot * cos[...] - half_turn(grad_rot) * sin[...]
    raw = raw_ref[...]
    inverse = norm_stats(raw)
    normed = raw * inverse
    gain_out[...] = jnp.sum(grad_normed * normed, axis=0, keepdims=True)
    grad_k = norm_backward(grad_normed, normed, inverse, gain[...]).astype(BF16)
    kv_out[:, :size] = grad_k
    kv_out[:, size:] = grad_v
    full = from_q[...] + contract_last(grad_k, wk[...]) + contract_last(grad_v, wv[...])
    scr[...] = full.astype(BF16)
    half = own_out.shape[0]
    for out, core in ((send_out, 1 - ids[1] % 2), (own_out, ids[1] % 2)):
        out[...] = scr[pl.ds(pl.multiple_of(core * half, half), half)]


def half_kernel(own, other, *refs):
    pieces, (out, sums_out, *sends) = refs[:4], refs[4:]
    out[...] = added((own, other)).astype(BF16)
    total = added(pieces)
    experts, part = total.shape[0], sums_out.shape[1]
    wide = total.shape[1] // 2
    for k, target in enumerate((sums_out, *sends)):
        target[:experts] = total[:, k * part : (k + 1) * part].astype(target.dtype)
        target[experts:] = total[:, wide + k * part : wide + (k + 1) * part].astype(target.dtype)


def token_rows_kernel(ids, tok, gain, branch, own, other, rows_out, gain_out):
    half = own.shape[0]
    mine = pl.ds(pl.multiple_of(ids[1] % 2 * half, half), half)
    grad_in = added((own, other))
    wide = tok[mine].astype(F32)
    inverse = norm_stats(wide)
    normed = wide * inverse
    rows_out[...] = (
        branch[mine].astype(F32) + norm_backward(grad_in, normed, inverse, gain[...])
    ).astype(BF16)
    gain_out[...] = 0.5 * jnp.sum(grad_in * normed, axis=0, keepdims=True)


def sums_kernel(parts, router_out, post_out, q_out, k_out, gain_out):
    devices = parts.shape[0]
    experts, step = router_out.shape[0], router_out.shape[1] // devices
    base = experts // 2
    total = parts[0].astype(F32)[base:]
    for d in range(1, devices):
        total = total + parts[d].astype(F32)[base:]
    q_out[...] = total[1:2]
    k_out[...] = total[2:3]
    part = gain_out.shape[1]
    for j in range(-(-part // 128)):
        lanes = min(128, part)
        gain_out[:, j * 128 : j * 128 + lanes] = total[3 + j : 4 + j, :lanes]
    group = 128 // step
    for g in range(devices // group):
        held = range(g * group, (g + 1) * group)
        here = slice(g * 128, (g + 1) * 128)
        wide = [parts[d].astype(F32) for d in held]
        router_out[:base, here] = jnp.concatenate([w[:base, :step] for w in wide], axis=1)
        router_out[base:, here] = jnp.concatenate(
            [w[:base, 64 : 64 + step] for w in wide], axis=1
        )
        post_out[:, here] = jnp.concatenate([w[base : base + 1, :step] for w in wide], axis=1)


def join_kernel(ids, own, other, gain_part, q_gain, k_gain, *refs):
    sums, (out, parts_low, parts_out) = refs[:-3], refs[-3:]
    total = added(sums)
    wa_count = lax.axis_size("wa")
    experts, part = total.shape[0] // 2, total.shape[1]
    step = part // wa_count
    mine = total[:, :step]
    for w in range(1, wa_count):
        mine = jnp.where(ids[1] == w, total[:, w * step : (w + 1) * step], mine)
    router_part, post = mine[:experts], mine[experts : experts + 1]
    base = experts // 2
    parts_out[...] = jnp.zeros(parts_out.shape, F32)
    for d in range(parts_out.shape[0]):
        parts_out[d, :base, :step] = router_part[:base]
        parts_out[d, :base, 64 : 64 + step] = router_part[base:]
        parts_out[d, base : base + 1, :step] = post
        parts_out[d, base + 1 : base + 2] = q_gain[...]
        parts_out[d, base + 2 : base + 3] = k_gain[...]
        first = d // wa_count * part
        for j in range(-(-part // 128)):
            lanes = min(128, part)
            parts_out[d, base + 3 + j : base + 4 + j, :lanes] = gain_part[
                :, first + j * 128 : first + j * 128 + lanes
            ]
    parts_low[...] = parts_out[...].astype(BF16)
    parts_low.send()
    half = own.shape[0]
    for source, core in ((own, ids[1] % 2), (other, 1 - ids[1] % 2)):
        out[pl.ds(pl.multiple_of(core * half, half), half)] = source[...]


def token_order(wa, pieces, count, first, scr):
    part = scr.shape[1]
    wa_count = len(pieces)
    quarter = scr.shape[0] // (wa_count * count)
    for k, piece in enumerate(pieces):
        for c in range(count):
            row = pl.multiple_of((c * wa_count + (wa ^ k)) * quarter, quarter)
            scr[pl.ds(row, quarter)] = piece[c * quarter : (c + 1) * quarter, first : first + part]
    return scr[...]


def out_weight_kernel(ids, attended, *refs):
    pieces, (out, *sends) = refs[:4], refs[4:-2]
    scr, att_scr = refs[-2:]
    part, wide, rows = out.shape[1], scr.shape[1], scr.shape[0] // 4
    columns = token_order(ids[1], pieces, 4, wide, scr)
    for j in range(4):
        att_scr[j * rows : (j + 1) * rows] = attended[j, :rows]
    partial = contract_first(att_scr[...], columns)
    for k, target in enumerate((out, *sends)):
        target[...] = partial[:, k * part : (k + 1) * part].astype(target.dtype)


def in_weight_kernel(ids, queries, *refs):
    pieces, (own, *sends) = refs[:4], refs[4:-1]
    left, part = refs[-1], own.shape[0]
    partial = contract_first(token_order(ids[1], pieces, 4, 0, left), queries[...])
    for k, send in enumerate(sends, start=1):
        send[...] = partial[k * part : (k + 1) * part].astype(BF16)
        send.send()
    own[...] = partial[:part]


def kv_weight_kernel(ids, *refs):
    kvs, refs, rows = refs[:4], refs[4:-1], refs[-1]
    count = kvs[0].shape[0]
    for k, piece in enumerate(kvs):
        rows[pl.ds(pl.multiple_of((ids[3] ^ k) * count, count), count)] = piece[...]
    in_weight_kernel(ids, rows, *refs)


def last_kernel(lows, parts, hidden, out_own, wo_own, wq_own, kv_own, *refs):
    outs, refs = refs[:3], refs[3:]
    wos, wqs, kvs = [refs[j * (lows - 1) : (j + 1) * (lows - 1)] for j in range(3)]
    refs = refs[3 * (lows - 1) :]
    output, wo_out, wq_out, wk_out, wv_out = refs[:5]
    wo_out[...] = added((wo_own, *wos))
    wo_out.send()
    wq_out[...] = added((wq_own, *wqs))
    wq_out.send()
    total = added((kv_own, *kvs))
    size = wk_out.shape[1]
    wk_out[...] = total[:, :size]
    wv_out[...] = total[:, size:]
    output[...] = (hidden[...] + added((out_own, *outs))).astype(BF16)
    sums_kernel(parts, *refs[5:])


def bind(body, *sizes):
    return lambda *refs: body(*sizes, *refs)


def on_device(
    tokens,
    positions,
    routes,
    query_weight,
    key_matrix,
    value_matrix,
    out_weight,
    query_gain,
    key_gain,
    input_norm,
    post_norm,
    router,
    gate_weight,
    up_weight,
    down_weight,
    cotangent,
):
    lead_count, low_count = lax.axis_size("lead"), lax.axis_size("low")
    ctx_count = lead_count * low_count
    wa_count = lax.axis_size("wa")
    lead_id = lax.axis_index("lead")
    wa_id = lax.axis_index("wa")
    ctx_id = lead_id * low_count + lax.axis_index("low")
    plane_id = lax.axis_index("low") * wa_count + wa_id
    low_id = lax.axis_index("low")
    ids = jnp.stack([ctx_id, wa_id, ctx_id * wa_count + wa_id, lead_id, plane_id, low_id]).astype(I32)
    row_count, width = tokens.shape
    span = row_count // SEQS
    quarter = row_count // wa_count
    size = query_gain.shape[0]
    local_width = query_weight.shape[1]
    heads = local_width // size
    length = span * ctx_count
    experts = router.shape[1]
    top = routes.shape[1]
    hidden_units = gate_weight.shape[2]
    devices = ctx_count * wa_count
    planes = low_count * wa_count
    part = width // ctx_count
    capacity = max(2, (5 * quarter * top + 4 * experts - 1) // (4 * experts))
    group = -(-4 * capacity // 16) * 16 if planes > 8 else 4 * capacity
    slot_rows = planes * group
    extra = -(-2 * experts // 128) * 128
    everywhere, plane, blocks = ("lead", "low", "wa"), ("low", "wa"), ("lead", "low")
    gate_weight, up_weight, down_weight = gate_weight[0], up_weight[0], down_weight[0]
    input_norm, post_norm = input_norm[None], post_norm[None]
    query_gain, key_gain = query_gain[None], key_gain[None]

    halves = np.arange(size) % (size // 2)
    rates = np.exp(halves * (-2.0 * math.log(1000000.0) / size)).astype(np.float32)
    attention_input, kv_own, keys_raw, cosine, sine = vcall(
        kv_kernel,
        [
            ((row_count, width), BF16),
            ((row_count, 2 * size), BF16, "near"),
            ((row_count, size), F32),
            ((row_count, size), F32),
            ((row_count, size), F32),
        ],
        tokens, input_norm, key_matrix, value_matrix, positions[None], jnp.asarray(rates)[None],
        key_gain,
        flops=4 * row_count * width * size,
    )
    kv_all = exchange([kv_own] * ctx_count, blocks)

    q_heads, queries_raw = vcall(
        query_kernel,
        [
            ((SEQS, heads * span, size), BF16),
            ((SEQS, heads * span, size), F32),
        ],
        attention_input, query_weight, cosine, sine, query_gain,
        flops=2 * row_count * width * local_width,
    )

    (cot_send,) = vcall(
        pack_kernel,
        [((quarter, width + 128), BF16, "near")],
        cotangent, routes.T,
        after=[q_heads],
    )
    cot_pieces = exchange([cot_send] * 4, "lead")

    keys_seq, values_seq, weights_low, attended_low, *branch = vcall(
        bind(attend_kernel, ctx_count),
        [
            ((SEQS, length, size), BF16),
            ((SEQS, length, size), BF16),
            ((SEQS, heads * span, length), BF16),
            ((row_count, local_width), BF16),
        ]
        + [((quarter, width), BF16, "near")] * wa_count,
        ids, q_heads, positions[None], out_weight, *near(kv_all),
        scratch=[pltpu.VMEM((row_count, width), BF16)],
        flops=2 * row_count * width * local_width + 4 * row_count * local_width * length,
        megabytes=48,
    )
    branch = exchange(branch, "wa")

    inner = np.arange(slot_rows) % group
    columns = np.zeros((8, slot_rows), np.int32)
    columns[0] = np.arange(slot_rows) // group
    columns[1] = np.minimum(inner // capacity, 3)
    columns[2] = np.where(inner < 4 * capacity, inner % capacity, -5)
    chosen, *cot_groups = vcall(
        bind(route_kernel, experts, top, planes),
        [((row_count, slot_rows), BF16)] + [((group, width), BF16)] * planes,
        ids, jnp.asarray(columns), *near(cot_pieces),
        after=[branch[0]],
        scratch=[
            pltpu.VMEM((4 * quarter, width + 128), BF16),
            pltpu.VMEM((slot_rows, width), F32),
        ],
        flops=2 * slot_rows * row_count * width,
    )
    send, hidden, probs = vcall(
        hidden_kernel,
        [
            ((quarter, width + extra), BF16, "near"),
            ((quarter, width), F32),
            ((quarter, experts), F32),
        ],
        ids, tokens, routes.T, post_norm, router.T, *near(branch),
        after=[chosen],
        flops=2 * quarter * width * experts,
    )

    cot_groups = exchange(cot_groups, plane)
    cot_rows, grad_raw = vcall(
        bind(cot_rows_kernel, planes),
        [((slot_rows, width), BF16), ((slot_rows, hidden_units), F32)],
        ids, down_weight, *cot_groups,
        scratch=[pltpu.VMEM((slot_rows, width), F32)],
        flops=2 * slot_rows * hidden_units * width,
    )

    rows_in, early_rows = vcall(
        pick_kernel,
        [
            ((slot_rows, width + extra), BF16),
            ((row_count + width // local_width * quarter, local_width), BF16),
        ],
        ids, chosen, attended_low, attention_input, *near(exchange([send] * 4, "lead")),
        after=cot_groups[1:],
        scratch=[pltpu.VMEM((row_count, width + extra), BF16)],
        flops=2 * slot_rows * row_count * width,
    )
    rows_in = swap(rows_in, plane)
    early_all = gather(early_rows, "lead").reshape(4, -1, local_width)
    activation, grad_gate_part, grad_up_part, row_prob, back = vcall(
        bind(expert_kernel, experts),
        [
            ((slot_rows, hidden_units), BF16),
            ((slot_rows, hidden_units), BF16),
            ((slot_rows, hidden_units), BF16),
            ((slot_rows, 128), F32),
            ((slot_rows, width + extra), BF16),
        ],
        ids, gate_weight, up_weight, grad_raw, Near(rows_in),
        split={1: 3, 2: 3},
        flops=8 * slot_rows * hidden_units * width,
        megabytes=48,
    )

    grad_gate_weight, grad_up_weight, grad_down_weight = vcall(
        expert_weights_kernel,
        [
            ((width, hidden_units), F32),
            ((width, hidden_units), F32),
            ((hidden_units, width), F32),
        ],
        rows_in, grad_gate_part, grad_up_part, activation, cot_rows, row_prob,
        split={-1: 4, -2: 4, -3: 3},
        flops=6 * slot_rows * hidden_units * width,
        megabytes=40,
    )

    def to_tokens(rows, after):
        return vcall(
            combine_kernel,
            [((quarter, rows.shape[1]), F32, "near")]
            + [((quarter, rows.shape[1]), BF16, "near")] * 3,
            ids, chosen, Near(rows),
            after=after,
            scratch=[pltpu.VMEM((row_count, rows.shape[1]), F32)],
            flops=2 * slot_rows * row_count * width,
        )

    back = swap(back, plane)
    back_pieces = exchange(to_tokens(back, [grad_gate_weight, early_all]), "lead")
    (out_rows,) = vcall(
        out_rows_kernel,
        [((slot_rows, width), BF16)],
        activation, down_weight, row_prob,
        after=back_pieces[1:],
        flops=2 * slot_rows * hidden_units * width,
    )
    out_made = out_rows
    out_rows = swap(out_rows, plane)
    grad_low, *late_rows = vcall(
        grad_hidden_kernel,
        [
            ((quarter, width), BF16, "near"),
        ]
        + [((quarter + experts + 16, width // 4), BF16, "near")] * 4,
        ids, hidden, probs, router.T, cotangent, post_norm, *near(back_pieces),
        scratch=[pltpu.VMEM((quarter + experts + 16, width), BF16)],
        flops=4 * quarter * width * experts,
    )

    grad_pieces = exchange([grad_low] * wa_count, "wa")
    late_all = exchange(late_rows, "lead")
    grad_queries, query_gain_part, kv_parts, grad_branch = vcall(
        bind(attend_back_kernel, ctx_count),
        [
            ((row_count, local_width), BF16),
            ((1, size), F32),
            ((ctx_count, row_count, 2 * size), BF16),
            ((row_count, width), BF16),
        ],
        ids, q_heads, keys_seq, values_seq, weights_low, queries_raw, out_weight,
        cosine, sine, query_gain, *near(grad_pieces),
        split={6: 4},
        after=late_all[1:] + [out_made],
        scratch=[pltpu.VMEM((heads * span, size), BF16)],
        flops=2 * row_count * width * local_width + 8 * row_count * local_width * length,
        megabytes=48,
    )
    kv_parts = swap(kv_parts, blocks)
    queries_all = gather(grad_queries, "lead")
    (from_queries,) = vcall(
        query_in_kernel,
        [((row_count, width), F32)],
        grad_queries, query_weight,
        flops=2 * row_count * width * local_width,
    )
    (weight_columns,) = vcall(
        bind(columns_kernel, low_count, quarter),
        [((4 * quarter + experts, 2 * low_count * part), BF16)],
        ids, early_all, *late_all,
        after=[from_queries],
        scratch=[pltpu.VMEM((4, quarter + experts + 16, width // 4), BF16)],
    )
    grad_kv, key_gain_part, grad_in_own, grad_in_send = vcall(
        grad_in_kernel,
        [
            ((row_count, 2 * size), BF16, "near"),
            ((1, size), F32),
            ((row_count // 2, width), BF16, "near"),
            ((row_count // 2, width), BF16, "near"),
        ],
        ids, from_queries, keys_raw, cosine, sine, key_gain, key_matrix, value_matrix, Near(kv_parts),
        scratch=[pltpu.VMEM((row_count, width), BF16)],
        flops=4 * row_count * width * size,
    )
    column_pieces = gather_wa_pieces(weight_columns)
    grad_in_half, sums_own, *sends = vcall(
        half_kernel,
        [((row_count // 2, width), BF16, "near"), ((2 * experts, part), F32)]
        + [((2 * experts, part), BF16, "near")] * (low_count - 1),
        Near(grad_in_own), Near(xor_permute(grad_in_send, "wa", 1)),
        *[Rows(piece, 4 * quarter, experts) for piece in column_pieces],
    )
    out_sums = to_tokens(out_rows, [grad_in_half])
    out_pieces = exchange(out_sums, "lead")
    sums = [sums_own] + [xor_permute(sends[k - 1], "low", k) for k in range(1, low_count)]
    grad_kv_all = exchange([grad_kv] * 4, "lead")
    out_weight_own, *sends = vcall(
        out_weight_kernel,
        [((local_width, part), F32)] + [((local_width, part), BF16)] * (low_count - 1),
        ids, early_all, *column_pieces,
        after=[grad_in_half],
        scratch=[
            pltpu.VMEM((4 * row_count, low_count * part), BF16),
            pltpu.VMEM((4 * row_count, local_width), BF16),
        ],
        flops=8 * row_count * low_count * local_width * part,
    )
    others = [xor_permute(sends[k - 1], "low", k) for k in range(1, low_count)]
    weight_own, *sends = vcall(
        in_weight_kernel,
        [((part, local_width), F32)] + [((part, local_width), BF16)] * (low_count - 1),
        ids, queries_all, *column_pieces,
        after=[grad_in_half],
        scratch=[pltpu.VMEM((4 * row_count, low_count * part), BF16)],
        flops=8 * row_count * low_count * local_width * part,
    )
    weight_others = [xor_permute(sends[k - 1], "low", k) for k in range(1, low_count)]
    token_rows, grad_input_part = vcall(
        token_rows_kernel,
        [((row_count // 2, width), BF16, "near"), ((1, width), F32)],
        ids, tokens, input_norm, grad_branch,
        Near(grad_in_half), Near(xor_permute(grad_in_half, "wa", 2)),
        after=[out_weight_own, weight_own] + grad_kv_all[1:],
    )
    sum_rows = -(-(experts // 2 + 3 + -(-part // 128)) // 16) * 16
    grad_tokens, small_parts = vcall(
        join_kernel,
        [
            ((row_count, width), BF16),
            ((devices, sum_rows, 128), BF16),
        ],
        ids, Near(token_rows), Near(xor_permute(token_rows, "wa", 1)),
        grad_input_part, query_gain_part, key_gain_part,
        *sums,
        after=others + [out_sums[0]],
        scratch=[pltpu.VMEM((devices, sum_rows, 128), F32)],
    )

    kv_weight_own, *sends = vcall(
        kv_weight_kernel,
        [((part, 2 * size), F32)] + [((part, 2 * size), BF16)] * (low_count - 1),
        ids, *grad_kv_all, *column_pieces,
        after=[small_parts],
        scratch=[
            pltpu.VMEM((4 * row_count, low_count * part), BF16),
            pltpu.VMEM((4 * row_count, 2 * size), BF16),
        ],
        flops=8 * row_count * low_count * 2 * size * part,
    )
    kv_others = [xor_permute(sends[k - 1], "low", k) for k in range(1, low_count)]
    (
        output, grad_out_weight, grad_query_weight, grad_key_weight, grad_value_weight,
        grad_router, grad_post_norm, grad_query_gain, grad_key_gain, grad_input_norm,
    ) = vcall(
        bind(last_kernel, low_count),
        [
            ((quarter, width), BF16),
            ((local_width, part), F32),
            ((part, local_width), F32),
            ((part, size), F32),
            ((part, size), F32),
            ((experts, width), F32),
            ((1, width), F32),
            ((1, size), F32),
            ((1, size), F32),
            ((1, part), F32),
        ],
        Near(swap(small_parts, everywhere)), hidden, out_sums[0], out_weight_own, weight_own,
        kv_weight_own, *out_pieces[1:], *others, *weight_others, *near(kv_others),
    )
    return (
        output,
        grad_tokens,
        grad_query_weight,
        grad_key_weight,
        grad_value_weight,
        grad_out_weight,
        grad_query_gain[0],
        grad_key_gain[0],
        grad_input_norm[0],
        grad_post_norm[0],
        grad_router.T,
        grad_gate_weight[None],
        grad_up_weight[None],
        grad_down_weight[None],
    )


def solution(mesh):
    ctx_count, wa_count = mesh.devices.shape
    finer = Mesh(mesh.devices.reshape(4, ctx_count // 4, wa_count), ("lead", "low", "wa"))
    return jax.shard_map(
        on_device,
        mesh=finer,
        in_specs=(
            P(("lead", "low"), None),
            P(("lead", "low")),
            P(("lead", "low", "wa"), None),
            P(None, "wa"),
            P(None, "wa"),
            P(None, "wa"),
            P("wa", None),
            P(),
            P(),
            P(),
            P(),
            P(),
            P(("lead", "low", "wa"), None, None),
            P(("lead", "low", "wa"), None, None),
            P(("lead", "low", "wa"), None, None),
            P(("lead", "low", "wa"), None),
        ),
        out_specs=(
            P(("lead", "low", "wa"), None),
            P(("lead", "low"), None),
            P(("lead", "low"), "wa"),
            P(("lead", "low"), "wa"),
            P(("lead", "low"), "wa"),
            P("wa", ("lead", "low")),
            P(),
            P(),
            P(("lead", "low")),
            P(),
            P(),
            P(("lead", "low", "wa"), None, None),
            P(("lead", "low", "wa"), None, None),
            P(("lead", "low", "wa"), None, None),
        ),
        check_vma=False,
    )
```

```python
import math

import jax
import jax.numpy as jnp
import numpy as np
from jax import lax
from jax.experimental import pallas as pl
from jax.experimental.pallas import tpu as pltpu
from jax.sharding import Mesh
from jax.sharding import PartitionSpec as P

SEQS = 2


EPSILON = 1e-06
BF16, F32, I32 = jnp.bfloat16, jnp.float32, jnp.int32


def dot(left, right):
    return jnp.dot(left, right, preferred_element_type=F32)


def contract_last(left, right):
    return lax.dot_general(
        left, right, (((1,), (1,)), ((), ())), preferred_element_type=F32
    )


def contract_first(left, right):
    return lax.dot_general(
        left, right, (((0,), (0,)), ((), ())), preferred_element_type=F32
    )


def split_low(values):
    high = values.astype(BF16)
    return high, (values - high.astype(F32)).astype(BF16)


def norm_stats(values):
    return lax.rsqrt(jnp.mean(values * values, axis=-1, keepdims=True) + EPSILON)


def norm_backward(grad_normed, normed, inverse, gain):
    scaled = grad_normed * gain
    return inverse * (scaled - normed * jnp.mean(scaled * normed, axis=-1, keepdims=True))


def half_turn(values):
    return pltpu.roll(values, values.shape[-1] // 2, values.ndim - 1)


def xor_permute(value, axis, offset):
    names = (axis,) if isinstance(axis, str) else axis
    count = math.prod(lax.axis_size(name) for name in names)
    return lax.ppermute(value, axis, [(i, i ^ offset) for i in range(count)])


def exchange(pieces, axis):
    return [pieces[0]] + [xor_permute(pieces[k], axis, k) for k in range(1, len(pieces))]


def gather_ctx_pieces(value):
    low_count = lax.axis_size("low")
    held = {j * low_count: v for j, v in enumerate(exchange([value] * 4, "lead"))}
    bit = 1
    while bit < low_count:
        held.update({k ^ bit: xor_permute(v, "low", bit) for k, v in list(held.items())})
        bit *= 2
    return [held[k] for k in range(4 * low_count)]


def gather_wa_pieces(value):
    over = xor_permute(value, "wa", 2)
    return [value, xor_permute(value, "wa", 1), over, xor_permute(over, "wa", 1)]


def gather(value, axis):
    return lax.all_gather(value, axis, axis=0, tiled=True)


def swap(value, axes):
    return lax.all_to_all(value, axes, split_axis=0, concat_axis=0, tiled=True)


class Incoming:
    def __init__(self, ref, copies):
        self.ref, self.copies = ref, dict(enumerate(copies))
        self.step = ref.shape[-1] // len(copies)
        self.shape, self.dtype, self.ndim = ref.shape, ref.dtype, ref.ndim

    def ready(self):
        for k in list(self.copies):
            self.copies.pop(k).wait()
        return self.ref

    def part(self, k):
        if k in self.copies:
            self.copies.pop(k).wait()
        return self.ref[:, k * self.step : (k + 1) * self.step]

    def __getitem__(self, index):
        return self.ready()[index]


class Outgoing:
    def __init__(self, ref, copies):
        self.ref, self.copies, self.sent = ref, copies, set()
        self.shape, self.dtype, self.ndim = ref.shape, ref.dtype, ref.ndim

    def send(self, part=None):
        for k, copy in enumerate(self.copies):
            if k not in self.sent and part in (None, k):
                copy.start()
                self.sent.add(k)

    def __getitem__(self, index):
        return self.ref[index]

    def __setitem__(self, index, value):
        self.ref[index] = value


class Near:
    def __init__(self, value):
        self.value = value


class Rows:
    def __init__(self, value, first, count):
        self.value, self.first, self.count = value, first, count


def near(values):
    return [Near(value) for value in values]


def vcall(body, outs, *operands, scratch=(), after=(), split=None, loose=(), flops=0, megabytes=24):
    split = split or {}
    close = [isinstance(o, Near) for o in operands]
    ranges = {i: (o.first, o.count) for i, o in enumerate(operands) if isinstance(o, Rows)}
    operands = [o.value if isinstance(o, (Near, Rows)) else o for o in operands]
    close_out = [len(o) > 2 for o in outs]
    outs = [o[:2] for o in outs]
    places = [i for i, o in enumerate(operands) if o.ndim > 1 and not close[i]]
    far_outs = [i for i, c in enumerate(close_out) if not c]
    arrays = [
        jax.ShapeDtypeStruct((ranges[i][1],) + operands[i].shape[1:], operands[i].dtype)
        if i in ranges
        else operands[i]
        for i in places
    ]
    sizes = [o.size * o.dtype.itemsize for o in arrays]
    in_parts = [split.get(i, 1) for i in places]
    out_parts = [split.get(-1 - i, 1) for i in far_outs]
    out_parts = [len(p) if isinstance(p, tuple) else p for p in out_parts]
    count = len(arrays)

    def kernel(*refs):
        given = list(refs[: len(operands)])
        rest = refs[len(operands) + len(after) + len(loose) :]
        results, rest = rest[: len(outs)], rest[len(outs) :]
        inner = count + len(far_outs)
        buffers, sems, own = rest[:inner], rest[inner], rest[inner + 1 :]
        used = 0
        incoming = []
        for k, i in enumerate(places):
            source, target, parts = given[i], buffers[k], in_parts[k]
            if i in ranges:
                source = source.at[pl.ds(*ranges[i])]
            copies = []
            for c in range(parts):
                step = source.shape[-1] // parts
                if parts > 1:
                    piece = (slice(None), pl.ds(c * step, step))
                    copy = pltpu.make_async_copy(source.at[piece], target.at[piece], sems.at[used])
                else:
                    copy = pltpu.make_async_copy(source, target, sems.at[used])
                copies.append(copy)
                used += 1
            incoming.append(copies)
            given[i] = Incoming(target, copies)
        for c in range(max(in_parts, default=0)):
            for k in sorted(range(count), key=lambda k: sizes[k] / in_parts[k]):
                if c < in_parts[k]:
                    incoming[k][c].start()
        leaving = [Outgoing(result, []) for result in results]
        for k, i in enumerate(far_outs):
            result, source, parts = results[i], buffers[count + k], out_parts[k]
            copies = []
            for c in range(parts):
                step = result.shape[0] // parts
                cuts = split.get(-1 - i)
                if isinstance(cuts, tuple) or parts > 1:
                    piece = pl.ds(c * step, step)
                    if isinstance(cuts, tuple):
                        piece = (slice(None), pl.ds(*cuts[c]))
                    copy = pltpu.make_async_copy(source.at[piece], result.at[piece], sems.at[used])
                else:
                    copy = pltpu.make_async_copy(source, result, sems.at[used])
                copies.append(copy)
                used += 1
            leaving[i] = Outgoing(source, copies)
        body(*given, *leaving, *own)
        for value in given:
            if isinstance(value, Incoming):
                value.ready()
        for value in leaving:
            value.send()
        for value in leaving:
            for copy in value.copies:
                copy.wait()

    moved = sum(sizes) + sum(math.prod(s) * jnp.dtype(d).itemsize for s, d in outs)
    in_hbm = pl.BlockSpec(memory_space=pltpu.HBM)

    def pinned(value):
        return pltpu.with_memory_space_constraint(value, pltpu.HBM)

    return pl.pallas_call(
        kernel,
        out_shape=[
            jax.ShapeDtypeStruct(s, d) if c else pltpu.HBM(s, d)
            for (s, d), c in zip(outs, close_out)
        ],
        in_specs=[
            pl.BlockSpec(memory_space=pltpu.SMEM)
            if o.ndim == 1
            else (pl.BlockSpec(memory_space=pltpu.VMEM) if c else in_hbm)
            for o, c in zip(operands, close)
        ]
        + [in_hbm] * len(after)
        + [pl.BlockSpec(memory_space=pl.ANY)] * len(loose),
        out_specs=[pl.BlockSpec(memory_space=pltpu.VMEM) if c else in_hbm for c in close_out],
        scratch_shapes=[pltpu.VMEM(o.shape, o.dtype) for o in arrays]
        + [pltpu.VMEM(*outs[i]) for i in far_outs]
        + [pltpu.SemaphoreType.DMA((max(1, sum(in_parts) + sum(out_parts)),))]
        + list(scratch),
        compiler_params=pltpu.CompilerParams(vmem_limit_bytes=megabytes << 20),
        cost_estimate=pl.CostEstimate(flops=flops, bytes_accessed=moved, transcendentals=0),
    )(*[pinned(o) if i in places else o for i, o in enumerate(operands)], *[pinned(o) for o in after], *loose)


def as_column(row):
    count = row.shape[1]
    here = row_index((count, count)) == lane_index((count, count))
    return jnp.sum(jnp.where(here, row.astype(F32), 0.0), axis=-1, keepdims=True)


def lane_index(shape):
    return lax.broadcasted_iota(I32, shape, len(shape) - 1)


def row_index(shape):
    return lax.broadcasted_iota(I32, shape, len(shape) - 2)


def kv_kernel(tok, gain, wk, wv, pos, rates, key_gain, a_out, kv_out, raw_out, cos, sin):
    wide = tok[...].astype(F32)
    low = (wide * norm_stats(wide) * gain[...]).astype(BF16)
    a_out[...] = low
    size = wk.shape[1]
    angles = as_column(pos[...]) * rates[...]
    cos[...] = jnp.cos(angles)
    sine = jnp.sin(angles)
    sin[...] = jnp.where(lane_index(sine.shape) < size // 2, -sine, sine)
    raw = dot(low, wk[...])
    raw_out[...] = raw
    scaled = raw * norm_stats(raw) * key_gain[...]
    key = (scaled * cos[...] + half_turn(scaled) * sin[...]).astype(BF16)
    value = dot(low, wv[...]).astype(BF16)
    kv_out[:, :size] = key
    kv_out[:, size:] = value


def query_kernel(a, wq, cos, sin, query_gain, q_out, raw_out):
    size = cos.shape[1]
    span = a.shape[0] // SEQS
    for h in range(wq.shape[1] // size):
        if h % 2 == 0:
            pair = dot(a[...], wq[:, h * size : (h + 2) * size])
        raw = pair[:, (h % 2) * size : (h % 2 + 1) * size]
        scaled = raw * norm_stats(raw) * query_gain[...]
        rot = (scaled * cos[...] + half_turn(scaled) * sin[...]).astype(BF16)
        for s in range(SEQS):
            q_out[s, h * span : (h + 1) * span] = rot[s * span : (s + 1) * span]
            raw_out[s, h * span : (h + 1) * span] = raw[s * span : (s + 1) * span]


def attend_kernel(count, ids, q, pos, wo, *refs):
    kv, (k_out, v_out, p_out, att_out) = refs[:count], refs[count : count + 4]
    pieces, scr = refs[count + 4 : -1], refs[-1]
    ctx = ids[0]
    span = pos.shape[1] // SEQS
    part = span // 2
    size = q.shape[2]
    rows = q.shape[1]
    length = count * span
    scaling = 1.0 / math.sqrt(size)

    def place_of(owner, inner):
        late = (2 * count - 1 - owner) * part + inner - part
        return jnp.where(inner < part, owner * part + inner, late)

    lane = lane_index((span, length))
    key_place = place_of(lane >> (span.bit_length() - 1), lane & (span - 1))
    query_place = place_of(ctx, row_index((span, length)))
    for s in range(SEQS):
        for j in range(count):
            here = pl.ds(pl.multiple_of((ctx ^ j) * span, span), span)
            k_out[s, here] = kv[j][s * span : (s + 1) * span, :size]
            v_out[s, here] = kv[j][s * span : (s + 1) * span, size:]
        start = query_place - as_column(pos[:, s * span : (s + 1) * span]).astype(I32)
        visible = (key_place <= query_place) & (key_place >= start)
        scores = contract_last(q[s], k_out[s]) * scaling
        scores = scores.reshape(rows // span, span, length)
        scores = jnp.where(visible[None], scores, -1e30)
        weights = jnp.exp(scores - jnp.max(scores, axis=-1, keepdims=True))
        weights = weights / jnp.sum(weights, axis=-1, keepdims=True)
        low = weights.reshape(rows, length).astype(BF16)
        p_out[s] = low
        attended = dot(low, v_out[s]).astype(BF16)
        for h in range(rows // span):
            att_out[s * span : (s + 1) * span, h * size : (h + 1) * size] = attended[
                h * span : (h + 1) * span
            ]
    for out in (k_out, v_out, p_out, att_out):
        out.send()
    split_rows(ids[1], dot(att_out[...], wo[...]), pieces, scr)


def split_rows(wa, full, pieces, scr):
    quarter = pieces[0].shape[0]
    scr[...] = full.astype(BF16)
    for k, piece in enumerate(pieces):
        first = pl.multiple_of((wa ^ k) * quarter, quarter)
        piece[...] = scr[pl.ds(first, quarter)]


def join_rows(wa, pieces, out):
    quarter = pieces[0].shape[0]
    for k, piece in enumerate(pieces):
        out[pl.ds(pl.multiple_of((wa ^ k) * quarter, quarter), quarter)] = piece[...]


def added(pieces):
    total = pieces[0][...].astype(F32)
    for piece in pieces[1:]:
        total = total + piece[...].astype(F32)
    return total


def own_rows(ids, array, quarter):
    return array[pl.ds(pl.multiple_of(ids[1] * quarter, quarter), quarter)].astype(F32)


def hot_routes(columns, width):
    lane = lane_index((columns[0].shape[0], width))
    hot = columns[0] == lane
    for column in columns[1:]:
        hot = hot | (column == lane)
    return hot


def hidden_kernel(ids, tok, routes, post_norm, router, *refs):
    pieces, (send, hidden_out, prob_out) = refs[:-3], refs[-3:]
    quarter, width = pieces[0].shape
    experts = router.shape[0]
    hidden = own_rows(ids, tok, quarter) + added(pieces)
    hidden_out[...] = hidden
    ffn = (hidden * norm_stats(hidden) * post_norm[...]).astype(BF16)
    named = [as_column(routes[j : j + 1]).astype(I32) for j in range(routes.shape[0])]
    hot = hot_routes(named, experts)
    logits = contract_last(ffn, router[...])
    masked = jnp.where(hot, logits, -1e30)
    exps = jnp.where(hot, jnp.exp(logits - jnp.max(masked, axis=-1, keepdims=True)), 0.0)
    probs = exps / jnp.sum(exps, axis=-1, keepdims=True)
    prob_out[...] = probs
    high, low = split_low(probs)
    send[:, :width] = ffn
    if send.shape[1] > width + 2 * experts:
        send[:, width:] = jnp.zeros((quarter, send.shape[1] - width), BF16)
    send[:, width : width + experts] = high
    send[:, width + experts : width + 2 * experts] = low


def pack_kernel(cot, routes, out):
    quarter, width = cot.shape
    out[:, :width] = cot[...]
    lane = lane_index((quarter, 128))
    named = jnp.zeros((quarter, 128), F32)
    for j in range(routes.shape[0]):
        named = jnp.where(lane == j, as_column(routes[j : j + 1]), named)
    out[:, width:] = named.astype(BF16)


def route_kernel(experts, top, planes, ids, columns, *refs):
    pieces, t_out, rows_out = refs[:4], refs[4], refs[5 : 5 + planes]
    scr, rows_scr = refs[5 + planes :]
    quarter = pieces[0].shape[0]
    width = rows_out[0].shape[1]
    total = 4 * quarter
    lanes = -(-experts // 128) * 128
    for k, piece in enumerate(pieces):
        scr[pl.ds(pl.multiple_of((ids[3] ^ k) * quarter, quarter), quarter)] = piece[...]
    named = scr[:, width : width + 128].astype(F32).astype(I32)
    hot = hot_routes([named[:, j : j + 1] for j in range(top)], lanes)
    row, col = row_index((total, total)), lane_index((total, total))
    shift = quarter.bit_length() - 1
    before = (row >= col) & ((row >> shift) == (col >> shift))
    counts = dot(before.astype(F32).astype(BF16), hot.astype(F32).astype(BF16))
    slots = jnp.where(hot, counts - 1.0, -1.0).astype(BF16)
    slot_rows = columns.shape[1]
    spread = row_index((lanes, slot_rows)) == (ids[3] * planes + columns[0:1])
    slot = dot(slots, spread.astype(F32).astype(BF16))
    lead = row_index((total, slot_rows)) >> shift
    chosen = (slot == columns[2:3].astype(F32)) & (lead == columns[1:2])
    chosen = chosen.astype(F32).astype(BF16)
    t_out[...] = chosen
    t_out.send()
    rows_scr[...] = contract_first(chosen, scr[:, :width])
    split_groups(ids[4], rows_scr, rows_out)


def split_groups(mine, scr, pieces):
    group = pieces[0].shape[0]
    for k, piece in enumerate(pieces):
        first = pl.multiple_of((mine ^ k) * group, group)
        piece[...] = scr[pl.ds(first, group)].astype(BF16)
        piece.send()


def join_groups(mine, pieces, scr):
    group = pieces[0].shape[0]
    for k, piece in enumerate(pieces):
        first = pl.multiple_of((mine ^ k) * group, group)
        scr[pl.ds(first, group)] = piece[...].astype(F32)
    return scr[...].astype(BF16)


def pick_kernel(ids, chosen, attended, att_in, *refs):
    pieces, (rows_out, attended_out, scr) = refs[:4], refs[4:]
    quarter = pieces[0].shape[0]
    for k, piece in enumerate(pieces):
        scr[pl.ds(pl.multiple_of((ids[3] ^ k) * quarter, quarter), quarter)] = piece[...]
    rows_out[...] = contract_first(chosen[...], scr[...]).astype(BF16)
    rows_out.send()
    count, wide = attended.shape
    attended_out[:count] = attended[...]
    mine = att_in[pl.ds(pl.multiple_of(ids[1] * quarter, quarter), quarter)]
    for j in range(mine.shape[1] // wide):
        row = count + j * quarter
        attended_out[row : row + quarter] = mine[:, j * wide : (j + 1) * wide]


def cot_rows_kernel(planes, ids, wd, *refs):
    pieces, (rows_out, grad_out, scr) = refs[:planes], refs[planes:]
    rows = join_groups(ids[4], pieces, scr)
    rows_out[...] = rows
    rows_out.send()
    grad_out[...] = contract_last(rows, wd[...])


def expert_kernel(experts, ids, wg, wu, grad_raw, rows_in, act_out, dg_out, du_out, prob_out, back):
    width = wg.shape[0]
    extra = rows_in.shape[1] - width
    total = rows_in.shape[0]
    rows = rows_in[:, :width]
    lane = lane_index((total, extra))
    mine_high, mine_low = lane == ids[2], lane == ids[2] + experts
    prob = jnp.sum(
        jnp.where(mine_high | mine_low, rows_in[:, width:].astype(F32), 0.0),
        axis=-1,
        keepdims=True,
    )
    prob_out[...] = jnp.broadcast_to(prob, prob_out.shape)
    gate_grad = jnp.zeros((total, 1), F32)
    step = wg.shape[1] // 3
    for c in range(3):
        here = slice(c * step, (c + 1) * step)
        gate, up = dot(rows, wg.part(c)), dot(rows, wu.part(c))
        sig = jax.nn.sigmoid(gate)
        lifted = gate * sig
        act = (lifted * up).astype(BF16)
        act_out[:, here] = act
        raw = grad_raw[:, here]
        gate_grad = gate_grad + jnp.sum(act.astype(F32) * raw, axis=-1, keepdims=True)
        grad_act = prob * raw
        dg_out[:, here] = (grad_act * up * sig * (1.0 + gate * (1.0 - sig))).astype(BF16)
        du_out[:, here] = (grad_act * lifted).astype(BF16)
    for out in (act_out, dg_out, du_out, prob_out):
        out.send()
    high = gate_grad.astype(BF16).astype(F32)
    tail = jnp.where(mine_high, high, jnp.where(mine_low, gate_grad - high, 0.0))
    back[:, width:] = tail.astype(BF16)
    for c in range(4):
        here = slice(c * width // 4, (c + 1) * width // 4)
        grad_in = contract_last(dg_out[...], wg[here]) + contract_last(du_out[...], wu[here])
        back[:, here] = grad_in.astype(BF16)
        back.send(c)


def expert_weights_kernel(rows, dg, du, act, cot_rows, prob, gate_out, up_out, down_out):
    width, units = gate_out.shape
    step = width // 4
    for c in range(4):
        here = slice(c * step, (c + 1) * step)
        left = rows[:, here]
        gate_out[here] = contract_first(left, dg[...])
        gate_out.send(c)
        up_out[here] = contract_first(left, du[...])
        up_out.send(c)
    grad_rows = (cot_rows[...].astype(F32) * prob[:, 0:1]).astype(BF16)
    step = units // 3
    for c in range(3):
        here = slice(c * step, (c + 1) * step)
        down_out[here] = contract_first(act[:, here], grad_rows)
        down_out.send(c)


def out_rows_kernel(act, wd, prob, rows_out):
    rows = dot(act[...], wd[...]).astype(BF16).astype(F32) * prob[:, 0:1]
    rows_out[...] = rows.astype(BF16)


def combine_kernel(ids, chosen, rows, *refs):
    pieces, scr = refs[:-1], refs[-1]
    quarter = pieces[0].shape[0]
    scr[...] = dot(chosen[...], rows[...])
    for k, out in enumerate(pieces):
        first = pl.multiple_of((ids[3] ^ k) * quarter, quarter)
        out[...] = scr[pl.ds(first, quarter)].astype(out.dtype)


def grad_hidden_kernel(ids, hidden_ref, prob_ref, router, cot, post_norm, *refs):
    pieces, low_out, lates, scr = refs[:4], refs[4], refs[5:9], refs[9]
    width = hidden_ref.shape[1]
    experts = router.shape[0]
    total = added(pieces)
    gate_grad = total[:, width : width + experts] + total[:, width + experts : width + 2 * experts]
    prob = prob_ref[...]
    grad_logits = prob * (gate_grad - jnp.sum(prob * gate_grad, axis=-1, keepdims=True))
    high, low = split_low(grad_logits)
    grad_ffn = total[:, :width] + (dot(high, router[...]) + dot(low, router[...]))
    hidden = hidden_ref[...]
    inverse = norm_stats(hidden)
    normed = hidden * inverse
    ffn = (normed * post_norm[...]).astype(BF16)
    grad = cot[...].astype(F32) + norm_backward(grad_ffn, normed, inverse, post_norm[...])
    grad = grad.astype(BF16)
    low_out[...] = grad
    router_part = (contract_first(high, ffn) + contract_first(low, ffn)).astype(BF16)
    post = jnp.sum(grad_ffn * normed, axis=0, keepdims=True)
    post = jnp.where(row_index((16, width)) == 0, post, 0.0).astype(BF16)
    quarter = hidden.shape[0]
    scr[:quarter] = grad
    scr[quarter : quarter + experts] = router_part
    scr[quarter + experts :] = post
    wide = lates[0].shape[1]
    for k, out in enumerate(lates):
        out[...] = scr[:, pl.ds(pl.multiple_of((ids[3] ^ k) * wide, wide), wide)]


def block_at(low, k, blocks):
    value = blocks[0].astype(F32)
    for b in range(1, len(blocks)):
        value = jnp.where((low ^ k) == b, blocks[b].astype(F32), value)
    return value.astype(blocks[0].dtype)


def attend_back_kernel(
    count, ids, q, keys, values, p, raw_ref, wo, cos, sin, gain, *refs
):
    pieces, (gq_out, gain_out, kv_out, branch_out, dq_scr) = refs[:4], refs[4:]
    join_rows(ids[1], pieces, branch_out)
    branch_out.send()
    size, rows = q.shape[2], q.shape[1]
    span = branch_out.shape[0] // SEQS
    heads = rows // span
    scaling = 1.0 / math.sqrt(size)
    step = branch_out.shape[1] // 4
    grad_att = contract_last(branch_out[:, :step], wo.part(0))
    for c in range(1, 4):
        grad_att = grad_att + contract_last(branch_out[:, c * step : (c + 1) * step], wo.part(c))
    grad_att = grad_att.astype(BF16)
    gain_sum = jnp.zeros((1, size), F32)
    for s in range(SEQS):
        rows_s = grad_att[s * span : (s + 1) * span]
        for h in range(heads):
            dq_scr[h * span : (h + 1) * span] = rows_s[:, h * size : (h + 1) * size]
        grad_o = dq_scr[...]
        low = p[s]
        grad_p = contract_last(grad_o, values[s])
        weights = low.astype(F32)
        delta = jnp.sum(weights * grad_p, axis=-1, keepdims=True)
        grad_s = (weights * (grad_p - delta)).astype(BF16)
        grad_v = contract_first(low, grad_o).astype(BF16)
        grad_k = (contract_first(grad_s, q[s]) * scaling).astype(BF16)
        for j in range(count):
            kv_out[j, s * span : (s + 1) * span, :size] = grad_k[j * span : (j + 1) * span]
            kv_out[j, s * span : (s + 1) * span, size:] = grad_v[j * span : (j + 1) * span]
        grad_q = dot(grad_s, keys[s]) * scaling
        cosine, sine = cos[s * span : (s + 1) * span], sin[s * span : (s + 1) * span]
        for h in range(heads):
            grad_rot = grad_q[h * span : (h + 1) * span]
            grad_normed = grad_rot * cosine - half_turn(grad_rot) * sine
            raw = raw_ref[s, h * span : (h + 1) * span]
            inverse = norm_stats(raw)
            normed = raw * inverse
            gain_sum = gain_sum + jnp.sum(grad_normed * normed, axis=0, keepdims=True)
            gq_out[s * span : (s + 1) * span, h * size : (h + 1) * size] = norm_backward(
                grad_normed, normed, inverse, gain[...]
            ).astype(BF16)
    gain_out[...] = gain_sum


def query_in_kernel(gq, wq, out):
    out[...] = contract_last(gq[...], wq[...])


def columns_kernel(lows, rows, ids, early, *refs):
    pieces, (col_out, late) = refs[:4], refs[4:]
    wide = col_out.shape[1] // 2
    part = wide // lows
    for k, piece in enumerate(pieces):
        late[ids[3] ^ k] = piece[...]
    quarter = rows
    experts = late.shape[1] - 16 - quarter
    per_row = early.shape[2] // wide
    row = early.shape[1] - 4 // per_row * quarter + ids[3] // per_row * quarter
    here = pl.ds(pl.multiple_of(row, quarter), quarter)
    lane = pl.ds(pl.multiple_of(ids[3] % per_row * wide, wide), wide)

    def place(target_rows, first, values):
        blocks = [values[:, b * part : (b + 1) * part] for b in range(lows)]
        for k in range(lows):
            col_out[target_rows, first + k * part : first + (k + 1) * part] = block_at(
                ids[5], k, blocks
            ).astype(BF16)

    total = jnp.zeros((late.shape[1] - quarter, wide), F32)
    for j in range(4):
        target = slice(j * quarter, (j + 1) * quarter)
        place(target, 0, early[j, here, lane])
        place(target, wide, late[j, :quarter])
        total = total + late[j, quarter:].astype(F32)
    target = slice(4 * quarter, 4 * quarter + experts)
    place(target, 0, total[:experts])
    post = jnp.where(row_index((experts, wide)) == 0, total[experts : experts + 1], 0.0)
    place(target, wide, post)


def grad_in_kernel(ids, from_q, raw_ref, cos, sin, gain, wk, wv, parts, kv_out, gain_out, own_out, send_out, scr):
    size = wk.shape[1]
    total = added([parts[k] for k in range(parts.shape[0])])
    grad_v = total[:, size:].astype(BF16)
    grad_rot = total[:, :size]
    grad_normed = grad_rot * cos[...] - half_turn(grad_rot) * sin[...]
    raw = raw_ref[...]
    inverse = norm_stats(raw)
    normed = raw * inverse
    gain_out[...] = jnp.sum(grad_normed * normed, axis=0, keepdims=True)
    grad_k = norm_backward(grad_normed, normed, inverse, gain[...]).astype(BF16)
    kv_out[:, :size] = grad_k
    kv_out[:, size:] = grad_v
    full = from_q[...] + contract_last(grad_k, wk[...]) + contract_last(grad_v, wv[...])
    scr[...] = full.astype(BF16)
    half = own_out.shape[0]
    for out, core in ((send_out, 1 - ids[1] % 2), (own_out, ids[1] % 2)):
        out[...] = scr[pl.ds(pl.multiple_of(core * half, half), half)]


def half_kernel(own, other, *refs):
    pieces, (out, sums_out, *sends) = refs[:4], refs[4:]
    out[...] = added((own, other)).astype(BF16)
    total = added(pieces)
    experts, part = total.shape[0], sums_out.shape[1]
    wide = total.shape[1] // 2
    for k, target in enumerate((sums_out, *sends)):
        target[:experts] = total[:, k * part : (k + 1) * part].astype(target.dtype)
        target[experts:] = total[:, wide + k * part : wide + (k + 1) * part].astype(target.dtype)


def token_rows_kernel(ids, tok, gain, branch, own, other, rows_out, gain_out):
    half = own.shape[0]
    mine = pl.ds(pl.multiple_of(ids[1] % 2 * half, half), half)
    grad_in = added((own, other))
    wide = tok[mine].astype(F32)
    inverse = norm_stats(wide)
    normed = wide * inverse
    rows_out[...] = (
        branch[mine].astype(F32) + norm_backward(grad_in, normed, inverse, gain[...])
    ).astype(BF16)
    gain_out[...] = 0.5 * jnp.sum(grad_in * normed, axis=0, keepdims=True)


def sums_kernel(parts, router_out, post_out, q_out, k_out, gain_out):
    devices = parts.shape[0]
    experts, step = router_out.shape[0], router_out.shape[1] // devices
    base = experts // 2
    total = parts[0].astype(F32)[base:]
    for d in range(1, devices):
        total = total + parts[d].astype(F32)[base:]
    q_out[...] = total[1:2]
    k_out[...] = total[2:3]
    part = gain_out.shape[1]
    for j in range(-(-part // 128)):
        lanes = min(128, part)
        gain_out[:, j * 128 : j * 128 + lanes] = total[3 + j : 4 + j, :lanes]
    group = 128 // step
    for g in range(devices // group):
        held = range(g * group, (g + 1) * group)
        here = slice(g * 128, (g + 1) * 128)
        wide = [parts[d].astype(F32) for d in held]
        router_out[:base, here] = jnp.concatenate([w[:base, :step] for w in wide], axis=1)
        router_out[base:, here] = jnp.concatenate(
            [w[:base, 64 : 64 + step] for w in wide], axis=1
        )
        post_out[:, here] = jnp.concatenate([w[base : base + 1, :step] for w in wide], axis=1)


def join_kernel(ids, own, other, gain_part, q_gain, k_gain, *refs):
    sums, (out, parts_low, parts_out) = refs[:-3], refs[-3:]
    total = added(sums)
    wa_count = lax.axis_size("wa")
    experts, part = total.shape[0] // 2, total.shape[1]
    step = part // wa_count
    mine = total[:, :step]
    for w in range(1, wa_count):
        mine = jnp.where(ids[1] == w, total[:, w * step : (w + 1) * step], mine)
    router_part, post = mine[:experts], mine[experts : experts + 1]
    base = experts // 2
    parts_out[...] = jnp.zeros(parts_out.shape, F32)
    for d in range(parts_out.shape[0]):
        parts_out[d, :base, :step] = router_part[:base]
        parts_out[d, :base, 64 : 64 + step] = router_part[base:]
        parts_out[d, base : base + 1, :step] = post
        parts_out[d, base + 1 : base + 2] = q_gain[...]
        parts_out[d, base + 2 : base + 3] = k_gain[...]
        first = d // wa_count * part
        for j in range(-(-part // 128)):
            lanes = min(128, part)
            parts_out[d, base + 3 + j : base + 4 + j, :lanes] = gain_part[
                :, first + j * 128 : first + j * 128 + lanes
            ]
    parts_low[...] = parts_out[...].astype(BF16)
    parts_low.send()
    half = own.shape[0]
    for source, core in ((own, ids[1] % 2), (other, 1 - ids[1] % 2)):
        out[pl.ds(pl.multiple_of(core * half, half), half)] = source[...]


def token_order(wa, pieces, count, first, scr):
    part = scr.shape[1]
    wa_count = len(pieces)
    quarter = scr.shape[0] // (wa_count * count)
    for k, piece in enumerate(pieces):
        for c in range(count):
            row = pl.multiple_of((c * wa_count + (wa ^ k)) * quarter, quarter)
            scr[pl.ds(row, quarter)] = piece[c * quarter : (c + 1) * quarter, first : first + part]
    return scr[...]


def out_weight_kernel(ids, attended, *refs):
    pieces, (out, *sends) = refs[:4], refs[4:-2]
    scr, att_scr = refs[-2:]
    part, wide, rows = out.shape[1], scr.shape[1], scr.shape[0] // 4
    columns = token_order(ids[1], pieces, 4, wide, scr)
    for j in range(4):
        att_scr[j * rows : (j + 1) * rows] = attended[j, :rows]
    partial = contract_first(att_scr[...], columns)
    for k, target in enumerate((out, *sends)):
        target[...] = partial[:, k * part : (k + 1) * part].astype(target.dtype)


def in_weight_kernel(ids, queries, *refs):
    pieces, (own, *sends) = refs[:4], refs[4:-1]
    left, part = refs[-1], own.shape[0]
    partial = contract_first(token_order(ids[1], pieces, 4, 0, left), queries[...])
    for k, send in enumerate(sends, start=1):
        send[...] = partial[k * part : (k + 1) * part].astype(BF16)
        send.send()
    own[...] = partial[:part]


def kv_weight_kernel(ids, *refs):
    kvs, refs, rows = refs[:4], refs[4:-1], refs[-1]
    count = kvs[0].shape[0]
    for k, piece in enumerate(kvs):
        rows[pl.ds(pl.multiple_of((ids[3] ^ k) * count, count), count)] = piece[...]
    in_weight_kernel(ids, rows, *refs)


def last_kernel(lows, parts, hidden, out_own, wo_own, wq_own, kv_own, *refs):
    outs, refs = refs[:3], refs[3:]
    wos, wqs, kvs = [refs[j * (lows - 1) : (j + 1) * (lows - 1)] for j in range(3)]
    refs = refs[3 * (lows - 1) :]
    output, wo_out, wq_out, wk_out, wv_out = refs[:5]
    wo_out[...] = added((wo_own, *wos))
    wo_out.send()
    wq_out[...] = added((wq_own, *wqs))
    wq_out.send()
    total = added((kv_own, *kvs))
    size = wk_out.shape[1]
    wk_out[...] = total[:, :size]
    wv_out[...] = total[:, size:]
    output[...] = (hidden[...] + added((out_own, *outs))).astype(BF16)
    sums_kernel(parts, *refs[5:])


def bind(body, *sizes):
    return lambda *refs: body(*sizes, *refs)


def on_device(
    tokens,
    positions,
    routes,
    query_weight,
    key_matrix,
    value_matrix,
    out_weight,
    query_gain,
    key_gain,
    input_norm,
    post_norm,
    router,
    gate_weight,
    up_weight,
    down_weight,
    cotangent,
):
    lead_count, low_count = lax.axis_size("lead"), lax.axis_size("low")
    ctx_count = lead_count * low_count
    wa_count = lax.axis_size("wa")
    lead_id = lax.axis_index("lead")
    wa_id = lax.axis_index("wa")
    ctx_id = lead_id * low_count + lax.axis_index("low")
    plane_id = lax.axis_index("low") * wa_count + wa_id
    low_id = lax.axis_index("low")
    ids = jnp.stack([ctx_id, wa_id, ctx_id * wa_count + wa_id, lead_id, plane_id, low_id]).astype(I32)
    row_count, width = tokens.shape
    span = row_count // SEQS
    quarter = row_count // wa_count
    size = query_gain.shape[0]
    local_width = query_weight.shape[1]
    heads = local_width // size
    length = span * ctx_count
    experts = router.shape[1]
    top = routes.shape[1]
    hidden_units = gate_weight.shape[2]
    devices = ctx_count * wa_count
    planes = low_count * wa_count
    part = width // ctx_count
    capacity = max(2, (5 * quarter * top + 4 * experts - 1) // (4 * experts))
    group = -(-4 * capacity // 16) * 16 if planes > 8 else 4 * capacity
    slot_rows = planes * group
    extra = -(-2 * experts // 128) * 128
    everywhere, plane, blocks = ("lead", "low", "wa"), ("low", "wa"), ("lead", "low")
    gate_weight, up_weight, down_weight = gate_weight[0], up_weight[0], down_weight[0]
    input_norm, post_norm = input_norm[None], post_norm[None]
    query_gain, key_gain = query_gain[None], key_gain[None]

    halves = np.arange(size) % (size // 2)
    rates = np.exp(halves * (-2.0 * math.log(1000000.0) / size)).astype(np.float32)
    attention_input, kv_own, keys_raw, cosine, sine = vcall(
        kv_kernel,
        [
            ((row_count, width), BF16),
            ((row_count, 2 * size), BF16, "near"),
            ((row_count, size), F32),
            ((row_count, size), F32),
            ((row_count, size), F32),
        ],
        tokens, input_norm, key_matrix, value_matrix, positions[None], jnp.asarray(rates)[None],
        key_gain,
        flops=4 * row_count * width * size,
    )
    kv_all = exchange([kv_own] * ctx_count, blocks)

    q_heads, queries_raw = vcall(
        query_kernel,
        [
            ((SEQS, heads * span, size), BF16),
            ((SEQS, heads * span, size), F32),
        ],
        attention_input, query_weight, cosine, sine, query_gain,
        flops=2 * row_count * width * local_width,
    )

    (cot_send,) = vcall(
        pack_kernel,
        [((quarter, width + 128), BF16, "near")],
        cotangent, routes.T,
        after=[q_heads],
    )
    cot_pieces = exchange([cot_send] * 4, "lead")

    keys_seq, values_seq, weights_low, attended_low, *branch = vcall(
        bind(attend_kernel, ctx_count),
        [
            ((SEQS, length, size), BF16),
            ((SEQS, length, size), BF16),
            ((SEQS, heads * span, length), BF16),
            ((row_count, local_width), BF16),
        ]
        + [((quarter, width), BF16, "near")] * wa_count,
        ids, q_heads, positions[None], out_weight, *near(kv_all),
        scratch=[pltpu.VMEM((row_count, width), BF16)],
        flops=2 * row_count * width * local_width + 4 * row_count * local_width * length,
        megabytes=48,
    )
    branch = exchange(branch, "wa")

    inner = np.arange(slot_rows) % group
    columns = np.zeros((8, slot_rows), np.int32)
    columns[0] = np.arange(slot_rows) // group
    columns[1] = np.minimum(inner // capacity, 3)
    columns[2] = np.where(inner < 4 * capacity, inner % capacity, -5)
    chosen, *cot_groups = vcall(
        bind(route_kernel, experts, top, planes),
        [((row_count, slot_rows), BF16)] + [((group, width), BF16)] * planes,
        ids, jnp.asarray(columns), *near(cot_pieces),
        after=[branch[0]],
        scratch=[
            pltpu.VMEM((4 * quarter, width + 128), BF16),
            pltpu.VMEM((slot_rows, width), F32),
        ],
        flops=2 * slot_rows * row_count * width,
    )
    send, hidden, probs = vcall(
        hidden_kernel,
        [
            ((quarter, width + extra), BF16, "near"),
            ((quarter, width), F32),
            ((quarter, experts), F32),
        ],
        ids, tokens, routes.T, post_norm, router.T, *near(branch),
        after=[chosen],
        flops=2 * quarter * width * experts,
    )

    cot_groups = exchange(cot_groups, plane)
    cot_rows, grad_raw = vcall(
        bind(cot_rows_kernel, planes),
        [((slot_rows, width), BF16), ((slot_rows, hidden_units), F32)],
        ids, down_weight, *cot_groups,
        scratch=[pltpu.VMEM((slot_rows, width), F32)],
        flops=2 * slot_rows * hidden_units * width,
    )

    rows_in, early_rows = vcall(
        pick_kernel,
        [
            ((slot_rows, width + extra), BF16),
            ((row_count + width // local_width * quarter, local_width), BF16),
        ],
        ids, chosen, attended_low, attention_input, *near(exchange([send] * 4, "lead")),
        after=cot_groups[1:],
        scratch=[pltpu.VMEM((row_count, width + extra), BF16)],
        flops=2 * slot_rows * row_count * width,
    )
    rows_in = swap(rows_in, plane)
    early_all = gather(early_rows, "lead").reshape(4, -1, local_width)
    activation, grad_gate_part, grad_up_part, row_prob, back = vcall(
        bind(expert_kernel, experts),
        [
            ((slot_rows, hidden_units), BF16),
            ((slot_rows, hidden_units), BF16),
            ((slot_rows, hidden_units), BF16),
            ((slot_rows, 128), F32),
            ((slot_rows, width + extra), BF16),
        ],
        ids, gate_weight, up_weight, grad_raw, Near(rows_in),
        split={1: 3, 2: 3, -5: tuple((c * width // 4, width // 4 + (extra if c == 3 else 0)) for c in range(4))},
        flops=8 * slot_rows * hidden_units * width,
        megabytes=48,
    )

    grad_gate_weight, grad_up_weight, grad_down_weight = vcall(
        expert_weights_kernel,
        [
            ((width, hidden_units), F32),
            ((width, hidden_units), F32),
            ((hidden_units, width), F32),
        ],
        rows_in, grad_gate_part, grad_up_part, activation, cot_rows, row_prob,
        split={-1: 4, -2: 4, -3: 3},
        flops=6 * slot_rows * hidden_units * width,
        megabytes=40,
    )

    def to_tokens(rows, after, place):
        return vcall(
            combine_kernel,
            [((quarter, rows.shape[1]), F32, *place)]
            + [((quarter, rows.shape[1]), BF16, "near")] * 3,
            ids, chosen, Near(rows),
            after=after,
            scratch=[pltpu.VMEM((row_count, rows.shape[1]), F32)],
            flops=2 * slot_rows * row_count * width,
        )

    back = swap(back, plane)
    back_pieces = exchange(to_tokens(back, [grad_gate_weight, early_all], ["near"]), "lead")
    (out_rows,) = vcall(
        out_rows_kernel,
        [((slot_rows, width), BF16)],
        activation, down_weight, row_prob,
        after=back_pieces[1:],
        flops=2 * slot_rows * hidden_units * width,
    )
    out_made = out_rows
    out_rows = swap(out_rows, plane)
    grad_low, *late_rows = vcall(
        grad_hidden_kernel,
        [
            ((quarter, width), BF16, "near"),
        ]
        + [((quarter + experts + 16, width // 4), BF16, "near")] * 4,
        ids, hidden, probs, router.T, cotangent, post_norm, *near(back_pieces),
        scratch=[pltpu.VMEM((quarter + experts + 16, width), BF16)],
        flops=4 * quarter * width * experts,
    )

    grad_pieces = exchange([grad_low] * wa_count, "wa")
    late_all = exchange(late_rows, "lead")
    grad_queries, query_gain_part, kv_parts, grad_branch = vcall(
        bind(attend_back_kernel, ctx_count),
        [
            ((row_count, local_width), BF16),
            ((1, size), F32),
            ((ctx_count, row_count, 2 * size), BF16),
            ((row_count, width), BF16),
        ],
        ids, q_heads, keys_seq, values_seq, weights_low, queries_raw, out_weight,
        cosine, sine, query_gain, *near(grad_pieces),
        split={6: 4},
        after=[out_made],
        loose=late_all[1:],
        scratch=[pltpu.VMEM((heads * span, size), BF16)],
        flops=2 * row_count * width * local_width + 8 * row_count * local_width * length,
        megabytes=48,
    )
    kv_parts = swap(kv_parts, blocks)
    queries_all = gather(grad_queries, "lead")
    (from_queries,) = vcall(
        query_in_kernel,
        [((row_count, width), F32)],
        grad_queries, query_weight,
        flops=2 * row_count * width * local_width,
    )
    (weight_columns,) = vcall(
        bind(columns_kernel, low_count, quarter),
        [((4 * quarter + experts, 2 * low_count * part), BF16)],
        ids, early_all, *near(late_all),
        after=[from_queries],
        scratch=[pltpu.VMEM((4, quarter + experts + 16, width // 4), BF16)],
    )
    grad_kv, key_gain_part, grad_in_own, grad_in_send = vcall(
        grad_in_kernel,
        [
            ((row_count, 2 * size), BF16, "near"),
            ((1, size), F32),
            ((row_count // 2, width), BF16, "near"),
            ((row_count // 2, width), BF16, "near"),
        ],
        ids, from_queries, keys_raw, cosine, sine, key_gain, key_matrix, value_matrix, Near(kv_parts),
        scratch=[pltpu.VMEM((row_count, width), BF16)],
        flops=4 * row_count * width * size,
    )
    column_pieces = gather_wa_pieces(weight_columns)
    grad_in_half, sums_own, *sends = vcall(
        half_kernel,
        [((row_count // 2, width), BF16, "near"), ((2 * experts, part), F32)]
        + [((2 * experts, part), BF16, "near")] * (low_count - 1),
        Near(grad_in_own), Near(xor_permute(grad_in_send, "wa", 1)),
        *[Rows(piece, 4 * quarter, experts) for piece in column_pieces],
    )
    out_sums = to_tokens(out_rows, [grad_in_half], [])
    out_pieces = exchange(out_sums, "lead")
    sums = [sums_own] + [xor_permute(sends[k - 1], "low", k) for k in range(1, low_count)]
    grad_kv_all = exchange([grad_kv] * 4, "lead")
    out_weight_own, *sends = vcall(
        out_weight_kernel,
        [((local_width, part), F32)] + [((local_width, part), BF16)] * (low_count - 1),
        ids, early_all, *column_pieces,
        after=[grad_in_half],
        scratch=[
            pltpu.VMEM((4 * row_count, low_count * part), BF16),
            pltpu.VMEM((4 * row_count, local_width), BF16),
        ],
        flops=8 * row_count * low_count * local_width * part,
    )
    others = [xor_permute(sends[k - 1], "low", k) for k in range(1, low_count)]
    weight_own, *sends = vcall(
        in_weight_kernel,
        [((part, local_width), F32)] + [((part, local_width), BF16)] * (low_count - 1),
        ids, queries_all, *column_pieces,
        after=[grad_in_half],
        scratch=[pltpu.VMEM((4 * row_count, low_count * part), BF16)],
        flops=8 * row_count * low_count * local_width * part,
    )
    weight_others = [xor_permute(sends[k - 1], "low", k) for k in range(1, low_count)]
    token_rows, grad_input_part = vcall(
        token_rows_kernel,
        [((row_count // 2, width), BF16, "near"), ((1, width), F32)],
        ids, tokens, input_norm, grad_branch,
        Near(grad_in_half), Near(xor_permute(grad_in_half, "wa", 2)),
        after=[out_weight_own, weight_own],
        loose=grad_kv_all[1:],
    )
    sum_rows = -(-(experts // 2 + 3 + -(-part // 128)) // 16) * 16
    grad_tokens, small_parts = vcall(
        join_kernel,
        [
            ((row_count, width), BF16),
            ((devices, sum_rows, 128), BF16),
        ],
        ids, Near(token_rows), Near(xor_permute(token_rows, "wa", 1)),
        grad_input_part, query_gain_part, key_gain_part,
        *sums,
        after=[out_sums[0]],
        loose=others,
        scratch=[pltpu.VMEM((devices, sum_rows, 128), F32)],
    )

    kv_weight_own, *sends = vcall(
        kv_weight_kernel,
        [((part, 2 * size), F32)] + [((part, 2 * size), BF16)] * (low_count - 1),
        ids, *near(grad_kv_all), *column_pieces,
        after=[small_parts],
        scratch=[
            pltpu.VMEM((4 * row_count, low_count * part), BF16),
            pltpu.VMEM((4 * row_count, 2 * size), BF16),
        ],
        flops=8 * row_count * low_count * 2 * size * part,
    )
    kv_others = [xor_permute(sends[k - 1], "low", k) for k in range(1, low_count)]
    (
        output, grad_out_weight, grad_query_weight, grad_key_weight, grad_value_weight,
        grad_router, grad_post_norm, grad_query_gain, grad_key_gain, grad_input_norm,
    ) = vcall(
        bind(last_kernel, low_count),
        [
            ((quarter, width), BF16),
            ((local_width, part), F32),
            ((part, local_width), F32),
            ((part, size), F32),
            ((part, size), F32),
            ((experts, width), F32),
            ((1, width), F32),
            ((1, size), F32),
            ((1, size), F32),
            ((1, part), F32),
        ],
        Near(swap(small_parts, everywhere)), hidden, out_sums[0], out_weight_own, weight_own,
        kv_weight_own, *out_pieces[1:], *near(others + weight_others + kv_others),
    )
    return (
        output,
        grad_tokens,
        grad_query_weight,
        grad_key_weight,
        grad_value_weight,
        grad_out_weight,
        grad_query_gain[0],
        grad_key_gain[0],
        grad_input_norm[0],
        grad_post_norm[0],
        grad_router.T,
        grad_gate_weight[None],
        grad_up_weight[None],
        grad_down_weight[None],
    )


def solution(mesh):
    ctx_count, wa_count = mesh.devices.shape
    finer = Mesh(mesh.devices.reshape(4, ctx_count // 4, wa_count), ("lead", "low", "wa"))
    return jax.shard_map(
        on_device,
        mesh=finer,
        in_specs=(
            P(("lead", "low"), None),
            P(("lead", "low")),
            P(("lead", "low", "wa"), None),
            P(None, "wa"),
            P(None, "wa"),
            P(None, "wa"),
            P("wa", None),
            P(),
            P(),
            P(),
            P(),
            P(),
            P(("lead", "low", "wa"), None, None),
            P(("lead", "low", "wa"), None, None),
            P(("lead", "low", "wa"), None, None),
            P(("lead", "low", "wa"), None),
        ),
        out_specs=(
            P(("lead", "low", "wa"), None),
            P(("lead", "low"), None),
            P(("lead", "low"), "wa"),
            P(("lead", "low"), "wa"),
            P(("lead", "low"), "wa"),
            P("wa", ("lead", "low")),
            P(),
            P(),
            P(("lead", "low")),
            P(),
            P(),
            P(("lead", "low", "wa"), None, None),
            P(("lead", "low", "wa"), None, None),
            P(("lead", "low", "wa"), None, None),
        ),
        check_vma=False,
    )
```

```python
import math

import jax
import jax.numpy as jnp
import numpy as np
from jax import lax
from jax.experimental import pallas as pl
from jax.experimental.pallas import tpu as pltpu
from jax.sharding import Mesh
from jax.sharding import PartitionSpec as P

SEQS = 2


EPSILON = 1e-06
BF16, F32, I32 = jnp.bfloat16, jnp.float32, jnp.int32


def dot(left, right):
    return jnp.dot(left, right, preferred_element_type=F32)


def contract_last(left, right):
    return lax.dot_general(
        left, right, (((1,), (1,)), ((), ())), preferred_element_type=F32
    )


def contract_first(left, right):
    return lax.dot_general(
        left, right, (((0,), (0,)), ((), ())), preferred_element_type=F32
    )


def split_low(values):
    high = values.astype(BF16)
    return high, (values - high.astype(F32)).astype(BF16)


def norm_stats(values):
    return lax.rsqrt(jnp.mean(values * values, axis=-1, keepdims=True) + EPSILON)


def norm_backward(grad_normed, normed, inverse, gain):
    scaled = grad_normed * gain
    return inverse * (scaled - normed * jnp.mean(scaled * normed, axis=-1, keepdims=True))


def half_turn(values):
    return pltpu.roll(values, values.shape[-1] // 2, values.ndim - 1)


def xor_permute(value, axis, offset):
    names = (axis,) if isinstance(axis, str) else axis
    count = math.prod(lax.axis_size(name) for name in names)
    return lax.ppermute(value, axis, [(i, i ^ offset) for i in range(count)])


def exchange(pieces, axis):
    return [pieces[0]] + [xor_permute(pieces[k], axis, k) for k in range(1, len(pieces))]


def gather_ctx_pieces(value):
    low_count = lax.axis_size("low")
    held = {j * low_count: v for j, v in enumerate(exchange([value] * 4, "lead"))}
    bit = 1
    while bit < low_count:
        held.update({k ^ bit: xor_permute(v, "low", bit) for k, v in list(held.items())})
        bit *= 2
    return [held[k] for k in range(4 * low_count)]


def gather_wa_pieces(value):
    over = xor_permute(value, "wa", 2)
    return [value, xor_permute(value, "wa", 1), over, xor_permute(over, "wa", 1)]


def gather(value, axis):
    return lax.all_gather(value, axis, axis=0, tiled=True)


def swap(value, axes):
    return lax.all_to_all(value, axes, split_axis=0, concat_axis=0, tiled=True)


class Incoming:
    def __init__(self, ref, copies):
        self.ref, self.copies = ref, dict(enumerate(copies))
        self.step = ref.shape[-1] // len(copies)
        self.shape, self.dtype, self.ndim = ref.shape, ref.dtype, ref.ndim

    def ready(self):
        for k in list(self.copies):
            self.copies.pop(k).wait()
        return self.ref

    def part(self, k):
        if k in self.copies:
            self.copies.pop(k).wait()
        return self.ref[:, k * self.step : (k + 1) * self.step]

    def __getitem__(self, index):
        return self.ready()[index]


class Outgoing:
    def __init__(self, ref, copies):
        self.ref, self.copies, self.sent = ref, copies, set()
        self.shape, self.dtype, self.ndim = ref.shape, ref.dtype, ref.ndim

    def send(self, part=None):
        for k, copy in enumerate(self.copies):
            if k not in self.sent and part in (None, k):
                copy.start()
                self.sent.add(k)

    def __getitem__(self, index):
        return self.ref[index]

    def __setitem__(self, index, value):
        self.ref[index] = value


class Near:
    def __init__(self, value):
        self.value = value


class Rows:
    def __init__(self, value, first, count):
        self.value, self.first, self.count = value, first, count


def near(values):
    return [Near(value) for value in values]


def vcall(body, outs, *operands, scratch=(), after=(), split=None, loose=(), flops=0, megabytes=24):
    split = split or {}
    close = [isinstance(o, Near) for o in operands]
    ranges = {i: (o.first, o.count) for i, o in enumerate(operands) if isinstance(o, Rows)}
    operands = [o.value if isinstance(o, (Near, Rows)) else o for o in operands]
    close_out = [len(o) > 2 for o in outs]
    outs = [o[:2] for o in outs]
    places = [i for i, o in enumerate(operands) if o.ndim > 1 and not close[i]]
    far_outs = [i for i, c in enumerate(close_out) if not c]
    arrays = [
        jax.ShapeDtypeStruct((ranges[i][1],) + operands[i].shape[1:], operands[i].dtype)
        if i in ranges
        else operands[i]
        for i in places
    ]
    sizes = [o.size * o.dtype.itemsize for o in arrays]
    in_parts = [split.get(i, 1) for i in places]
    out_parts = [split.get(-1 - i, 1) for i in far_outs]
    out_parts = [len(p) if isinstance(p, tuple) else p for p in out_parts]
    count = len(arrays)

    def kernel(*refs):
        given = list(refs[: len(operands)])
        rest = refs[len(operands) + len(after) + len(loose) :]
        results, rest = rest[: len(outs)], rest[len(outs) :]
        inner = count + len(far_outs)
        buffers, sems, own = rest[:inner], rest[inner], rest[inner + 1 :]
        used = 0
        incoming = []
        for k, i in enumerate(places):
            source, target, parts = given[i], buffers[k], in_parts[k]
            if i in ranges:
                source = source.at[pl.ds(*ranges[i])]
            copies = []
            for c in range(parts):
                step = source.shape[-1] // parts
                if parts > 1:
                    piece = (slice(None), pl.ds(c * step, step))
                    copy = pltpu.make_async_copy(source.at[piece], target.at[piece], sems.at[used])
                else:
                    copy = pltpu.make_async_copy(source, target, sems.at[used])
                copies.append(copy)
                used += 1
            incoming.append(copies)
            given[i] = Incoming(target, copies)
        for c in range(max(in_parts, default=0)):
            for k in sorted(range(count), key=lambda k: sizes[k] / in_parts[k]):
                if c < in_parts[k]:
                    incoming[k][c].start()
        leaving = [Outgoing(result, []) for result in results]
        for k, i in enumerate(far_outs):
            result, source, parts = results[i], buffers[count + k], out_parts[k]
            copies = []
            for c in range(parts):
                step = result.shape[0] // parts
                cuts = split.get(-1 - i)
                if isinstance(cuts, tuple) or parts > 1:
                    piece = pl.ds(c * step, step)
                    if isinstance(cuts, tuple):
                        piece = (slice(None), pl.ds(*cuts[c]))
                    copy = pltpu.make_async_copy(source.at[piece], result.at[piece], sems.at[used])
                else:
                    copy = pltpu.make_async_copy(source, result, sems.at[used])
                copies.append(copy)
                used += 1
            leaving[i] = Outgoing(source, copies)
        body(*given, *leaving, *own)
        for value in given:
            if isinstance(value, Incoming):
                value.ready()
        for value in leaving:
            value.send()
        for value in leaving:
            for copy in value.copies:
                copy.wait()

    moved = sum(sizes) + sum(math.prod(s) * jnp.dtype(d).itemsize for s, d in outs)
    in_hbm = pl.BlockSpec(memory_space=pltpu.HBM)

    def pinned(value):
        return pltpu.with_memory_space_constraint(value, pltpu.HBM)

    return pl.pallas_call(
        kernel,
        out_shape=[
            jax.ShapeDtypeStruct(s, d) if c else pltpu.HBM(s, d)
            for (s, d), c in zip(outs, close_out)
        ],
        in_specs=[
            pl.BlockSpec(memory_space=pltpu.SMEM)
            if o.ndim == 1
            else (pl.BlockSpec(memory_space=pltpu.VMEM) if c else in_hbm)
            for o, c in zip(operands, close)
        ]
        + [in_hbm] * len(after)
        + [pl.BlockSpec(memory_space=pl.ANY)] * len(loose),
        out_specs=[pl.BlockSpec(memory_space=pltpu.VMEM) if c else in_hbm for c in close_out],
        scratch_shapes=[pltpu.VMEM(o.shape, o.dtype) for o in arrays]
        + [pltpu.VMEM(*outs[i]) for i in far_outs]
        + [pltpu.SemaphoreType.DMA((max(1, sum(in_parts) + sum(out_parts)),))]
        + list(scratch),
        compiler_params=pltpu.CompilerParams(vmem_limit_bytes=megabytes << 20),
        cost_estimate=pl.CostEstimate(flops=flops, bytes_accessed=moved, transcendentals=0),
    )(*[pinned(o) if i in places else o for i, o in enumerate(operands)], *[pinned(o) for o in after], *loose)


def as_column(row):
    count = row.shape[1]
    here = row_index((count, count)) == lane_index((count, count))
    return jnp.sum(jnp.where(here, row.astype(F32), 0.0), axis=-1, keepdims=True)


def lane_index(shape):
    return lax.broadcasted_iota(I32, shape, len(shape) - 1)


def row_index(shape):
    return lax.broadcasted_iota(I32, shape, len(shape) - 2)


def kv_kernel(tok, gain, wk, wv, pos, rates, key_gain, a_out, kv_out, raw_out, cos, sin):
    wide = tok[...].astype(F32)
    low = (wide * norm_stats(wide) * gain[...]).astype(BF16)
    a_out[...] = low
    size = wk.shape[1]
    angles = as_column(pos[...]) * rates[...]
    cos[...] = jnp.cos(angles)
    sine = jnp.sin(angles)
    sin[...] = jnp.where(lane_index(sine.shape) < size // 2, -sine, sine)
    raw = dot(low, wk[...])
    raw_out[...] = raw
    scaled = raw * norm_stats(raw) * key_gain[...]
    key = (scaled * cos[...] + half_turn(scaled) * sin[...]).astype(BF16)
    value = dot(low, wv[...]).astype(BF16)
    kv_out[:, :size] = key
    kv_out[:, size:] = value


def query_kernel(a, wq, cos, sin, query_gain, q_out, raw_out):
    size = cos.shape[1]
    span = a.shape[0] // SEQS
    for h in range(wq.shape[1] // size):
        if h % 2 == 0:
            pair = dot(a[...], wq[:, h * size : (h + 2) * size])
        raw = pair[:, (h % 2) * size : (h % 2 + 1) * size]
        scaled = raw * norm_stats(raw) * query_gain[...]
        rot = (scaled * cos[...] + half_turn(scaled) * sin[...]).astype(BF16)
        for s in range(SEQS):
            q_out[s, h * span : (h + 1) * span] = rot[s * span : (s + 1) * span]
            raw_out[s, h * span : (h + 1) * span] = raw[s * span : (s + 1) * span]


def attend_kernel(count, ids, q, pos, wo, *refs):
    kv, (k_out, v_out, p_out, att_out) = refs[:count], refs[count : count + 4]
    pieces, scr = refs[count + 4 : -1], refs[-1]
    ctx = ids[0]
    span = pos.shape[1] // SEQS
    part = span // 2
    size = q.shape[2]
    rows = q.shape[1]
    length = count * span
    scaling = 1.0 / math.sqrt(size)

    def place_of(owner, inner):
        late = (2 * count - 1 - owner) * part + inner - part
        return jnp.where(inner < part, owner * part + inner, late)

    lane = lane_index((span, length))
    key_place = place_of(lane >> (span.bit_length() - 1), lane & (span - 1))
    query_place = place_of(ctx, row_index((span, length)))
    for s in range(SEQS):
        for j in range(count):
            here = pl.ds(pl.multiple_of((ctx ^ j) * span, span), span)
            k_out[s, here] = kv[j][s * span : (s + 1) * span, :size]
            v_out[s, here] = kv[j][s * span : (s + 1) * span, size:]
        start = query_place - as_column(pos[:, s * span : (s + 1) * span]).astype(I32)
        visible = (key_place <= query_place) & (key_place >= start)
        scores = contract_last(q[s], k_out[s]) * scaling
        scores = scores.reshape(rows // span, span, length)
        scores = jnp.where(visible[None], scores, -1e30)
        weights = jnp.exp(scores - jnp.max(scores, axis=-1, keepdims=True))
        weights = weights / jnp.sum(weights, axis=-1, keepdims=True)
        low = weights.reshape(rows, length).astype(BF16)
        p_out[s] = low
        attended = dot(low, v_out[s]).astype(BF16)
        for h in range(rows // span):
            att_out[s * span : (s + 1) * span, h * size : (h + 1) * size] = attended[
                h * span : (h + 1) * span
            ]
    for out in (k_out, v_out, p_out, att_out):
        out.send()
    split_rows(ids[1], dot(att_out[...], wo[...]), pieces, scr)


def split_rows(wa, full, pieces, scr):
    quarter = pieces[0].shape[0]
    scr[...] = full.astype(BF16)
    for k, piece in enumerate(pieces):
        first = pl.multiple_of((wa ^ k) * quarter, quarter)
        piece[...] = scr[pl.ds(first, quarter)]


def join_rows(wa, pieces, out):
    quarter = pieces[0].shape[0]
    for k, piece in enumerate(pieces):
        out[pl.ds(pl.multiple_of((wa ^ k) * quarter, quarter), quarter)] = piece[...]


def added(pieces):
    total = pieces[0][...].astype(F32)
    for piece in pieces[1:]:
        total = total + piece[...].astype(F32)
    return total


def own_rows(ids, array, quarter):
    return array[pl.ds(pl.multiple_of(ids[1] * quarter, quarter), quarter)].astype(F32)


def hot_routes(columns, width):
    lane = lane_index((columns[0].shape[0], width))
    hot = columns[0] == lane
    for column in columns[1:]:
        hot = hot | (column == lane)
    return hot


def hidden_kernel(ids, tok, routes, post_norm, router, *refs):
    pieces, (send, hidden_out, prob_out) = refs[:-3], refs[-3:]
    quarter, width = pieces[0].shape
    experts = router.shape[0]
    hidden = own_rows(ids, tok, quarter) + added(pieces)
    hidden_out[...] = hidden
    ffn = (hidden * norm_stats(hidden) * post_norm[...]).astype(BF16)
    named = [as_column(routes[j : j + 1]).astype(I32) for j in range(routes.shape[0])]
    hot = hot_routes(named, experts)
    logits = contract_last(ffn, router[...])
    masked = jnp.where(hot, logits, -1e30)
    exps = jnp.where(hot, jnp.exp(logits - jnp.max(masked, axis=-1, keepdims=True)), 0.0)
    probs = exps / jnp.sum(exps, axis=-1, keepdims=True)
    prob_out[...] = probs
    high, low = split_low(probs)
    send[:, :width] = ffn
    if send.shape[1] > width + 2 * experts:
        send[:, width:] = jnp.zeros((quarter, send.shape[1] - width), BF16)
    send[:, width : width + experts] = high
    send[:, width + experts : width + 2 * experts] = low


def pack_kernel(cot, routes, out):
    quarter, width = cot.shape
    out[:, :width] = cot[...]
    lane = lane_index((quarter, 128))
    named = jnp.zeros((quarter, 128), F32)
    for j in range(routes.shape[0]):
        named = jnp.where(lane == j, as_column(routes[j : j + 1]), named)
    out[:, width:] = named.astype(BF16)


def route_kernel(experts, top, planes, ids, columns, *refs):
    pieces, t_out, rows_out = refs[:4], refs[4], refs[5 : 5 + planes]
    scr, rows_scr = refs[5 + planes :]
    quarter = pieces[0].shape[0]
    width = rows_out[0].shape[1]
    total = 4 * quarter
    lanes = -(-experts // 128) * 128
    for k, piece in enumerate(pieces):
        scr[pl.ds(pl.multiple_of((ids[3] ^ k) * quarter, quarter), quarter)] = piece[...]
    named = scr[:, width : width + 128].astype(F32).astype(I32)
    hot = hot_routes([named[:, j : j + 1] for j in range(top)], lanes)
    row, col = row_index((total, total)), lane_index((total, total))
    shift = quarter.bit_length() - 1
    before = (row >= col) & ((row >> shift) == (col >> shift))
    counts = dot(before.astype(F32).astype(BF16), hot.astype(F32).astype(BF16))
    slots = jnp.where(hot, counts - 1.0, -1.0).astype(BF16)
    slot_rows = columns.shape[1]
    spread = row_index((lanes, slot_rows)) == (ids[3] * planes + columns[0:1])
    slot = dot(slots, spread.astype(F32).astype(BF16))
    lead = row_index((total, slot_rows)) >> shift
    chosen = (slot == columns[2:3].astype(F32)) & (lead == columns[1:2])
    chosen = chosen.astype(F32).astype(BF16)
    t_out[...] = chosen
    t_out.send()
    rows_scr[...] = contract_first(chosen, scr[:, :width])
    split_groups(ids[4], rows_scr, rows_out)


def split_groups(mine, scr, pieces):
    group = pieces[0].shape[0]
    for k, piece in enumerate(pieces):
        first = pl.multiple_of((mine ^ k) * group, group)
        piece[...] = scr[pl.ds(first, group)].astype(BF16)
        piece.send()


def join_groups(mine, pieces, scr):
    group = pieces[0].shape[0]
    for k, piece in enumerate(pieces):
        first = pl.multiple_of((mine ^ k) * group, group)
        scr[pl.ds(first, group)] = piece[...].astype(F32)
    return scr[...].astype(BF16)


def pick_kernel(ids, chosen, attended, att_in, *refs):
    pieces, (rows_out, attended_out, scr) = refs[:4], refs[4:]
    quarter = pieces[0].shape[0]
    for k, piece in enumerate(pieces):
        scr[pl.ds(pl.multiple_of((ids[3] ^ k) * quarter, quarter), quarter)] = piece[...]
    rows_out[...] = contract_first(chosen[...], scr[...]).astype(BF16)
    rows_out.send()
    count, wide = attended.shape
    attended_out[:count] = attended[...]
    mine = att_in[pl.ds(pl.multiple_of(ids[1] * quarter, quarter), quarter)]
    for j in range(mine.shape[1] // wide):
        row = count + j * quarter
        attended_out[row : row + quarter] = mine[:, j * wide : (j + 1) * wide]


def cot_rows_kernel(planes, ids, wd, *refs):
    pieces, (rows_out, grad_out, scr) = refs[:planes], refs[planes:]
    rows = join_groups(ids[4], pieces, scr)
    rows_out[...] = rows
    rows_out.send()
    grad_out[...] = contract_last(rows, wd[...])


def expert_kernel(experts, ids, wg, wu, grad_raw, rows_in, act_out, dg_out, du_out, prob_out, back):
    width = wg.shape[0]
    extra = rows_in.shape[1] - width
    total = rows_in.shape[0]
    rows = rows_in[:, :width]
    lane = lane_index((total, extra))
    mine_high, mine_low = lane == ids[2], lane == ids[2] + experts
    prob = jnp.sum(
        jnp.where(mine_high | mine_low, rows_in[:, width:].astype(F32), 0.0),
        axis=-1,
        keepdims=True,
    )
    prob_out[...] = jnp.broadcast_to(prob, prob_out.shape)
    gate_grad = jnp.zeros((total, 1), F32)
    step = wg.shape[1] // 3
    for c in range(3):
        here = slice(c * step, (c + 1) * step)
        gate, up = dot(rows, wg.part(c)), dot(rows, wu.part(c))
        sig = jax.nn.sigmoid(gate)
        lifted = gate * sig
        act = (lifted * up).astype(BF16)
        act_out[:, here] = act
        raw = grad_raw[:, here]
        gate_grad = gate_grad + jnp.sum(act.astype(F32) * raw, axis=-1, keepdims=True)
        grad_act = prob * raw
        dg_out[:, here] = (grad_act * up * sig * (1.0 + gate * (1.0 - sig))).astype(BF16)
        du_out[:, here] = (grad_act * lifted).astype(BF16)
    for out in (act_out, dg_out, du_out, prob_out):
        out.send()
    high = gate_grad.astype(BF16).astype(F32)
    tail = jnp.where(mine_high, high, jnp.where(mine_low, gate_grad - high, 0.0))
    back[:, width:] = tail.astype(BF16)
    for c in range(4):
        here = slice(c * width // 4, (c + 1) * width // 4)
        grad_in = contract_last(dg_out[...], wg[here]) + contract_last(du_out[...], wu[here])
        back[:, here] = grad_in.astype(BF16)
        back.send(c)


def expert_weights_kernel(rows, dg, du, act, cot_rows, prob, gate_out, up_out, down_out):
    width, units = gate_out.shape
    step = width // 4
    for c in range(4):
        here = slice(c * step, (c + 1) * step)
        left = rows[:, here]
        gate_out[here] = contract_first(left, dg[...])
        gate_out.send(c)
        up_out[here] = contract_first(left, du[...])
        up_out.send(c)
    grad_rows = (cot_rows[...].astype(F32) * prob[:, 0:1]).astype(BF16)
    step = units // 3
    for c in range(3):
        here = slice(c * step, (c + 1) * step)
        down_out[here] = contract_first(act[:, here], grad_rows)
        down_out.send(c)


def out_rows_kernel(act, wd, prob, rows_out):
    rows = dot(act[...], wd[...]).astype(BF16).astype(F32) * prob[:, 0:1]
    rows_out[...] = rows.astype(BF16)


def combine_kernel(ids, chosen, rows, *refs):
    pieces, scr = refs[:-1], refs[-1]
    quarter = pieces[0].shape[0]
    scr[...] = dot(chosen[...], rows[...])
    for k, out in enumerate(pieces):
        first = pl.multiple_of((ids[3] ^ k) * quarter, quarter)
        out[...] = scr[pl.ds(first, quarter)].astype(out.dtype)


def grad_hidden_kernel(ids, hidden_ref, prob_ref, router, cot, post_norm, *refs):
    pieces, low_out, lates, scr = refs[:4], refs[4], refs[5:9], refs[9]
    width = hidden_ref.shape[1]
    experts = router.shape[0]
    total = added(pieces)
    gate_grad = total[:, width : width + experts] + total[:, width + experts : width + 2 * experts]
    prob = prob_ref[...]
    grad_logits = prob * (gate_grad - jnp.sum(prob * gate_grad, axis=-1, keepdims=True))
    high, low = split_low(grad_logits)
    grad_ffn = total[:, :width] + (dot(high, router[...]) + dot(low, router[...]))
    hidden = hidden_ref[...]
    inverse = norm_stats(hidden)
    normed = hidden * inverse
    ffn = (normed * post_norm[...]).astype(BF16)
    grad = cot[...].astype(F32) + norm_backward(grad_ffn, normed, inverse, post_norm[...])
    grad = grad.astype(BF16)
    low_out[...] = grad
    router_part = (contract_first(high, ffn) + contract_first(low, ffn)).astype(BF16)
    post = jnp.sum(grad_ffn * normed, axis=0, keepdims=True)
    post = jnp.where(row_index((16, width)) == 0, post, 0.0).astype(BF16)
    quarter = hidden.shape[0]
    scr[:quarter] = grad
    scr[quarter : quarter + experts] = router_part
    scr[quarter + experts :] = post
    wide = lates[0].shape[1]
    for k, out in enumerate(lates):
        out[...] = scr[:, pl.ds(pl.multiple_of((ids[3] ^ k) * wide, wide), wide)]


def block_at(low, k, blocks):
    value = blocks[0].astype(F32)
    for b in range(1, len(blocks)):
        value = jnp.where((low ^ k) == b, blocks[b].astype(F32), value)
    return value.astype(blocks[0].dtype)


def attend_back_kernel(
    count, ids, q, keys, values, p, raw_ref, wo, cos, sin, gain, *refs
):
    pieces, (gq_out, gain_out, kv_out, branch_out, dq_scr) = refs[:4], refs[4:]
    join_rows(ids[1], pieces, branch_out)
    branch_out.send()
    size, rows = q.shape[2], q.shape[1]
    span = branch_out.shape[0] // SEQS
    heads = rows // span
    scaling = 1.0 / math.sqrt(size)
    step = branch_out.shape[1] // 4
    grad_att = contract_last(branch_out[:, :step], wo.part(0))
    for c in range(1, 4):
        grad_att = grad_att + contract_last(branch_out[:, c * step : (c + 1) * step], wo.part(c))
    grad_att = grad_att.astype(BF16)
    gain_sum = jnp.zeros((1, size), F32)
    for s in range(SEQS):
        rows_s = grad_att[s * span : (s + 1) * span]
        for h in range(heads):
            dq_scr[h * span : (h + 1) * span] = rows_s[:, h * size : (h + 1) * size]
        grad_o = dq_scr[...]
        low = p[s]
        grad_p = contract_last(grad_o, values[s])
        weights = low.astype(F32)
        delta = jnp.sum(weights * grad_p, axis=-1, keepdims=True)
        grad_s = (weights * (grad_p - delta)).astype(BF16)
        grad_v = contract_first(low, grad_o).astype(BF16)
        grad_k = (contract_first(grad_s, q[s]) * scaling).astype(BF16)
        for j in range(count):
            kv_out[j, s * span : (s + 1) * span, :size] = grad_k[j * span : (j + 1) * span]
            kv_out[j, s * span : (s + 1) * span, size:] = grad_v[j * span : (j + 1) * span]
        grad_q = dot(grad_s, keys[s]) * scaling
        cosine, sine = cos[s * span : (s + 1) * span], sin[s * span : (s + 1) * span]
        for h in range(heads):
            grad_rot = grad_q[h * span : (h + 1) * span]
            grad_normed = grad_rot * cosine - half_turn(grad_rot) * sine
            raw = raw_ref[s, h * span : (h + 1) * span]
            inverse = norm_stats(raw)
            normed = raw * inverse
            gain_sum = gain_sum + jnp.sum(grad_normed * normed, axis=0, keepdims=True)
            gq_out[s * span : (s + 1) * span, h * size : (h + 1) * size] = norm_backward(
                grad_normed, normed, inverse, gain[...]
            ).astype(BF16)
    gain_out[...] = gain_sum


def query_in_kernel(gq, wq, out):
    out[...] = contract_last(gq[...], wq[...])


def columns_kernel(lows, rows, ids, early, *refs):
    pieces, (col_out, late) = refs[:4], refs[4:]
    wide = col_out.shape[1] // 2
    part = wide // lows
    for k, piece in enumerate(pieces):
        late[ids[3] ^ k] = piece[...]
    quarter = rows
    experts = late.shape[1] - 16 - quarter
    per_row = early.shape[2] // wide
    row = early.shape[1] - 4 // per_row * quarter + ids[3] // per_row * quarter
    here = pl.ds(pl.multiple_of(row, quarter), quarter)
    lane = pl.ds(pl.multiple_of(ids[3] % per_row * wide, wide), wide)

    def place(target_rows, first, values):
        blocks = [values[:, b * part : (b + 1) * part] for b in range(lows)]
        for k in range(lows):
            col_out[target_rows, first + k * part : first + (k + 1) * part] = block_at(
                ids[5], k, blocks
            ).astype(BF16)

    total = jnp.zeros((late.shape[1] - quarter, wide), F32)
    for j in range(4):
        target = slice(j * quarter, (j + 1) * quarter)
        place(target, 0, early[j, here, lane])
        place(target, wide, late[j, :quarter])
        total = total + late[j, quarter:].astype(F32)
    target = slice(4 * quarter, 4 * quarter + experts)
    place(target, 0, total[:experts])
    post = jnp.where(row_index((experts, wide)) == 0, total[experts : experts + 1], 0.0)
    place(target, wide, post)


def grad_in_kernel(ids, from_q, raw_ref, cos, sin, gain, wk, wv, parts, kv_out, gain_out, own_out, send_out, scr):
    size = wk.shape[1]
    total = added([parts[k] for k in range(parts.shape[0])])
    grad_v = total[:, size:].astype(BF16)
    grad_rot = total[:, :size]
    grad_normed = grad_rot * cos[...] - half_turn(grad_rot) * sin[...]
    raw = raw_ref[...]
    inverse = norm_stats(raw)
    normed = raw * inverse
    gain_out[...] = jnp.sum(grad_normed * normed, axis=0, keepdims=True)
    grad_k = norm_backward(grad_normed, normed, inverse, gain[...]).astype(BF16)
    kv_out[:, :size] = grad_k
    kv_out[:, size:] = grad_v
    full = from_q[...] + contract_last(grad_k, wk[...]) + contract_last(grad_v, wv[...])
    scr[...] = full.astype(BF16)
    half = own_out.shape[0]
    for out, core in ((send_out, 1 - ids[1] % 2), (own_out, ids[1] % 2)):
        out[...] = scr[pl.ds(pl.multiple_of(core * half, half), half)]


def half_kernel(own, other, *refs):
    pieces, (out, sums_out, *sends) = refs[:4], refs[4:]
    out[...] = added((own, other)).astype(BF16)
    total = added(pieces)
    experts, part = total.shape[0], sums_out.shape[1]
    wide = total.shape[1] // 2
    for k, target in enumerate((sums_out, *sends)):
        target[:experts] = total[:, k * part : (k + 1) * part].astype(target.dtype)
        target[experts:] = total[:, wide + k * part : wide + (k + 1) * part].astype(target.dtype)


def token_rows_kernel(ids, tok, gain, branch, own, other, rows_out, gain_out):
    half = own.shape[0]
    mine = pl.ds(pl.multiple_of(ids[1] % 2 * half, half), half)
    grad_in = added((own, other))
    wide = tok[mine].astype(F32)
    inverse = norm_stats(wide)
    normed = wide * inverse
    rows_out[...] = (
        branch[mine].astype(F32) + norm_backward(grad_in, normed, inverse, gain[...])
    ).astype(BF16)
    gain_out[...] = 0.5 * jnp.sum(grad_in * normed, axis=0, keepdims=True)


def sums_kernel(parts, router_out, post_out, q_out, k_out, gain_out):
    devices = parts.shape[0]
    experts, step = router_out.shape[0], router_out.shape[1] // devices
    base = experts // 2
    total = parts[0].astype(F32)[base:]
    for d in range(1, devices):
        total = total + parts[d].astype(F32)[base:]
    q_out[...] = total[1:2]
    k_out[...] = total[2:3]
    part = gain_out.shape[1]
    for j in range(-(-part // 128)):
        lanes = min(128, part)
        gain_out[:, j * 128 : j * 128 + lanes] = total[3 + j : 4 + j, :lanes]
    group = 128 // step
    for g in range(devices // group):
        held = range(g * group, (g + 1) * group)
        here = slice(g * 128, (g + 1) * 128)
        wide = [parts[d].astype(F32) for d in held]
        router_out[:base, here] = jnp.concatenate([w[:base, :step] for w in wide], axis=1)
        router_out[base:, here] = jnp.concatenate(
            [w[:base, 64 : 64 + step] for w in wide], axis=1
        )
        post_out[:, here] = jnp.concatenate([w[base : base + 1, :step] for w in wide], axis=1)


def join_kernel(ids, own, other, gain_part, q_gain, k_gain, *refs):
    sums, (out, parts_low, parts_out) = refs[:-3], refs[-3:]
    total = added(sums)
    wa_count = lax.axis_size("wa")
    experts, part = total.shape[0] // 2, total.shape[1]
    step = part // wa_count
    mine = total[:, :step]
    for w in range(1, wa_count):
        mine = jnp.where(ids[1] == w, total[:, w * step : (w + 1) * step], mine)
    router_part, post = mine[:experts], mine[experts : experts + 1]
    base = experts // 2
    parts_out[...] = jnp.zeros(parts_out.shape, F32)
    for d in range(parts_out.shape[0]):
        parts_out[d, :base, :step] = router_part[:base]
        parts_out[d, :base, 64 : 64 + step] = router_part[base:]
        parts_out[d, base : base + 1, :step] = post
        parts_out[d, base + 1 : base + 2] = q_gain[...]
        parts_out[d, base + 2 : base + 3] = k_gain[...]
        first = d // wa_count * part
        for j in range(-(-part // 128)):
            lanes = min(128, part)
            parts_out[d, base + 3 + j : base + 4 + j, :lanes] = gain_part[
                :, first + j * 128 : first + j * 128 + lanes
            ]
    parts_low[...] = parts_out[...].astype(BF16)
    parts_low.send()
    half = own.shape[0]
    for source, core in ((own, ids[1] % 2), (other, 1 - ids[1] % 2)):
        out[pl.ds(pl.multiple_of(core * half, half), half)] = source[...]


def token_order(wa, pieces, count, first, scr):
    part = scr.shape[1]
    wa_count = len(pieces)
    quarter = scr.shape[0] // (wa_count * count)
    for k, piece in enumerate(pieces):
        for c in range(count):
            row = pl.multiple_of((c * wa_count + (wa ^ k)) * quarter, quarter)
            scr[pl.ds(row, quarter)] = piece[c * quarter : (c + 1) * quarter, first : first + part]
    return scr[...]


def out_weight_kernel(ids, attended, *refs):
    pieces, (out, *sends) = refs[:4], refs[4:-2]
    scr, att_scr = refs[-2:]
    part, wide, rows = out.shape[1], scr.shape[1], scr.shape[0] // 4
    columns = token_order(ids[1], pieces, 4, wide, scr)
    for j in range(4):
        att_scr[j * rows : (j + 1) * rows] = attended[j, :rows]
    partial = contract_first(att_scr[...], columns)
    for k, target in enumerate((out, *sends)):
        target[...] = partial[:, k * part : (k + 1) * part].astype(target.dtype)


def in_weight_kernel(ids, queries, *refs):
    pieces, (own, *sends) = refs[:4], refs[4:-1]
    left, part = refs[-1], own.shape[0]
    partial = contract_first(token_order(ids[1], pieces, 4, 0, left), queries[...])
    for k, send in enumerate(sends, start=1):
        send[...] = partial[k * part : (k + 1) * part].astype(BF16)
        send.send()
    own[...] = partial[:part]


def kv_weight_kernel(ids, *refs):
    kvs, refs, rows = refs[:4], refs[4:-1], refs[-1]
    count = kvs[0].shape[0]
    for k, piece in enumerate(kvs):
        rows[pl.ds(pl.multiple_of((ids[3] ^ k) * count, count), count)] = piece[...]
    in_weight_kernel(ids, rows, *refs)


def last_kernel(lows, parts, hidden, out_own, wo_own, wq_own, kv_own, *refs):
    outs, refs = refs[:3], refs[3:]
    wos, wqs, kvs = [refs[j * (lows - 1) : (j + 1) * (lows - 1)] for j in range(3)]
    refs = refs[3 * (lows - 1) :]
    output, wo_out, wq_out, wk_out, wv_out = refs[:5]
    wo_out[...] = added((wo_own, *wos))
    wo_out.send()
    wq_out[...] = added((wq_own, *wqs))
    wq_out.send()
    total = added((kv_own, *kvs))
    size = wk_out.shape[1]
    wk_out[...] = total[:, :size]
    wv_out[...] = total[:, size:]
    output[...] = (hidden[...] + added((out_own, *outs))).astype(BF16)
    sums_kernel(parts, *refs[5:])


def bind(body, *sizes):
    return lambda *refs: body(*sizes, *refs)


def on_device(
    tokens,
    positions,
    routes,
    query_weight,
    key_matrix,
    value_matrix,
    out_weight,
    query_gain,
    key_gain,
    input_norm,
    post_norm,
    router,
    gate_weight,
    up_weight,
    down_weight,
    cotangent,
):
    lead_count, low_count = lax.axis_size("lead"), lax.axis_size("low")
    ctx_count = lead_count * low_count
    wa_count = lax.axis_size("wa")
    lead_id = lax.axis_index("lead")
    wa_id = lax.axis_index("wa")
    ctx_id = lead_id * low_count + lax.axis_index("low")
    plane_id = lax.axis_index("low") * wa_count + wa_id
    low_id = lax.axis_index("low")
    ids = jnp.stack([ctx_id, wa_id, ctx_id * wa_count + wa_id, lead_id, plane_id, low_id]).astype(I32)
    row_count, width = tokens.shape
    span = row_count // SEQS
    quarter = row_count // wa_count
    size = query_gain.shape[0]
    local_width = query_weight.shape[1]
    heads = local_width // size
    length = span * ctx_count
    experts = router.shape[1]
    top = routes.shape[1]
    hidden_units = gate_weight.shape[2]
    devices = ctx_count * wa_count
    planes = low_count * wa_count
    part = width // ctx_count
    capacity = max(2, (5 * quarter * top + 4 * experts - 1) // (4 * experts))
    group = -(-4 * capacity // 16) * 16 if planes > 8 else 4 * capacity
    slot_rows = planes * group
    extra = -(-2 * experts // 128) * 128
    everywhere, plane, blocks = ("lead", "low", "wa"), ("low", "wa"), ("lead", "low")
    gate_weight, up_weight, down_weight = gate_weight[0], up_weight[0], down_weight[0]
    input_norm, post_norm = input_norm[None], post_norm[None]
    query_gain, key_gain = query_gain[None], key_gain[None]

    halves = np.arange(size) % (size // 2)
    rates = np.exp(halves * (-2.0 * math.log(1000000.0) / size)).astype(np.float32)
    attention_input, kv_own, keys_raw, cosine, sine = vcall(
        kv_kernel,
        [
            ((row_count, width), BF16),
            ((row_count, 2 * size), BF16, "near"),
            ((row_count, size), F32),
            ((row_count, size), F32),
            ((row_count, size), F32),
        ],
        tokens, input_norm, key_matrix, value_matrix, positions[None], jnp.asarray(rates)[None],
        key_gain,
        flops=4 * row_count * width * size,
    )
    kv_all = exchange([kv_own] * ctx_count, blocks)

    q_heads, queries_raw = vcall(
        query_kernel,
        [
            ((SEQS, heads * span, size), BF16),
            ((SEQS, heads * span, size), F32),
        ],
        attention_input, query_weight, cosine, sine, query_gain,
        flops=2 * row_count * width * local_width,
    )

    (cot_send,) = vcall(
        pack_kernel,
        [((quarter, width + 128), BF16, "near")],
        cotangent, routes.T,
        after=[q_heads],
    )
    cot_pieces = exchange([cot_send] * 4, "lead")

    keys_seq, values_seq, weights_low, attended_low, *branch = vcall(
        bind(attend_kernel, ctx_count),
        [
            ((SEQS, length, size), BF16),
            ((SEQS, length, size), BF16),
            ((SEQS, heads * span, length), BF16),
            ((row_count, local_width), BF16),
        ]
        + [((quarter, width), BF16, "near")] * wa_count,
        ids, q_heads, positions[None], out_weight, *near(kv_all),
        scratch=[pltpu.VMEM((row_count, width), BF16)],
        flops=2 * row_count * width * local_width + 4 * row_count * local_width * length,
        megabytes=48,
    )
    branch = exchange(branch, "wa")

    inner = np.arange(slot_rows) % group
    columns = np.zeros((8, slot_rows), np.int32)
    columns[0] = np.arange(slot_rows) // group
    columns[1] = np.minimum(inner // capacity, 3)
    columns[2] = np.where(inner < 4 * capacity, inner % capacity, -5)
    chosen, *cot_groups = vcall(
        bind(route_kernel, experts, top, planes),
        [((row_count, slot_rows), BF16)] + [((group, width), BF16)] * planes,
        ids, jnp.asarray(columns), *near(cot_pieces),
        loose=[branch[0]],
        scratch=[
            pltpu.VMEM((4 * quarter, width + 128), BF16),
            pltpu.VMEM((slot_rows, width), F32),
        ],
        flops=2 * slot_rows * row_count * width,
    )
    send, hidden, probs = vcall(
        hidden_kernel,
        [
            ((quarter, width + extra), BF16, "near"),
            ((quarter, width), F32),
            ((quarter, experts), F32),
        ],
        ids, tokens, routes.T, post_norm, router.T, *near(branch),
        after=[chosen],
        flops=2 * quarter * width * experts,
    )

    cot_groups = exchange(cot_groups, plane)
    cot_rows, grad_raw = vcall(
        bind(cot_rows_kernel, planes),
        [((slot_rows, width), BF16), ((slot_rows, hidden_units), F32)],
        ids, down_weight, *cot_groups,
        scratch=[pltpu.VMEM((slot_rows, width), F32)],
        flops=2 * slot_rows * hidden_units * width,
    )

    rows_in, early_rows = vcall(
        pick_kernel,
        [
            ((slot_rows, width + extra), BF16),
            ((row_count + width // local_width * quarter, local_width), BF16),
        ],
        ids, chosen, attended_low, attention_input, *near(exchange([send] * 4, "lead")),
        loose=cot_groups[1:],
        scratch=[pltpu.VMEM((row_count, width + extra), BF16)],
        flops=2 * slot_rows * row_count * width,
    )
    rows_in = swap(rows_in, plane)
    early_all = gather(early_rows, "lead").reshape(4, -1, local_width)
    activation, grad_gate_part, grad_up_part, row_prob, back = vcall(
        bind(expert_kernel, experts),
        [
            ((slot_rows, hidden_units), BF16),
            ((slot_rows, hidden_units), BF16),
            ((slot_rows, hidden_units), BF16),
            ((slot_rows, 128), F32),
            ((slot_rows, width + extra), BF16),
        ],
        ids, gate_weight, up_weight, grad_raw, Near(rows_in),
        split={1: 3, 2: 3, -5: tuple((c * width // 4, width // 4 + (extra if c == 3 else 0)) for c in range(4))},
        flops=8 * slot_rows * hidden_units * width,
        megabytes=48,
    )

    grad_gate_weight, grad_up_weight, grad_down_weight = vcall(
        expert_weights_kernel,
        [
            ((width, hidden_units), F32),
            ((width, hidden_units), F32),
            ((hidden_units, width), F32),
        ],
        rows_in, grad_gate_part, grad_up_part, activation, cot_rows, row_prob,
        split={-1: 4, -2: 4, -3: 3},
        flops=6 * slot_rows * hidden_units * width,
        megabytes=40,
    )

    def to_tokens(rows, after, place, loose=()):
        return vcall(
            combine_kernel,
            [((quarter, rows.shape[1]), F32, *place)]
            + [((quarter, rows.shape[1]), BF16, "near")] * 3,
            ids, chosen, Near(rows),
            after=after,
            loose=loose,
            scratch=[pltpu.VMEM((row_count, rows.shape[1]), F32)],
            flops=2 * slot_rows * row_count * width,
        )

    back = swap(back, plane)
    back_pieces = exchange(to_tokens(back, [grad_gate_weight, early_all], ["near"]), "lead")
    (out_rows,) = vcall(
        out_rows_kernel,
        [((slot_rows, width), BF16)],
        activation, down_weight, row_prob,
        after=back_pieces[1:],
        flops=2 * slot_rows * hidden_units * width,
    )
    out_made = out_rows
    out_rows = swap(out_rows, plane)
    grad_low, *late_rows = vcall(
        grad_hidden_kernel,
        [
            ((quarter, width), BF16, "near"),
        ]
        + [((quarter + experts + 16, width // 4), BF16, "near")] * 4,
        ids, hidden, probs, router.T, cotangent, post_norm, *near(back_pieces),
        scratch=[pltpu.VMEM((quarter + experts + 16, width), BF16)],
        flops=4 * quarter * width * experts,
    )

    grad_pieces = exchange([grad_low] * wa_count, "wa")
    late_all = exchange(late_rows, "lead")
    grad_queries, query_gain_part, kv_parts, grad_branch = vcall(
        bind(attend_back_kernel, ctx_count),
        [
            ((row_count, local_width), BF16),
            ((1, size), F32),
            ((ctx_count, row_count, 2 * size), BF16),
            ((row_count, width), BF16),
        ],
        ids, q_heads, keys_seq, values_seq, weights_low, queries_raw, out_weight,
        cosine, sine, query_gain, *near(grad_pieces),
        split={6: 4},
        after=[out_made],
        loose=late_all[1:],
        scratch=[pltpu.VMEM((heads * span, size), BF16)],
        flops=2 * row_count * width * local_width + 8 * row_count * local_width * length,
        megabytes=48,
    )
    kv_parts = swap(kv_parts, blocks)
    queries_all = gather(grad_queries, "lead")
    (from_queries,) = vcall(
        query_in_kernel,
        [((row_count, width), F32)],
        grad_queries, query_weight,
        flops=2 * row_count * width * local_width,
    )
    (weight_columns,) = vcall(
        bind(columns_kernel, low_count, quarter),
        [((4 * quarter + experts, 2 * low_count * part), BF16)],
        ids, early_all, *near(late_all),
        after=[from_queries],
        scratch=[pltpu.VMEM((4, quarter + experts + 16, width // 4), BF16)],
    )
    grad_kv, key_gain_part, grad_in_own, grad_in_send = vcall(
        grad_in_kernel,
        [
            ((row_count, 2 * size), BF16, "near"),
            ((1, size), F32),
            ((row_count // 2, width), BF16, "near"),
            ((row_count // 2, width), BF16, "near"),
        ],
        ids, from_queries, keys_raw, cosine, sine, key_gain, key_matrix, value_matrix, Near(kv_parts),
        scratch=[pltpu.VMEM((row_count, width), BF16)],
        flops=4 * row_count * width * size,
    )
    column_pieces = gather_wa_pieces(weight_columns)
    grad_in_half, sums_own, *sends = vcall(
        half_kernel,
        [((row_count // 2, width), BF16, "near"), ((2 * experts, part), F32)]
        + [((2 * experts, part), BF16, "near")] * (low_count - 1),
        Near(grad_in_own), Near(xor_permute(grad_in_send, "wa", 1)),
        *[Rows(piece, 4 * quarter, experts) for piece in column_pieces],
    )
    out_sums = to_tokens(out_rows, [], [], [grad_in_half])
    out_pieces = exchange(out_sums, "lead")
    sums = [sums_own] + [xor_permute(sends[k - 1], "low", k) for k in range(1, low_count)]
    grad_kv_all = exchange([grad_kv] * 4, "lead")
    out_weight_own, *sends = vcall(
        out_weight_kernel,
        [((local_width, part), F32)] + [((local_width, part), BF16)] * (low_count - 1),
        ids, early_all, *column_pieces,
        loose=[grad_in_half],
        scratch=[
            pltpu.VMEM((4 * row_count, low_count * part), BF16),
            pltpu.VMEM((4 * row_count, local_width), BF16),
        ],
        flops=8 * row_count * low_count * local_width * part,
    )
    others = [xor_permute(sends[k - 1], "low", k) for k in range(1, low_count)]
    weight_own, *sends = vcall(
        in_weight_kernel,
        [((part, local_width), F32)] + [((part, local_width), BF16)] * (low_count - 1),
        ids, queries_all, *column_pieces,
        loose=[grad_in_half],
        scratch=[pltpu.VMEM((4 * row_count, low_count * part), BF16)],
        flops=8 * row_count * low_count * local_width * part,
    )
    weight_others = [xor_permute(sends[k - 1], "low", k) for k in range(1, low_count)]
    token_rows, grad_input_part = vcall(
        token_rows_kernel,
        [((row_count // 2, width), BF16, "near"), ((1, width), F32)],
        ids, tokens, input_norm, grad_branch,
        Near(grad_in_half), Near(xor_permute(grad_in_half, "wa", 2)),
        after=[out_weight_own, weight_own],
        loose=grad_kv_all[1:],
    )
    sum_rows = -(-(experts // 2 + 3 + -(-part // 128)) // 16) * 16
    grad_tokens, small_parts = vcall(
        join_kernel,
        [
            ((row_count, width), BF16),
            ((devices, sum_rows, 128), BF16),
        ],
        ids, Near(token_rows), Near(xor_permute(token_rows, "wa", 1)),
        grad_input_part, query_gain_part, key_gain_part,
        *sums,
        after=[out_sums[0]],
        loose=others,
        scratch=[pltpu.VMEM((devices, sum_rows, 128), F32)],
    )

    kv_weight_own, *sends = vcall(
        kv_weight_kernel,
        [((part, 2 * size), F32)] + [((part, 2 * size), BF16)] * (low_count - 1),
        ids, *near(grad_kv_all), *column_pieces,
        after=[small_parts],
        scratch=[
            pltpu.VMEM((4 * row_count, low_count * part), BF16),
            pltpu.VMEM((4 * row_count, 2 * size), BF16),
        ],
        flops=8 * row_count * low_count * 2 * size * part,
    )
    kv_others = [xor_permute(sends[k - 1], "low", k) for k in range(1, low_count)]
    (
        output, grad_out_weight, grad_query_weight, grad_key_weight, grad_value_weight,
        grad_router, grad_post_norm, grad_query_gain, grad_key_gain, grad_input_norm,
    ) = vcall(
        bind(last_kernel, low_count),
        [
            ((quarter, width), BF16),
            ((local_width, part), F32),
            ((part, local_width), F32),
            ((part, size), F32),
            ((part, size), F32),
            ((experts, width), F32),
            ((1, width), F32),
            ((1, size), F32),
            ((1, size), F32),
            ((1, part), F32),
        ],
        Near(swap(small_parts, everywhere)), hidden, out_sums[0], out_weight_own, weight_own,
        kv_weight_own, *near(out_pieces[1:] + others + weight_others + kv_others),
    )
    return (
        output,
        grad_tokens,
        grad_query_weight,
        grad_key_weight,
        grad_value_weight,
        grad_out_weight,
        grad_query_gain[0],
        grad_key_gain[0],
        grad_input_norm[0],
        grad_post_norm[0],
        grad_router.T,
        grad_gate_weight[None],
        grad_up_weight[None],
        grad_down_weight[None],
    )


def solution(mesh):
    ctx_count, wa_count = mesh.devices.shape
    finer = Mesh(mesh.devices.reshape(4, ctx_count // 4, wa_count), ("lead", "low", "wa"))
    return jax.shard_map(
        on_device,
        mesh=finer,
        in_specs=(
            P(("lead", "low"), None),
            P(("lead", "low")),
            P(("lead", "low", "wa"), None),
            P(None, "wa"),
            P(None, "wa"),
            P(None, "wa"),
            P("wa", None),
            P(),
            P(),
            P(),
            P(),
            P(),
            P(("lead", "low", "wa"), None, None),
            P(("lead", "low", "wa"), None, None),
            P(("lead", "low", "wa"), None, None),
            P(("lead", "low", "wa"), None),
        ),
        out_specs=(
            P(("lead", "low", "wa"), None),
            P(("lead", "low"), None),
            P(("lead", "low"), "wa"),
            P(("lead", "low"), "wa"),
            P(("lead", "low"), "wa"),
            P("wa", ("lead", "low")),
            P(),
            P(),
            P(("lead", "low")),
            P(),
            P(),
            P(("lead", "low", "wa"), None, None),
            P(("lead", "low", "wa"), None, None),
            P(("lead", "low", "wa"), None, None),
        ),
        check_vma=False,
    )
```
